32 devices in a mesh: dp: 8 (over y, x, core), tensor: 4 (over z).
Axes of the slice: x: 2, y: 2, z: 4, core: 2. Of those that a mesh axis runs over, the one named last changes fastest.
Arguments:
- tokens: bfloat16 [32768, 2048], P(('dp', 'tensor')), may hold values from -6 to 6
- lengths: int32 [8, 3], P('dp'), may hold values from 1024 to 2048, as said below
- first_norm_gain: float32 [2048], replicated, may hold values from 0.5 to 1.5
- w_in: bfloat16 [2048, 2048], P(None, 'tensor'), may hold values from -0.125 to 0.125
- w_forget: bfloat16 [2048, 2048], P(None, 'tensor'), may hold values from -0.125 to 0.125
- w_gate: bfloat16 [2048, 2048], P(None, 'tensor'), may hold values from -0.125 to 0.125
- lower_bound: float32 [2048], P('tensor'), may hold values from 0.3 to 0.97
- gate_gain: float32 [2048], P('tensor'), may hold values from 0.5 to 1.5
- w_out: bfloat16 [2048, 2048], P('tensor'), may hold values from -0.25 to 0.25
- feedforward_gain: float32 [2048], replicated, may hold values from 0.5 to 1.5
- w_up: bfloat16 [2048, 5632], P(None, 'tensor'), may hold values from -0.125 to 0.125
- w_glu: bfloat16 [2048, 5632], P(None, 'tensor'), may hold values from -0.125 to 0.125
- w_down: bfloat16 [5632, 2048], P('tensor'), may hold values from -0.15625 to 0.15625
- cotangent: bfloat16 [32768, 2048], P(('dp', 'tensor')), may hold values from -6 to 6
Outputs:
- output: bfloat16 [32768, 2048], P(('dp', 'tensor'))
- token_gradient: float32 [32768, 2048], P(('dp', 'tensor'))
- grad_norm_gain: float32 [2048], replicated
- grad_w_in: float32 [2048, 2048], P('dp', 'tensor')
- grad_w_forget: float32 [2048, 2048], P('dp', 'tensor')
- grad_w_gate: float32 [2048, 2048], P('dp', 'tensor')
- grad_lower_bound: float32 [2048], replicated
- grad_gate_gain: float32 [2048], replicated
- grad_w_out: float32 [2048, 2048], P('tensor', 'dp')
- grad_mlp_gain: float32 [2048], replicated
- grad_w_up: float32 [2048, 5632], P('dp', 'tensor')
- grad_w_glu: float32 [2048, 5632], P('dp', 'tensor')
- grad_w_down: float32 [5632, 2048], P('tensor', 'dp')
- mean_forget: float32 [], replicated
The draws below stay inside these ranges and needn't reach their ends.
Inputs may be any that keep to these rules, and one draw needn't show every extreme that they name: `lengths`: each row sums to 4096; each row holds one sequence of 2048 tokens, at a position drawn from the seed; the other two sum to 2048 and are 1024 or more each.
All inputs are finite; a program needn't handle non-finite values.
Results may differ from the reference program's by a relative error of at most 0.014.
Values may be sent and summed in bfloat16 or wider, within the bound.
A program may use at most 448 MiB of HBM per device.

```python
import jax
import jax.numpy as jnp
from jax import lax

D = 2048
FF = 5632
MINLEN = 1024
TOK_DP = 4096
TOKENS = 32768
N_DP = 8


def draw_lengths(key, part):
    key = jax.random.fold_in(key, 7)
    first_key, second_key = jax.random.split(key)
    half = TOK_DP // 2
    cut = jax.random.randint(first_key, (N_DP,), MINLEN, half - MINLEN + 1)
    shorter = jnp.stack([cut, half - cut], axis=1)
    place = jax.random.randint(second_key, (N_DP, 1), 0, 3)
    slots = jnp.arange(3, dtype=jnp.int32)[None, :]
    index = jnp.clip(jnp.where(slots < place, slots, slots - 1), 0, 1)
    picked = jnp.take_along_axis(shorter, index, axis=1)
    return jnp.where(slots == place, half, picked).astype(jnp.int32)


def block_scale(key, dims, cuts, low, top_value):
    gain, own = 1.0, jax.random.fold_in(key, 6)
    for axis_at, shards_of in cuts:
        heights = jnp.exp(jax.random.uniform(jax.random.fold_in(own, axis_at), (shards_of,), jnp.float32, low / len(cuts), top_value / len(cuts)))
        gain = gain * jnp.repeat(heights, dims[axis_at] // shards_of).reshape([-1 if axis == axis_at else 1 for axis in range(len(dims))])
    return gain


def bell_draw(key, shape, deviation, bound, cuts=(), kind=jnp.bfloat16):
    level = block_scale(key, shape, cuts, -0.22, 0.18) if cuts else 1.0
    drawn = jax.random.normal(key, shape, jnp.float32) * deviation * level
    return jnp.minimum(jnp.maximum(drawn, -bound), bound).astype(kind)


def setup_inputs(seed: int = 0) -> dict:
    streams_of = jax.random.split(jax.random.key(seed), 15)
    return {
        "tokens": bell_draw(streams_of[0], (TOKENS, D), 1.0, 6.0, ((0, 32),)),
        "lengths": draw_lengths(jax.random.fold_in(streams_of[14], 71), 0),
        "first_norm_gain": jnp.clip(1.0 + 0.1 * jax.random.normal(streams_of[2], (D,), jnp.float32), 0.5, 1.5),
        "w_in": bell_draw(streams_of[3], (D, D), D ** -0.5, 0.125, ((1, 4),)),
        "w_forget": bell_draw(streams_of[4], (D, D), D ** -0.5, 0.125, ((1, 4),)),
        "w_gate": bell_draw(streams_of[5], (D, D), D ** -0.5, 0.125, ((1, 4),)),
        "lower_bound": jnp.clip(0.3 + 0.67 * jax.random.uniform(streams_of[6], (D,), jnp.float32) ** block_scale(streams_of[6], (D,), ((0, 4),), -0.2, 0.2), 0.3, 0.97),
        "gate_gain": jnp.clip(1.0 + 0.1 * jax.random.normal(streams_of[7], (D,), jnp.float32), 0.5, 1.5),
        "w_out": bell_draw(streams_of[8], (D, D), (D // 4) ** -0.5, 0.25, ((0, 4),)),
        "feedforward_gain": jnp.clip(1.0 + 0.1 * jax.random.normal(streams_of[9], (D,), jnp.float32), 0.5, 1.5),
        "w_up": bell_draw(streams_of[10], (D, FF), D ** -0.5, 0.125, ((1, 4),)),
        "w_glu": bell_draw(streams_of[11], (D, FF), D ** -0.5, 0.125, ((1, 4),)),
        "w_down": bell_draw(streams_of[12], (FF, D), (FF // 4) ** -0.5, 0.15625, ((0, 4),)),
        "cotangent": bell_draw(streams_of[13], (TOKENS, D), 1.0, 6.0, ((0, 32),)),
    }


EPS = 1e-06

@jax.custom_vjp
def low(v):
    return lax.optimization_barrier(v.astype(jnp.bfloat16)).astype(jnp.float32)

@jax.custom_vjp
def low_back(v):
    return v

def low_keep(v):
    return (low(v), None)

def low_pass(kept, upstream_gradient):
    return (upstream_gradient,)

def back_keep(v):
    return (v, None)

def back_low(kept, upstream_gradient):
    return (low(upstream_gradient),)
low.defvjp(low_keep, low_pass)
low_back.defvjp(back_keep, back_low)

def matmul(left, right):
    return jnp.dot(left, right, precision=lax.Precision.HIGHEST, preferred_element_type=jnp.float32)

def affine(early, late):
    return (early[0] * late[0], late[0] * early[1] + late[1])

def keep_mask(lengths_row, total):
    ends = jnp.cumsum(lengths_row)
    starts = ends - lengths_row
    rows = jnp.arange(total, dtype=jnp.int32)
    flag = jnp.any(rows[:, None] == starts[None, :].astype(jnp.int32), axis=1)
    return jnp.where(flag, 0.0, 1.0).astype(jnp.float32)[:, None]

def group_forward(xg, lengths_row, params):
    first_norm_gain, w_in, w_forget, w_gate, lower_bound, gate_gain, w_out, feedforward_gain, w_up, w_glu, w_down = params
    inverse_rms1 = lax.rsqrt(lax.optimization_barrier(jnp.mean(xg * xg, axis=1, keepdims=True)) + EPS)
    normalized_rows = low(xg * inverse_rms1 * first_norm_gain)
    p_in = low_back(matmul(normalized_rows, w_in))
    p_forget = low_back(matmul(normalized_rows, w_forget))
    p_gate = low_back(matmul(normalized_rows, w_gate))
    lam = lower_bound + (1.0 - lower_bound) * jax.nn.sigmoid(p_forget)
    inject = jax.nn.silu(p_in) * (1.0 - lam)
    decay = lam * keep_mask(lengths_row, xg.shape[0])
    _, state = lax.associative_scan(affine, (decay, inject), axis=0)
    scale = lax.rsqrt(lax.optimization_barrier(jnp.mean(state * state, axis=1, keepdims=True)) + EPS)
    mixed = low(state * scale * gate_gain * jax.nn.silu(p_gate))
    residual_stream = xg + low_back(matmul(mixed, w_out))
    inverse_rms2 = lax.rsqrt(lax.optimization_barrier(jnp.mean(residual_stream * residual_stream, axis=1, keepdims=True)) + EPS)
    middle_stream = low(residual_stream * inverse_rms2 * feedforward_gain)
    up = low_back(matmul(middle_stream, w_up))
    glu = low_back(matmul(middle_stream, w_glu))
    hidden = low(jax.nn.silu(glu) * up)
    return (residual_stream + matmul(hidden, w_down), jnp.sum(lam))

def reference(tokens, lengths, first_norm_gain, w_in, w_forget, w_gate, lower_bound, gate_gain, w_out, feedforward_gain, w_up, w_glu, w_down, cotangent):
    params = (first_norm_gain, w_in.astype(jnp.float32), w_forget.astype(jnp.float32), w_gate.astype(jnp.float32), lower_bound, gate_gain, w_out.astype(jnp.float32), feedforward_gain, w_up.astype(jnp.float32), w_glu.astype(jnp.float32), w_down.astype(jnp.float32))
    input_float32 = tokens.astype(jnp.float32)

    def forward(xf, weights):
        groups = xf.reshape(N_DP, TOK_DP, D)

        def one(item):
            return group_forward(item[0], item[1], weights)
        outs, sums = lax.map(jax.checkpoint(one), (groups, lengths))
        return (outs.reshape(N_DP * TOK_DP, D), jnp.sum(sums))
    result, pullback, forget_sum = jax.vjp(forward, input_float32, params, has_aux=True)
    grad_x, grads = pullback(cotangent.astype(jnp.float32))
    mean_forget = forget_sum / (N_DP * TOK_DP * D)
    return (result.astype(jnp.bfloat16), grad_x, grads[0], grads[1], grads[2], grads[3], grads[4], grads[5], grads[6], grads[7], grads[8], grads[9], grads[10], mean_forget)
```

```python
import functools

import jax
import jax.numpy as jnp
from jax import lax
from jax.experimental import pallas as pl
from jax.experimental.pallas import tpu as pltpu
from jax.sharding import Mesh
from jax.sharding import PartitionSpec as P

EPS = 1e-06
VMEM_LIMIT = 60 * 1024 * 1024
F32 = jnp.float32
BF16 = jnp.bfloat16


def params(**kw):
    return pltpu.CompilerParams(vmem_limit_bytes=VMEM_LIMIT, **kw)


def nn(left, right):
    return lax.dot_general(left, right, (((1,), (0,)), ((), ())), preferred_element_type=F32)


def nt(left, right):
    return lax.dot_general(left, right, (((1,), (1,)), ((), ())), preferred_element_type=F32)


def tn(left, right):
    return lax.dot_general(left, right, (((0,), (0,)), ((), ())), preferred_element_type=F32)


def sigmoid(v):
    return jax.nn.sigmoid(v)


def whole(shape):
    zeros = (0,) * len(shape)
    return pl.BlockSpec(shape, lambda *_: zeros)


def proj_kernel(x_ref, w_ref, o_ref):
    o_ref[0] = nn(x_ref[...], w_ref[0])


def project(normed, w3, chans):
    rows, width = normed.shape
    ways, _, wide = w3.shape
    return pl.pallas_call(
        proj_kernel,
        grid=(ways, wide // chans),
        in_specs=[
            whole((rows, width)),
            pl.BlockSpec((1, width, chans), lambda t, j: (t, 0, j)),
        ],
        out_specs=pl.BlockSpec((1, rows, chans), lambda t, j: (t, 0, j)),
        out_shape=jax.ShapeDtypeStruct((ways, rows, wide), F32),
        compiler_params=params(),
        name="project",
    )(normed, w3)


def gates(p_in, p_forget, lower, ids, starts):
    sig = sigmoid(p_forget)
    lam = lower + (1.0 - lower) * sig
    fresh = ids == starts[0]
    for s in starts[1:]:
        fresh = jnp.logical_or(fresh, ids == s)
    keep = jnp.where(fresh, 0.0, 1.0)
    return sig, lam, keep


def forward_total_kernel(starts_ref, p_ref, lower_ref, o_ref):
    rows, chans = p_ref.shape[1], p_ref.shape[2] // 2
    lower = lower_ref[0]
    starts = [starts_ref[i] for i in range(starts_ref.shape[0])]
    iota = lax.broadcasted_iota(jnp.int32, (8, chans), 0)

    def step(g, carry):
        total, last = carry
        at = pl.multiple_of(g * 8, 8)
        p_in = p_ref[0, pl.ds(at, 8), :chans]
        p_forget = p_ref[0, pl.ds(at, 8), chans:]
        _, lam, keep = gates(p_in, p_forget, lower, iota + at, starts)
        a = lam * keep
        b = p_in * sigmoid(p_in) * (1.0 - lam)
        for s in (1, 2, 4):
            b = a * pltpu.roll(b, s, 0) + b
            a = a * pltpu.roll(a, s, 0)
        a, b = a[7:8], b[7:8]
        return total * a, a * last + b

    total, last = lax.fori_loop(
        0, rows // 8, step, (jnp.ones((1, chans), F32), jnp.zeros((1, chans), F32)), unroll=2
    )
    o_ref[0, 0:1] = total
    o_ref[0, 1:2] = last


def forward_total(p, lower, starts):
    ways, rows, wide = p.shape
    chans = wide // 3
    return pl.pallas_call(
        forward_total_kernel,
        grid=(ways,),
        in_specs=[
            pl.BlockSpec(memory_space=pltpu.SMEM),
            pl.BlockSpec((1, rows, 2 * chans), lambda t: (t, 0, 0)),
            pl.BlockSpec((1, 1, chans), lambda t: (t, 0, 0)),
        ],
        out_specs=pl.BlockSpec((1, 2, chans), lambda t: (t, 0, 0)),
        out_shape=jax.ShapeDtypeStruct((ways, 2, chans), F32),
        compiler_params=params(),
        name="forward_total",
    )(starts, p, lower)


def forward_scan_kernel(starts_ref, p_ref, lower_ref, gain_ref, enter_ref, state_ref, mixed_ref, lam_ref, held):
    ways, rows, wide = p_ref.shape
    chans = wide // 3
    block = pl.program_id(0)
    starts = [starts_ref[i] for i in range(starts_ref.shape[0])]
    iota = lax.broadcasted_iota(jnp.int32, (8, chans), 0)

    @pl.when(block == 0)
    def _():
        held[...] = enter_ref[...]
        lam_ref[...] = jnp.zeros_like(lam_ref)

    for t in range(ways):
        lower = lower_ref[t]

        def step(g, carry):
            before, lam_sum = carry
            at = pl.multiple_of(g * 8, 8)
            p_in = p_ref[t, pl.ds(at, 8), :chans]
            p_forget = p_ref[t, pl.ds(at, 8), chans : 2 * chans]
            _, lam, keep = gates(p_in, p_forget, lower, iota + (at + block * rows), starts)
            a = lam * keep
            b = p_in * sigmoid(p_in) * (1.0 - lam)
            for s in (1, 2, 4):
                far = iota >= s
                b = jnp.where(far, a * pltpu.roll(b, s, 0) + b, b)
                a = jnp.where(far, a * pltpu.roll(a, s, 0), a)
            state = a * before + b
            state_ref[t, pl.ds(at, 8), :] = state
            return state[7:8], lam_sum + lam

        last, lam_sum = lax.fori_loop(
            0, rows // 8, step, (held[t], jnp.zeros((8, chans), F32)), unroll=2
        )
        held[t] = last
        lam_ref[t] += lam_sum

    squares = jnp.zeros((rows, 1), F32)
    for t in range(ways):
        state = state_ref[t]
        squares += jnp.sum(state * state, axis=1, keepdims=True)
    scale = lax.rsqrt(squares / (ways * chans) + EPS)
    for t in range(ways):
        gate = p_ref[t, :, 2 * chans :]
        mixed = state_ref[t] * scale * gain_ref[t] * (gate * sigmoid(gate))
        mixed_ref[t] = mixed.astype(BF16)


def forward_scan(p, lower, gain, starts, enter):
    ways, rows, wide = p.shape
    chans = wide // 3
    part = min(rows, 128)
    return pl.pallas_call(
        forward_scan_kernel,
        grid=(rows // part,),
        in_specs=[
            pl.BlockSpec(memory_space=pltpu.SMEM),
            pl.BlockSpec((ways, part, wide), lambda i: (0, i, 0)),
            whole((ways, 1, chans)),
            whole((ways, 1, chans)),
            whole((ways, 1, chans)),
        ],
        out_specs=[
            pl.BlockSpec((ways, part, chans), lambda i: (0, i, 0)),
            pl.BlockSpec((ways, part, chans), lambda i: (0, i, 0)),
            whole((ways, 8, chans)),
        ],
        out_shape=[
            jax.ShapeDtypeStruct((ways, rows, chans), F32),
            jax.ShapeDtypeStruct((ways, rows, chans), BF16),
            jax.ShapeDtypeStruct((ways, 8, chans), F32),
        ],
        scratch_shapes=[pltpu.VMEM((ways, 1, chans), F32)],
        compiler_params=params(),
        name="forward_scan",
    )(starts, p, lower, gain, enter)


def backward_total_kernel(
    starts_ref, pf_ref, pg_ref, state_ref, gm_ref, lower_ref, gain_ref,
    gstate_ref, ggate_ref, dgain_ref, total_ref, held,
):
    ways, rows, chans = pf_ref.shape
    step_id = pl.program_id(0)
    block = pl.num_programs(0) - 1 - step_id
    starts = [starts_ref[i] for i in range(starts_ref.shape[0])]
    iota = lax.broadcasted_iota(jnp.int32, (8, chans), 0)
    width = ways * chans

    @pl.when(step_id == 0)
    def _():
        held[...] = jnp.zeros_like(held)
        dgain_ref[...] = jnp.zeros_like(dgain_ref)

    squares = jnp.zeros((rows, 1), F32)
    cross = jnp.zeros((rows, 1), F32)
    for t in range(ways):
        state = state_ref[t]
        gate = pg_ref[t]
        inner = gm_ref[t] * gain_ref[t] * (gate * sigmoid(gate))
        gstate_ref[t] = inner
        squares += jnp.sum(state * state, axis=1, keepdims=True)
        cross += jnp.sum(inner * state, axis=1, keepdims=True)
    scale = lax.rsqrt(squares / width + EPS)
    pull = scale * scale * scale * cross / width
    for t in range(ways):
        state = state_ref[t]
        gate = pg_ref[t]
        sig = sigmoid(gate)
        slope = sig * (1.0 + gate * (1.0 - sig))
        unit = gm_ref[t] * state * scale
        ggate_ref[t] = (unit * gain_ref[t] * slope).astype(BF16)
        dgain_ref[t] += jnp.sum((unit * (gate * sig)).reshape(rows // 8, 8, chans), axis=0)
        gstate_ref[t] = gstate_ref[t] * scale - state * pull

    for t in range(ways):
        lower = lower_ref[t]

        def step(k, last):
            at = pl.multiple_of(rows - 8 - k * 8, 8)
            p_forget = pf_ref[t, pl.ds(at, 8), :]
            _, lam, keep = gates(None, p_forget, lower, iota + (at + block * rows), starts)
            a = lam * keep
            b = a * gstate_ref[t, pl.ds(at, 8), :]
            for s in (1, 2, 4):
                b = a * pltpu.roll(b, 8 - s, 0) + b
                a = a * pltpu.roll(a, 8 - s, 0)
            return a[0:1] * last + b[0:1]

        held[t] = lax.fori_loop(0, rows // 8, step, held[t], unroll=2)
    total_ref[...] = held[...]


def backward_total(p, state, g_mixed, lower, gain, starts):
    ways, rows, wide = p.shape
    chans = wide // 3
    part = min(rows, 128)
    last = rows // part - 1
    back = lambda i: (0, last - i, 0)
    block = pl.BlockSpec((ways, part, chans), back)
    return pl.pallas_call(
        backward_total_kernel,
        grid=(rows // part,),
        in_specs=[
            pl.BlockSpec(memory_space=pltpu.SMEM),
            pl.BlockSpec((ways, part, chans), lambda i: (0, last - i, 1)),
            pl.BlockSpec((ways, part, chans), lambda i: (0, last - i, 2)),
            block,
            block,
            whole((ways, 1, chans)),
            whole((ways, 1, chans)),
        ],
        out_specs=[block, block, whole((ways, 8, chans)), whole((ways, 1, chans))],
        out_shape=[
            jax.ShapeDtypeStruct((ways, rows, chans), F32),
            jax.ShapeDtypeStruct((ways, rows, chans), BF16),
            jax.ShapeDtypeStruct((ways, 8, chans), F32),
            jax.ShapeDtypeStruct((ways, 1, chans), F32),
        ],
        scratch_shapes=[pltpu.VMEM((ways, 1, chans), F32)],
        compiler_params=params(),
        name="backward_total",
    )(starts, p, p, state, g_mixed, lower, gain)


def backward_scan_kernel(
    starts_ref, pi_ref, pf_ref, state_ref, early_ref, gstate_ref, lower_ref, enter_ref, after_ref,
    gin_ref, gforget_ref, dlower_ref, held,
):
    ways, rows, chans = pi_ref.shape
    step_id = pl.program_id(0)
    block = pl.num_programs(0) - 1 - step_id
    starts = [starts_ref[i] for i in range(starts_ref.shape[0])]
    iota = lax.broadcasted_iota(jnp.int32, (8, chans), 0)

    @pl.when(step_id == 0)
    def _():
        held[...] = after_ref[...]
        dlower_ref[...] = jnp.zeros_like(dlower_ref)

    for t in range(ways):
        lower = lower_ref[t]
        first = jnp.where(block == 0, enter_ref[t], early_ref[t, 7:8])

        def eight(at, after, before):
            p_in = pi_ref[t, pl.ds(at, 8), :]
            p_forget = pf_ref[t, pl.ds(at, 8), :]
            grad = gstate_ref[t, pl.ds(at, 8), :]
            state = state_ref[t, pl.ds(at, 8), :]
            sig, lam, keep = gates(None, p_forget, lower, iota + (at + block * rows), starts)
            a = lam * keep
            b = a * grad
            for s in (1, 2, 4):
                near = iota < 8 - s
                b = jnp.where(near, a * pltpu.roll(b, 8 - s, 0) + b, b)
                a = jnp.where(near, a * pltpu.roll(a, 8 - s, 0), a)
            handed = a * after + b
            carry = grad + jnp.where(iota == 7, after, pltpu.roll(handed, 7, 0))
            previous = jnp.where(iota == 0, before, pltpu.roll(state, 1, 0))
            sig_in = sigmoid(p_in)
            act = p_in * sig_in
            g_lam = carry * previous * keep - carry * act
            g_in = carry * (1.0 - lam) * (sig_in * (1.0 + p_in * (1.0 - sig_in)))
            lower_part = g_lam * (1.0 - sig)
            g_forget = lower_part * (1.0 - lower) * sig
            return handed[0:1], g_in, g_forget, lower_part

        def step(k, carry):
            after, total = carry
            at = pl.multiple_of(rows - 16 - k * 16, 16)
            middle = state_ref[t, pl.ds(at, 8), :][7:8]
            ahead = jnp.maximum(at - 8, 0)
            held_before = state_ref[t, pl.ds(pl.multiple_of(ahead, 8), 8), :][7:8]
            before = jnp.where(at == 0, first, held_before)
            after, in_late, forget_late, part_late = eight(pl.multiple_of(at + 8, 8), after, middle)
            after, in_early, forget_early, part_early = eight(at, after, before)
            gin_ref[t, pl.ds(at, 16), :] = jnp.concatenate([in_early, in_late], 0).astype(BF16)
            gforget_ref[t, pl.ds(at, 16), :] = jnp.concatenate([forget_early, forget_late], 0).astype(BF16)
            return after, total + part_late + part_early

        after, total = lax.fori_loop(
            0, rows // 16, step, (held[t], jnp.zeros((8, chans), F32))
        )
        held[t] = after
        dlower_ref[t] += total


def backward_scan(p, state, g_state, lower, starts, enter, after):
    ways, rows, wide = p.shape
    chans = wide // 3
    part = min(rows, 128)
    last = rows // part - 1
    block = pl.BlockSpec((ways, part, chans), lambda i: (0, last - i, 0))
    eights = part // 8
    return pl.pallas_call(
        backward_scan_kernel,
        grid=(rows // part,),
        in_specs=[
            pl.BlockSpec(memory_space=pltpu.SMEM),
            pl.BlockSpec((ways, part, chans), lambda i: (0, last - i, 0)),
            pl.BlockSpec((ways, part, chans), lambda i: (0, last - i, 1)),
            block,
            pl.BlockSpec((ways, 8, chans), lambda i: (0, jnp.maximum((last - i) * eights - 1, 0), 0)),
            block,
            whole((ways, 1, chans)),
            whole((ways, 1, chans)),
            whole((ways, 1, chans)),
        ],
        out_specs=[block, block, whole((ways, 8, chans))],
        out_shape=[
            jax.ShapeDtypeStruct((ways, rows, chans), BF16),
            jax.ShapeDtypeStruct((ways, rows, chans), BF16),
            jax.ShapeDtypeStruct((ways, 8, chans), F32),
        ],
        scratch_shapes=[pltpu.VMEM((ways, 1, chans), F32)],
        compiler_params=params(),
        name="backward_scan",
    )(starts, p, p, state, state, g_state, lower, enter, after)


def branch_kernel(mixed_ref, w_ref, x_ref, gain_ref, resid_ref, middle_ref):
    ways = mixed_ref.shape[0]
    total = x_ref[...].astype(F32)
    acc = nn(mixed_ref[0], w_ref[0])
    for t in range(1, ways):
        acc += nn(mixed_ref[t], w_ref[t])
    resid = total + acc
    resid_ref[...] = resid
    inverse = lax.rsqrt(jnp.mean(resid * resid, axis=1, keepdims=True) + EPS)
    middle_ref[...] = (resid * inverse * gain_ref[...]).astype(BF16)


def branch(mixed, w_out, tokens, gain):
    ways, rows, chans = mixed.shape
    width = tokens.shape[1]
    part = min(rows, 256)
    line = pl.BlockSpec((part, width), lambda i: (i, 0))
    return pl.pallas_call(
        branch_kernel,
        grid=(rows // part,),
        in_specs=[
            pl.BlockSpec((ways, part, chans), lambda i: (0, i, 0)),
            whole((ways, chans, width)),
            line,
            whole((1, width)),
        ],
        out_specs=[line, line],
        out_shape=[
            jax.ShapeDtypeStruct((rows, width), F32),
            jax.ShapeDtypeStruct((rows, width), BF16),
        ],
        compiler_params=params(),
        name="branch",
    )(mixed, w_out, tokens, gain)


def up_kernel(x_ref, up_ref, glu_ref, hidden_ref, act_ref, slope_ref):
    x = x_ref[...]
    glu = nn(x, glu_ref[0])
    sig = sigmoid(glu)
    act = glu * sig
    up = nn(x, up_ref[0])
    hidden_ref[0] = (act * up).astype(BF16)
    act_ref[0] = act.astype(BF16)
    slope_ref[0] = (up * (sig * (1.0 + glu * (1.0 - sig)))).astype(BF16)


def feed_up(middle, w_up, w_glu):
    rows, width = middle.shape
    ways, _, units = w_up.shape
    part = min(rows, 512)
    weights = pl.BlockSpec((1, width, units), lambda t, i: (t, 0, 0))
    out = pl.BlockSpec((1, part, units), lambda t, i: (t, i, 0))
    return pl.pallas_call(
        up_kernel,
        grid=(ways, rows // part),
        in_specs=[pl.BlockSpec((part, width), lambda t, i: (i, 0)), weights, weights],
        out_specs=[out, out, out],
        out_shape=[jax.ShapeDtypeStruct((ways, rows, units), BF16)] * 3,
        compiler_params=params(),
        name="feed_up",
    )(middle, w_up, w_glu)


def down_kernel(h_ref, w_ref, resid_ref, o_ref):
    acc = nn(h_ref[0], w_ref[0])
    for t in range(1, h_ref.shape[0]):
        acc += nn(h_ref[t], w_ref[t])
    o_ref[...] = (resid_ref[...] + acc).astype(BF16)


def feed_down(hidden, w_down, resid):
    ways, rows, units = hidden.shape
    width = w_down.shape[2]
    part = 512
    return pl.pallas_call(
        down_kernel,
        grid=(width // part,),
        in_specs=[
            whole((ways, rows, units)),
            pl.BlockSpec((ways, units, part), lambda j: (0, 0, j)),
            pl.BlockSpec((rows, part), lambda j: (0, j)),
        ],
        out_specs=pl.BlockSpec((rows, part), lambda j: (0, j)),
        out_shape=jax.ShapeDtypeStruct((rows, width), BF16),
        compiler_params=params(),
        name="feed_down",
    )(hidden, w_down, resid)


def hidden_grad_kernel(dy_ref, w_ref, act_ref, slope_ref, gup_ref, gglu_ref):
    g_hidden = nt(dy_ref[...], w_ref[0])
    gup_ref[0] = (g_hidden * act_ref[0].astype(F32)).astype(BF16)
    gglu_ref[0] = (g_hidden * slope_ref[0].astype(F32)).astype(BF16)


def hidden_grad(dy, w_down, act, slope):
    rows, width = dy.shape
    ways, units, _ = w_down.shape
    part = min(rows, 512)
    out = pl.BlockSpec((1, part, units), lambda t, i: (t, i, 0))
    return pl.pallas_call(
        hidden_grad_kernel,
        grid=(ways, rows // part),
        in_specs=[
            pl.BlockSpec((part, width), lambda t, i: (i, 0)),
            pl.BlockSpec((1, units, width), lambda t, i: (t, 0, 0)),
            out,
            out,
        ],
        out_specs=[out, out],
        out_shape=[jax.ShapeDtypeStruct((ways, rows, units), BF16)] * 2,
        compiler_params=params(),
        name="hidden_grad",
    )(dy, w_down, act, slope)


def back_kernel(n, *refs):
    g_refs, w_refs, o_ref = refs[:n], refs[n : 2 * n], refs[2 * n]
    acc = nt(g_refs[0][0], w_refs[0][0])
    for g_ref, w_ref in zip(g_refs[1:], w_refs[1:]):
        acc += nt(g_ref[0], w_ref[0])
    first = pl.program_id(1) == 0

    @pl.when(first)
    def _():
        o_ref[...] = acc

    @pl.when(jnp.logical_not(first))
    def _():
        o_ref[...] += acc


def back(grads, weights, picks, units):
    ways, rows, _ = grads[0].shape
    width = weights[0].shape[1]
    part = min(width, 1024)
    return pl.pallas_call(
        functools.partial(back_kernel, len(grads)),
        grid=(width // part, ways),
        in_specs=[pl.BlockSpec((1, rows, units), lambda j, t: (t, 0, 0)) for _ in grads]
        + [pl.BlockSpec((1, part, units), functools.partial(lambda k, j, t: (t, j, k), k)) for k in picks],
        out_specs=pl.BlockSpec((rows, part), lambda j, t: (0, j)),
        out_shape=jax.ShapeDtypeStruct((rows, width), F32),
        compiler_params=params(),
        name="back",
    )(*grads, *weights)


def mixed_grad_kernel(g_ref, w_ref, o_ref):
    o_ref[0] = nt(g_ref[...], w_ref[0])


def mixed_grad(g_branch, w_out):
    rows, width = g_branch.shape
    ways, chans, _ = w_out.shape
    return pl.pallas_call(
        mixed_grad_kernel,
        grid=(ways,),
        in_specs=[whole((rows, width)), pl.BlockSpec((1, chans, width), lambda t: (t, 0, 0))],
        out_specs=pl.BlockSpec((1, rows, chans), lambda t: (t, 0, 0)),
        out_shape=jax.ShapeDtypeStruct((ways, rows, chans), F32),
        compiler_params=params(),
        name="mixed_grad",
    )(g_branch, w_out)


def by_rows_kernel(chips, n, *refs):
    left_ref, right_refs, o_ref = refs[0], refs[1 : 1 + n], refs[-1]
    add_ref = refs[1 + n] if len(refs) == n + 3 else None
    each = o_ref.shape[2]
    at = 0
    for right_ref in right_refs:
        wide = right_ref.shape[2]
        acc = tn(left_ref[...], right_ref[0])
        for j in range(chips):
            got = acc[j * each : (j + 1) * each]
            if add_ref is not None:
                got = got + add_ref[j, 0, :, at : at + wide].astype(F32)
            o_ref[j, 0, :, at : at + wide] = got.astype(BF16)
        at += wide


def by_rows(left, rights, add, chips):
    rows, tall = left.shape
    ways = rights[0].shape[0]
    each = tall // chips
    wide = sum(r.shape[2] for r in rights)
    block = pl.BlockSpec((chips, 1, each, wide), lambda t: (0, t, 0, 0))
    return pl.pallas_call(
        functools.partial(by_rows_kernel, chips, len(rights)),
        grid=(ways,),
        in_specs=[whole((rows, tall))]
        + [pl.BlockSpec((1, rows, r.shape[2]), lambda t: (t, 0, 0)) for r in rights]
        + ([block] if add is not None else []),
        out_specs=block,
        out_shape=jax.ShapeDtypeStruct((chips, ways, each, wide), BF16),
        compiler_params=params(),
        name="by_rows",
    )(left, *rights, *([add] if add is not None else []))


def by_cols_kernel(chips, *refs):
    left_ref, right_ref, o_ref = refs[0], refs[1], refs[-1]
    add_ref = refs[2] if len(refs) == 4 else None
    each = o_ref.shape[3]
    acc = tn(left_ref[0], right_ref[...])
    for j in range(chips):
        got = acc[:, j * each : (j + 1) * each]
        if add_ref is not None:
            got = got + add_ref[j, 0].astype(F32)
        o_ref[j, 0] = got.astype(BF16)


def by_cols(left, right, add, chips):
    ways, rows, tall = left.shape
    wide = right.shape[1]
    each = wide // chips
    block = pl.BlockSpec((chips, 1, tall, each), lambda t: (0, t, 0, 0))
    return pl.pallas_call(
        functools.partial(by_cols_kernel, chips),
        grid=(ways,),
        in_specs=[pl.BlockSpec((1, rows, tall), lambda t: (t, 0, 0)), whole((rows, wide))]
        + ([block] if add is not None else []),
        out_specs=block,
        out_shape=jax.ShapeDtypeStruct((chips, ways, tall, each), BF16),
        compiler_params=params(),
        name="by_cols",
    )(left, right, *([add] if add is not None else []))


def norm_pullback(upstream_gradient, unit_rows, inverse_rms, gain_vector):
    scaled_rows = upstream_gradient * gain_vector
    return inverse_rms * (
        scaled_rows - unit_rows * jnp.mean(scaled_rows * unit_rows, axis=1, keepdims=True)
    )


SWAP = ((0, 1), (1, 0))


def local(
    tokens,
    lengths,
    first_norm_gain,
    w_in,
    w_forget,
    w_gate,
    lower_bound,
    gate_gain,
    w_out,
    feedforward_gain,
    w_up,
    w_glu,
    w_down,
    cotangent,
):
    rows, width = tokens.shape
    chans = w_in.shape[1]
    units = w_up.shape[1]
    ways = lax.axis_size("tensor")
    chips = lax.axis_size("chip")
    groups = 2 * chips
    way = lax.axis_index("tensor")
    core = lax.axis_index("core")
    group = lax.axis_index("chip") * 2 + core
    every = ("tensor", "chip", "core")

    def mine(weights):
        tall = weights.shape[0] // groups
        return lax.dynamic_slice_in_dim(weights, group * tall, tall, 0)

    def gather(piece):
        return lax.all_gather(piece, every, axis=0, tiled=True)

    w3 = gather(jnp.concatenate([mine(w_in), mine(w_forget), mine(w_gate)], axis=1))
    w3 = w3.reshape(ways, width, 3 * chans)
    w_out_all = gather(mine(w_out)).reshape(ways, chans, width)
    w_glu_all = gather(mine(w_glu)).reshape(ways, width, units)
    w_up_all = gather(mine(w_up)).reshape(ways, width, units)
    w_down_all = gather(mine(w_down)).reshape(ways, units, width)

    lower = lax.all_gather(lower_bound, "tensor", axis=0).reshape(ways, 1, chans)
    gain = lax.all_gather(gate_gain, "tensor", axis=0).reshape(ways, 1, chans)
    l0, l1 = lengths[0, 0], lengths[0, 1]
    starts = jnp.stack([jnp.zeros_like(l0), l0, l0 + l1]) - way * rows

    x = tokens.astype(F32)
    inverse1 = lax.rsqrt(jnp.mean(x * x, axis=1, keepdims=True) + EPS)
    normed = (x * inverse1 * first_norm_gain).astype(BF16)

    p = project(normed, w3, chans)
    totals = forward_total(p, lower, starts)
    all_totals = lax.all_gather(totals, "tensor", axis=0)
    enter = jnp.zeros((ways, 1, chans), F32)
    seen = jnp.zeros((ways, 1, chans), F32)
    for k in range(ways - 1):
        seen = all_totals[k, :, 0:1] * seen + all_totals[k, :, 1:2]
        enter = jnp.where(way == k + 1, seen, enter)
    state, mixed, lam_sum = forward_scan(p, lower, gain, starts, enter)

    resid, middle = branch(mixed, w_out_all, tokens, feedforward_gain.reshape(1, width))
    hidden, act, slope = feed_up(middle, w_up_all, w_glu_all)

    def halves(array):
        cut = array.reshape(rows, chips, 2, width // groups)
        pick = lambda c: lax.dynamic_index_in_dim(cut, c, 2, False).reshape(rows, width // 2)
        return pick(1 - core), pick(core)

    def swap(array):
        return lax.ppermute(array, "core", SWAP)

    def scatter(array):
        array = lax.psum_scatter(array, "chip", scatter_dimension=0, tiled=True)
        array = array.reshape(array.shape[1:])
        array = lax.psum_scatter(array, "tensor", scatter_dimension=0, tiled=True)
        return array.reshape(array.shape[1:]).astype(F32)

    def grad_rows(left, rights):
        theirs, ours = left
        return scatter(by_rows(ours, rights, swap(by_rows(theirs, rights, None, chips)), chips))

    def grad_cols(left, right):
        theirs, ours = right
        return scatter(by_cols(left, ours, swap(by_cols(left, theirs, None, chips)), chips))

    grad_w_down = grad_cols(hidden, halves(cotangent))
    output = feed_down(hidden, w_down_all, resid)

    g_up, g_glu = hidden_grad(cotangent, w_down_all, act, slope)
    middle_halves = halves(middle)
    grad_w_up = grad_rows(middle_halves, [g_up])
    grad_w_glu = grad_rows(middle_halves, [g_glu])
    g_middle = back([g_up, g_glu], [w_up_all, w_glu_all], [0, 0], units)

    inverse2 = lax.rsqrt(jnp.mean(resid * resid, axis=1, keepdims=True) + EPS)
    unit2 = resid * inverse2
    mlp_gain_part = jnp.sum(g_middle * unit2, axis=0)
    g_resid = cotangent.astype(F32) + norm_pullback(g_middle, unit2, inverse2, feedforward_gain)
    g_branch = g_resid.astype(BF16)
    grad_w_out = grad_cols(mixed, halves(g_branch))
    g_mixed = mixed_grad(g_branch, w_out_all)

    g_state, g_gate, gain_part, back_totals = backward_total(p, state, g_mixed, lower, gain, starts)
    all_back = lax.all_gather(back_totals, "tensor", axis=0)
    after = jnp.zeros((ways, 1, chans), F32)
    seen = jnp.zeros((ways, 1, chans), F32)
    for k in range(ways - 1, 0, -1):
        seen = all_totals[k, :, 0:1] * seen + all_back[k]
        after = jnp.where(way == k - 1, seen, after)
    g_in, g_forget, lower_part = backward_scan(p, state, g_state, lower, starts, enter, after)

    normed_halves = halves(normed)
    grad_three = grad_rows(normed_halves, [g_in, g_forget, g_gate])
    g_normed = back([g_in, g_forget, g_gate], [w3, w3, w3], [0, 1, 2], chans)

    unit1 = x * inverse1
    norm_gain_part = jnp.sum(g_normed * unit1, axis=0)
    token_gradient = g_resid + norm_pullback(g_normed, unit1, inverse1, first_norm_gain)

    small = jnp.stack(
        [
            norm_gain_part,
            mlp_gain_part,
            jnp.sum(gain_part, axis=1).reshape(width),
            jnp.sum(lower_part, axis=1).reshape(width),
            jnp.sum(lam_sum, axis=1).reshape(width),
        ]
    )
    small = lax.psum(small, every)
    mean_forget = jnp.sum(small[4]) / (rows * ways * groups * width)
    return (
        output,
        token_gradient,
        small[0],
        grad_three[:, :chans],
        grad_three[:, chans : 2 * chans],
        grad_three[:, 2 * chans :],
        small[3],
        small[2],
        grad_w_out,
        small[1],
        grad_w_up,
        grad_w_glu,
        grad_w_down,
        mean_forget,
    )


def solution(mesh):
    groups, ways = mesh.shape["dp"], mesh.shape["tensor"]
    parts = Mesh(mesh.devices.reshape(groups // 2, 2, ways), ("chip", "core", "tensor"))
    dp = ("chip", "core")
    tokens = P(("chip", "core", "tensor"), None)
    return jax.shard_map(
        local,
        mesh=parts,
        in_specs=(
            tokens,
            P(dp, None),
            P(),
            P(None, "tensor"),
            P(None, "tensor"),
            P(None, "tensor"),
            P("tensor"),
            P("tensor"),
            P("tensor", None),
            P(),
            P(None, "tensor"),
            P(None, "tensor"),
            P("tensor", None),
            tokens,
        ),
        out_specs=(
            tokens,
            tokens,
            P(),
            P(dp, "tensor"),
            P(dp, "tensor"),
            P(dp, "tensor"),
            P(),
            P(),
            P("tensor", dp),
            P(),
            P(dp, "tensor"),
            P(dp, "tensor"),
            P("tensor", dp),
            P(),
        ),
        check_vma=False,
    )
```

```python
import functools

import jax
import jax.numpy as jnp
from jax import lax
from jax.experimental import pallas as pl
from jax.experimental.pallas import tpu as pltpu
from jax.sharding import Mesh
from jax.sharding import PartitionSpec as P

EPS = 1e-06
VMEM_LIMIT = 60 * 1024 * 1024
F32 = jnp.float32
BF16 = jnp.bfloat16
MESH = pl.DeviceIdType.MESH
SPLITS = (True, True, True, True, True)


def params(**kw):
    return pltpu.CompilerParams(vmem_limit_bytes=VMEM_LIMIT, **kw)


def nn(left, right):
    return lax.dot_general(left, right, (((1,), (0,)), ((), ())), preferred_element_type=F32)


def nt(left, right):
    return lax.dot_general(left, right, (((1,), (1,)), ((), ())), preferred_element_type=F32)


def tn(left, right):
    return lax.dot_general(left, right, (((0,), (0,)), ((), ())), preferred_element_type=F32)


def sigmoid(v):
    return jax.nn.sigmoid(v)


def whole(shape):
    zeros = (0,) * len(shape)
    return pl.BlockSpec(shape, lambda *_: zeros)


GATHER_SLOTS = 9


def gather_kernel(n, ways, *refs):
    ins, outs, held = refs[:n], refs[n : 2 * n], refs[2 * n : 3 * n]
    in_sem, own_sem, send_sem, recv_sem = refs[3 * n :]
    way = lax.axis_index("tensor")
    chip = lax.axis_index("chip")
    core = lax.axis_index("core")
    chip_x = chip + 1 - 2 * lax.rem(chip, 2)
    chip_y = lax.rem(chip + 2, 4)
    chip_d = 3 - chip
    here = chip * 2 + core
    over_x, over_y, over_d = chip_x * 2 + core, chip_y * 2 + core, chip_d * 2 + core
    x_id, y_id, core_id = {"chip": chip_x}, {"chip": chip_y}, {"core": 1 - core}

    barrier = pltpu.get_barrier_semaphore()
    for target in (x_id, y_id, core_id):
        pl.semaphore_signal(barrier, inc=1, device_id=target, device_id_type=MESH)

    @pl.when(way > 0)
    def _():
        pl.semaphore_signal(barrier, inc=1, device_id={"tensor": way - 1}, device_id_type=MESH)

    @pl.when(way < ways - 1)
    def _():
        pl.semaphore_signal(barrier, inc=1, device_id={"tensor": way + 1}, device_id_type=MESH)

    ends = jnp.where(way == 0, 1, 0) + jnp.where(way == ways - 1, 1, 0)
    pl.semaphore_wait(barrier, 5 - ends)

    def piece(k, shard, owner, part=None):
        tall = ins[k].shape[0] // 8
        start, size = owner * tall, tall
        if part is not None:
            size = tall // 2
            start = start + part * size
        return outs[k].at[shard, pl.ds(pl.multiple_of(start, 8), size)]

    def copy(src, dst, k, kind, slot, target):
        return pltpu.make_async_remote_copy(
            src_ref=src,
            dst_ref=dst,
            send_sem=send_sem.at[k, kind, slot],
            recv_sem=recv_sem.at[k, kind, slot],
            device_id=target,
            device_id_type=MESH,
        )

    def along(block, k, kind, slot, target):
        return copy(block, block, k, kind, slot, target)

    def first(k, up):
        tall = ins[k].shape[0] // 8
        src = ins[k].at[pl.ds(pl.multiple_of(here * tall, 8), tall)]
        return copy(src, piece(k, way, here), k, 0 if up else 1, 0, {"tensor": way + (1 if up else -1)})

    def guard(hop, up):
        arrives = way >= hop if up else way + hop < ways
        goes_on = jnp.logical_and(arrives, way < ways - 1) if up else jnp.logical_and(arrives, way > 0)
        return arrives, goes_on

    def shard_of(hop, up):
        return way - hop if up else way + hop

    def z_copy(k, hop, up):
        kind = 2 * (hop - 1) + (0 if up else 1)
        return along(piece(k, shard_of(hop, up), here), k, kind, 0, {"tensor": way + (1 if up else -1)})

    def z_next(k, hop, up):
        kind = 2 * hop + (0 if up else 1)
        return along(piece(k, shard_of(hop, up), here), k, kind, 0, {"tensor": way + (1 if up else -1)})

    def plane(k, hop, up):
        kind = 2 * (hop - 1) + (0 if up else 1)
        s = shard_of(hop, up)
        make = lambda block, slot, target: (lambda: along(block, k, kind, slot, target))
        return dict(
            x=make(piece(k, s, here), 1, x_id),
            y=make(piece(k, s, here), 2, y_id),
            dy=make(piece(k, s, over_x, 0), 3, y_id),
            dx=make(piece(k, s, over_y, 1), 4, x_id),
            c0=make(piece(k, s, here), 5, core_id),
            c1=make(piece(k, s, over_x), 6, core_id),
            c2=make(piece(k, s, over_y), 7, core_id),
            c3=make(piece(k, s, over_d), 8, core_id),
        )

    def both(fn):
        for up in (True, False):
            fn(up)

    def start_own(k):
        @pl.when(way < ways - 1)
        def _():
            first(k, True).start()

        @pl.when(way > 0)
        def _():
            first(k, False).start()

    def stage1(k, hop):
        def run(up):
            arrives, goes_on = guard(hop, up)

            @pl.when(arrives)
            def _():
                z_copy(k, hop, up).wait_recv()
                to = plane(k, hop, up)
                to["x"]().start()
                to["y"]().start()
                to["c0"]().start()

            if hop < ways - 1:

                @pl.when(goes_on)
                def _():
                    z_next(k, hop, up).start()

        both(run)

    def stage2(k, hop):
        def run(up):
            @pl.when(guard(hop, up)[0])
            def _():
                to = plane(k, hop, up)
                to["x"]().wait_recv()
                to["dy"]().start()
                to["c1"]().start()
                to["y"]().wait_recv()
                to["dx"]().start()
                to["c2"]().start()

        both(run)

    def stage3(k, hop):
        def run(up):
            @pl.when(guard(hop, up)[0])
            def _():
                to = plane(k, hop, up)
                to["dy"]().wait_recv()
                to["dx"]().wait_recv()
                to["c3"]().start()

        both(run)

    def finish(k, hop):
        def run(up):
            arrives, goes_on = guard(hop, up)

            @pl.when(arrives)
            def _():
                to = plane(k, hop, up)
                for name in ("c0", "c1", "c2", "c3"):
                    to[name]().wait_recv()
                for name in to:
                    to[name]().wait_send()

            if hop < ways - 1:

                @pl.when(goes_on)
                def _():
                    z_next(k, hop, up).wait_send()

        both(run)

    steps = [(k, hop) for k in range(n) for hop in range(1, ways)]
    start_own(0)
    load = lambda k: pltpu.make_async_copy(ins[k], held[k], in_sem.at[k])
    own = lambda k: pltpu.make_async_copy(held[k], outs[k].at[way], own_sem.at[k])
    for k in range(n):
        load(k).start()
    for i in range(len(steps) + 2):
        if i < len(steps):
            k, hop = steps[i]
            if hop == 1:
                load(k).wait()
                own(k).start()
                if k + 1 < n:
                    start_own(k + 1)
            stage1(k, hop)
        if 0 <= i - 1 < len(steps):
            stage2(*steps[i - 1])
        if 0 <= i - 2 < len(steps):
            stage3(*steps[i - 2])
    for k in range(n):
        own(k).wait()

        @pl.when(way < ways - 1)
        def _():
            first(k, True).wait_send()

        @pl.when(way > 0)
        def _():
            first(k, False).wait_send()

        for hop in range(1, ways):
            finish(k, hop)


def gather_weights(shards, ways):
    n = len(shards)
    any_space = pl.BlockSpec(memory_space=pl.ANY)
    kinds = 2 * (ways - 1)
    return pl.pallas_call(
        functools.partial(gather_kernel, n, ways),
        in_specs=[any_space] * n,
        out_specs=[any_space] * n,
        out_shape=[jax.ShapeDtypeStruct((ways,) + w.shape, w.dtype) for w in shards],
        scratch_shapes=[pltpu.VMEM(w.shape, w.dtype) for w in shards]
        + [
            pltpu.SemaphoreType.DMA((n,)),
            pltpu.SemaphoreType.DMA((n,)),
            pltpu.SemaphoreType.DMA((n, kinds, GATHER_SLOTS)),
            pltpu.SemaphoreType.DMA((n, kinds, GATHER_SLOTS)),
        ],
        compiler_params=params(collective_id=1, has_side_effects=True),
        name="gather_weights",
    )(*shards)


def proj_kernel(x_ref, w_ref, o_ref):
    o_ref[0] = nn(x_ref[...], w_ref[0])


def project(normed, w3, chans):
    rows, width = normed.shape
    ways, _, wide = w3.shape
    return pl.pallas_call(
        proj_kernel,
        grid=(ways, wide // chans),
        in_specs=[
            whole((rows, width)),
            pl.BlockSpec((1, width, chans), lambda t, j: (t, 0, j)),
        ],
        out_specs=pl.BlockSpec((1, rows, chans), lambda t, j: (t, 0, j)),
        out_shape=jax.ShapeDtypeStruct((ways, rows, wide), F32),
        compiler_params=params(),
        name="project",
    )(normed, w3)


def gates(p_in, p_forget, lower, ids, starts):
    sig = sigmoid(p_forget)
    lam = lower + (1.0 - lower) * sig
    fresh = ids == starts[0]
    for s in starts[1:]:
        fresh = jnp.logical_or(fresh, ids == s)
    keep = jnp.where(fresh, 0.0, 1.0)
    return sig, lam, keep


def forward_total_kernel(starts_ref, p_ref, lower_ref, o_ref):
    rows, chans = p_ref.shape[1], p_ref.shape[2] // 2
    lower = lower_ref[0]
    starts = [starts_ref[i] for i in range(starts_ref.shape[0])]
    iota = lax.broadcasted_iota(jnp.int32, (8, chans), 0)

    def step(g, carry):
        total, last = carry
        at = pl.multiple_of(g * 8, 8)
        p_in = p_ref[0, pl.ds(at, 8), :chans]
        p_forget = p_ref[0, pl.ds(at, 8), chans:]
        _, lam, keep = gates(p_in, p_forget, lower, iota + at, starts)
        a = lam * keep
        b = p_in * sigmoid(p_in) * (1.0 - lam)
        for s in (1, 2, 4):
            b = a * pltpu.roll(b, s, 0) + b
            a = a * pltpu.roll(a, s, 0)
        a, b = a[7:8], b[7:8]
        return total * a, a * last + b

    total, last = lax.fori_loop(
        0, rows // 8, step, (jnp.ones((1, chans), F32), jnp.zeros((1, chans), F32)), unroll=2
    )
    o_ref[0, 0:1] = total
    o_ref[0, 1:2] = last


def forward_total(p, lower, starts):
    ways, rows, wide = p.shape
    chans = wide // 3
    return pl.pallas_call(
        forward_total_kernel,
        grid=(ways,),
        in_specs=[
            pl.BlockSpec(memory_space=pltpu.SMEM),
            pl.BlockSpec((1, rows, 2 * chans), lambda t: (t, 0, 0)),
            pl.BlockSpec((1, 1, chans), lambda t: (t, 0, 0)),
        ],
        out_specs=pl.BlockSpec((1, 2, chans), lambda t: (t, 0, 0)),
        out_shape=jax.ShapeDtypeStruct((ways, 2, chans), F32),
        compiler_params=params(),
        name="forward_total",
    )(starts, p, lower)


def forward_scan_kernel(starts_ref, p_ref, lower_ref, gain_ref, enter_ref, state_ref, mixed_ref, lam_ref, held):
    ways, rows, wide = p_ref.shape
    chans = wide // 3
    block = pl.program_id(0)
    starts = [starts_ref[i] for i in range(starts_ref.shape[0])]
    iota = lax.broadcasted_iota(jnp.int32, (8, chans), 0)

    @pl.when(block == 0)
    def _():
        held[...] = enter_ref[...]
        lam_ref[...] = jnp.zeros_like(lam_ref)

    for t in range(ways):
        lower = lower_ref[t]

        def step(g, carry):
            before, lam_sum = carry
            at = pl.multiple_of(g * 8, 8)
            p_in = p_ref[t, pl.ds(at, 8), :chans]
            p_forget = p_ref[t, pl.ds(at, 8), chans : 2 * chans]
            _, lam, keep = gates(p_in, p_forget, lower, iota + (at + block * rows), starts)
            a = lam * keep
            b = p_in * sigmoid(p_in) * (1.0 - lam)
            for s in (1, 2, 4):
                far = iota >= s
                b = jnp.where(far, a * pltpu.roll(b, s, 0) + b, b)
                a = jnp.where(far, a * pltpu.roll(a, s, 0), a)
            state = a * before + b
            state_ref[t, pl.ds(at, 8), :] = state
            return state[7:8], lam_sum + lam

        last, lam_sum = lax.fori_loop(
            0, rows // 8, step, (held[t], jnp.zeros((8, chans), F32)), unroll=2
        )
        held[t] = last
        lam_ref[t] += lam_sum

    squares = jnp.zeros((rows, 1), F32)
    for t in range(ways):
        state = state_ref[t]
        squares += jnp.sum(state * state, axis=1, keepdims=True)
    scale = lax.rsqrt(squares / (ways * chans) + EPS)
    for t in range(ways):
        gate = p_ref[t, :, 2 * chans :]
        mixed = state_ref[t] * scale * gain_ref[t] * (gate * sigmoid(gate))
        mixed_ref[t] = mixed.astype(BF16)


def forward_scan(p, lower, gain, starts, enter):
    ways, rows, wide = p.shape
    chans = wide // 3
    part = min(rows, 128)
    return pl.pallas_call(
        forward_scan_kernel,
        grid=(rows // part,),
        in_specs=[
            pl.BlockSpec(memory_space=pltpu.SMEM),
            pl.BlockSpec((ways, part, wide), lambda i: (0, i, 0)),
            whole((ways, 1, chans)),
            whole((ways, 1, chans)),
            whole((ways, 1, chans)),
        ],
        out_specs=[
            pl.BlockSpec((ways, part, chans), lambda i: (0, i, 0)),
            pl.BlockSpec((ways, part, chans), lambda i: (0, i, 0)),
            whole((ways, 8, chans)),
        ],
        out_shape=[
            jax.ShapeDtypeStruct((ways, rows, chans), F32),
            jax.ShapeDtypeStruct((ways, rows, chans), BF16),
            jax.ShapeDtypeStruct((ways, 8, chans), F32),
        ],
        scratch_shapes=[pltpu.VMEM((ways, 1, chans), F32)],
        compiler_params=params(),
        name="forward_scan",
    )(starts, p, lower, gain, enter)


def backward_total_kernel(
    starts_ref, pf_ref, pg_ref, state_ref, gm_ref, lower_ref, gain_ref,
    gstate_ref, ggate_ref, dgain_ref, total_ref, held,
):
    ways, rows, chans = pf_ref.shape
    step_id = pl.program_id(0)
    block = pl.num_programs(0) - 1 - step_id
    starts = [starts_ref[i] for i in range(starts_ref.shape[0])]
    iota = lax.broadcasted_iota(jnp.int32, (8, chans), 0)
    width = ways * chans

    @pl.when(step_id == 0)
    def _():
        held[...] = jnp.zeros_like(held)
        dgain_ref[...] = jnp.zeros_like(dgain_ref)

    squares = jnp.zeros((rows, 1), F32)
    cross = jnp.zeros((rows, 1), F32)
    for t in range(ways):
        state = state_ref[t]
        gate = pg_ref[t]
        inner = gm_ref[t] * gain_ref[t] * (gate * sigmoid(gate))
        gstate_ref[t] = inner
        squares += jnp.sum(state * state, axis=1, keepdims=True)
        cross += jnp.sum(inner * state, axis=1, keepdims=True)
    scale = lax.rsqrt(squares / width + EPS)
    pull = scale * scale * scale * cross / width
    for t in range(ways):
        state = state_ref[t]
        gate = pg_ref[t]
        sig = sigmoid(gate)
        slope = sig * (1.0 + gate * (1.0 - sig))
        unit = gm_ref[t] * state * scale
        ggate_ref[t] = (unit * gain_ref[t] * slope).astype(BF16)
        dgain_ref[t] += jnp.sum((unit * (gate * sig)).reshape(rows // 8, 8, chans), axis=0)
        gstate_ref[t] = gstate_ref[t] * scale - state * pull

    for t in range(ways):
        lower = lower_ref[t]

        def step(k, last):
            at = pl.multiple_of(rows - 8 - k * 8, 8)
            p_forget = pf_ref[t, pl.ds(at, 8), :]
            _, lam, keep = gates(None, p_forget, lower, iota + (at + block * rows), starts)
            a = lam * keep
            b = a * gstate_ref[t, pl.ds(at, 8), :]
            for s in (1, 2, 4):
                b = a * pltpu.roll(b, 8 - s, 0) + b
                a = a * pltpu.roll(a, 8 - s, 0)
            return a[0:1] * last + b[0:1]

        held[t] = lax.fori_loop(0, rows // 8, step, held[t], unroll=2)
    total_ref[...] = held[...]


def backward_total(p, state, g_mixed, lower, gain, starts):
    ways, rows, wide = p.shape
    chans = wide // 3
    part = min(rows, 128)
    last = rows // part - 1
    back = lambda i: (0, last - i, 0)
    block = pl.BlockSpec((ways, part, chans), back)
    return pl.pallas_call(
        backward_total_kernel,
        grid=(rows // part,),
        in_specs=[
            pl.BlockSpec(memory_space=pltpu.SMEM),
            pl.BlockSpec((ways, part, chans), lambda i: (0, last - i, 1)),
            pl.BlockSpec((ways, part, chans), lambda i: (0, last - i, 2)),
            block,
            block,
            whole((ways, 1, chans)),
            whole((ways, 1, chans)),
        ],
        out_specs=[block, block, whole((ways, 8, chans)), whole((ways, 1, chans))],
        out_shape=[
            jax.ShapeDtypeStruct((ways, rows, chans), F32),
            jax.ShapeDtypeStruct((ways, rows, chans), BF16),
            jax.ShapeDtypeStruct((ways, 8, chans), F32),
            jax.ShapeDtypeStruct((ways, 1, chans), F32),
        ],
        scratch_shapes=[pltpu.VMEM((ways, 1, chans), F32)],
        compiler_params=params(),
        name="backward_total",
    )(starts, p, p, state, g_mixed, lower, gain)


def backward_scan_kernel(
    starts_ref, pi_ref, pf_ref, state_ref, early_ref, gstate_ref, lower_ref, enter_ref, after_ref,
    gin_ref, gforget_ref, dlower_ref, held,
):
    ways, rows, chans = pi_ref.shape
    step_id = pl.program_id(0)
    block = pl.num_programs(0) - 1 - step_id
    starts = [starts_ref[i] for i in range(starts_ref.shape[0])]
    iota = lax.broadcasted_iota(jnp.int32, (8, chans), 0)

    @pl.when(step_id == 0)
    def _():
        held[...] = after_ref[...]
        dlower_ref[...] = jnp.zeros_like(dlower_ref)

    for t in range(ways):
        lower = lower_ref[t]
        first = jnp.where(block == 0, enter_ref[t], early_ref[t, 7:8])

        def eight(at, after, before):
            p_in = pi_ref[t, pl.ds(at, 8), :]
            p_forget = pf_ref[t, pl.ds(at, 8), :]
            grad = gstate_ref[t, pl.ds(at, 8), :]
            state = state_ref[t, pl.ds(at, 8), :]
            sig, lam, keep = gates(None, p_forget, lower, iota + (at + block * rows), starts)
            a = lam * keep
            b = a * grad
            for s in (1, 2, 4):
                near = iota < 8 - s
                b = jnp.where(near, a * pltpu.roll(b, 8 - s, 0) + b, b)
                a = jnp.where(near, a * pltpu.roll(a, 8 - s, 0), a)
            handed = a * after + b
            carry = grad + jnp.where(iota == 7, after, pltpu.roll(handed, 7, 0))
            previous = jnp.where(iota == 0, before, pltpu.roll(state, 1, 0))
            sig_in = sigmoid(p_in)
            act = p_in * sig_in
            g_lam = carry * previous * keep - carry * act
            g_in = carry * (1.0 - lam) * (sig_in * (1.0 + p_in * (1.0 - sig_in)))
            lower_part = g_lam * (1.0 - sig)
            g_forget = lower_part * (1.0 - lower) * sig
            return handed[0:1], g_in, g_forget, lower_part

        def step(k, carry):
            after, total = carry
            at = pl.multiple_of(rows - 16 - k * 16, 16)
            middle = state_ref[t, pl.ds(at, 8), :][7:8]
            ahead = jnp.maximum(at - 8, 0)
            held_before = state_ref[t, pl.ds(pl.multiple_of(ahead, 8), 8), :][7:8]
            before = jnp.where(at == 0, first, held_before)
            after, in_late, forget_late, part_late = eight(pl.multiple_of(at + 8, 8), after, middle)
            after, in_early, forget_early, part_early = eight(at, after, before)
            gin_ref[t, pl.ds(at, 16), :] = jnp.concatenate([in_early, in_late], 0).astype(BF16)
            gforget_ref[t, pl.ds(at, 16), :] = jnp.concatenate([forget_early, forget_late], 0).astype(BF16)
            return after, total + part_late + part_early

        after, total = lax.fori_loop(
            0, rows // 16, step, (held[t], jnp.zeros((8, chans), F32))
        )
        held[t] = after
        dlower_ref[t] += total


def backward_scan(p, state, g_state, lower, starts, enter, after):
    ways, rows, wide = p.shape
    chans = wide // 3
    part = min(rows, 128)
    last = rows // part - 1
    block = pl.BlockSpec((ways, part, chans), lambda i: (0, last - i, 0))
    eights = part // 8
    return pl.pallas_call(
        backward_scan_kernel,
        grid=(rows // part,),
        in_specs=[
            pl.BlockSpec(memory_space=pltpu.SMEM),
            pl.BlockSpec((ways, part, chans), lambda i: (0, last - i, 0)),
            pl.BlockSpec((ways, part, chans), lambda i: (0, last - i, 1)),
            block,
            pl.BlockSpec((ways, 8, chans), lambda i: (0, jnp.maximum((last - i) * eights - 1, 0), 0)),
            block,
            whole((ways, 1, chans)),
            whole((ways, 1, chans)),
            whole((ways, 1, chans)),
        ],
        out_specs=[block, block, whole((ways, 8, chans))],
        out_shape=[
            jax.ShapeDtypeStruct((ways, rows, chans), BF16),
            jax.ShapeDtypeStruct((ways, rows, chans), BF16),
            jax.ShapeDtypeStruct((ways, 8, chans), F32),
        ],
        scratch_shapes=[pltpu.VMEM((ways, 1, chans), F32)],
        compiler_params=params(),
        name="backward_scan",
    )(starts, p, p, state, state, g_state, lower, enter, after)


def branch_kernel(mixed_ref, w_ref, x_ref, gain_ref, resid_ref, middle_ref):
    ways = mixed_ref.shape[0]
    total = x_ref[...].astype(F32)
    acc = nn(mixed_ref[0], w_ref[0])
    for t in range(1, ways):
        acc += nn(mixed_ref[t], w_ref[t])
    resid = total + acc
    resid_ref[...] = resid
    inverse = lax.rsqrt(jnp.mean(resid * resid, axis=1, keepdims=True) + EPS)
    middle_ref[...] = (resid * inverse * gain_ref[...]).astype(BF16)


def branch(mixed, w_out, tokens, gain):
    ways, rows, chans = mixed.shape
    width = tokens.shape[1]
    part = min(rows, 256)
    line = pl.BlockSpec((part, width), lambda i: (i, 0))
    return pl.pallas_call(
        branch_kernel,
        grid=(rows // part,),
        in_specs=[
            pl.BlockSpec((ways, part, chans), lambda i: (0, i, 0)),
            whole((ways, chans, width)),
            line,
            whole((1, width)),
        ],
        out_specs=[line, line],
        out_shape=[
            jax.ShapeDtypeStruct((rows, width), F32),
            jax.ShapeDtypeStruct((rows, width), BF16),
        ],
        compiler_params=params(),
        name="branch",
    )(mixed, w_out, tokens, gain)


def up_kernel(x_ref, up_ref, glu_ref, hidden_ref, act_ref, slope_ref):
    x = x_ref[...]
    glu = nn(x, glu_ref[0])
    sig = sigmoid(glu)
    act = glu * sig
    up = nn(x, up_ref[0])
    hidden_ref[0] = (act * up).astype(BF16)
    act_ref[0] = act.astype(BF16)
    slope_ref[0] = (up * (sig * (1.0 + glu * (1.0 - sig)))).astype(BF16)


def feed_up(middle, w_up, w_glu):
    rows, width = middle.shape
    ways, _, units = w_up.shape
    part = min(rows, 512)
    weights = pl.BlockSpec((1, width, units), lambda t, i: (t, 0, 0))
    out = pl.BlockSpec((1, part, units), lambda t, i: (t, i, 0))
    return pl.pallas_call(
        up_kernel,
        grid=(ways, rows // part),
        in_specs=[pl.BlockSpec((part, width), lambda t, i: (i, 0)), weights, weights],
        out_specs=[out, out, out],
        out_shape=[jax.ShapeDtypeStruct((ways, rows, units), BF16)] * 3,
        compiler_params=params(),
        name="feed_up",
    )(middle, w_up, w_glu)


def down_kernel(h_ref, w_ref, resid_ref, o_ref):
    acc = nn(h_ref[0], w_ref[0])
    for t in range(1, h_ref.shape[0]):
        acc += nn(h_ref[t], w_ref[t])
    o_ref[...] = (resid_ref[...] + acc).astype(BF16)


def feed_down(hidden, w_down, resid):
    ways, rows, units = hidden.shape
    width = w_down.shape[2]
    part = 512
    return pl.pallas_call(
        down_kernel,
        grid=(width // part,),
        in_specs=[
            whole((ways, rows, units)),
            pl.BlockSpec((ways, units, part), lambda j: (0, 0, j)),
            pl.BlockSpec((rows, part), lambda j: (0, j)),
        ],
        out_specs=pl.BlockSpec((rows, part), lambda j: (0, j)),
        out_shape=jax.ShapeDtypeStruct((rows, width), BF16),
        compiler_params=params(),
        name="feed_down",
    )(hidden, w_down, resid)


def hidden_grad_kernel(dy_ref, w_ref, act_ref, slope_ref, gup_ref, gglu_ref):
    g_hidden = nt(dy_ref[...], w_ref[0])
    gup_ref[0] = (g_hidden * act_ref[0].astype(F32)).astype(BF16)
    gglu_ref[0] = (g_hidden * slope_ref[0].astype(F32)).astype(BF16)


def hidden_grad(dy, w_down, act, slope):
    rows, width = dy.shape
    ways, units, _ = w_down.shape
    part = min(rows, 512)
    out = pl.BlockSpec((1, part, units), lambda t, i: (t, i, 0))
    return pl.pallas_call(
        hidden_grad_kernel,
        grid=(ways, rows // part),
        in_specs=[
            pl.BlockSpec((part, width), lambda t, i: (i, 0)),
            pl.BlockSpec((1, units, width), lambda t, i: (t, 0, 0)),
            out,
            out,
        ],
        out_specs=[out, out],
        out_shape=[jax.ShapeDtypeStruct((ways, rows, units), BF16)] * 2,
        compiler_params=params(),
        name="hidden_grad",
    )(dy, w_down, act, slope)


def back_kernel(n, *refs):
    g_refs, w_refs, o_ref = refs[:n], refs[n : 2 * n], refs[2 * n]
    acc = nt(g_refs[0][0], w_refs[0][0])
    for g_ref, w_ref in zip(g_refs[1:], w_refs[1:]):
        acc += nt(g_ref[0], w_ref[0])
    first = pl.program_id(1) == 0

    @pl.when(first)
    def _():
        o_ref[...] = acc

    @pl.when(jnp.logical_not(first))
    def _():
        o_ref[...] += acc


def back(grads, weights, picks, units):
    ways, rows, _ = grads[0].shape
    width = weights[0].shape[1]
    part = min(width, 1024)
    return pl.pallas_call(
        functools.partial(back_kernel, len(grads)),
        grid=(width // part, ways),
        in_specs=[pl.BlockSpec((1, rows, units), lambda j, t: (t, 0, 0)) for _ in grads]
        + [pl.BlockSpec((1, part, units), functools.partial(lambda k, j, t: (t, j, k), k)) for k in picks],
        out_specs=pl.BlockSpec((rows, part), lambda j, t: (0, j)),
        out_shape=jax.ShapeDtypeStruct((rows, width), F32),
        compiler_params=params(),
        name="back",
    )(*grads, *weights)


def mixed_grad_kernel(g_ref, w_ref, o_ref):
    o_ref[0] = nt(g_ref[...], w_ref[0])


def mixed_grad(g_branch, w_out):
    rows, width = g_branch.shape
    ways, chans, _ = w_out.shape
    return pl.pallas_call(
        mixed_grad_kernel,
        grid=(ways,),
        in_specs=[whole((rows, width)), pl.BlockSpec((1, chans, width), lambda t: (t, 0, 0))],
        out_specs=pl.BlockSpec((1, rows, chans), lambda t: (t, 0, 0)),
        out_shape=jax.ShapeDtypeStruct((ways, rows, chans), F32),
        compiler_params=params(),
        name="mixed_grad",
    )(g_branch, w_out)


def columns(ref, at_ref, chips, each):
    picks = [ref[:, pl.ds(pl.multiple_of(at_ref[j] * each, each), each)] for j in range(chips)]
    return jnp.concatenate(picks, axis=1)


def put(outs, adds, j, at, wide, value):
    if len(outs) == 1:
        if adds:
            value = value + adds[0][j, 0, :, at : at + wide].astype(F32)
        outs[0][j, 0, :, at : at + wide] = value.astype(BF16)
        return
    half = value.shape[0] // 2
    far_y, far_x = j // 2, j % 2
    spots = ((0 if far_y else 1, far_x), (2 if far_x else 3, far_y))
    for part, (which, row) in enumerate(spots):
        got = value[part * half : (part + 1) * half]
        if adds:
            got = got + adds[which][row, 0, :, at : at + wide].astype(F32)
        outs[which][row, 0, :, at : at + wide] = got.astype(BF16)


def by_rows_kernel(chips, n, n_out, each, at_ref, left_ref, *refs):
    rights, adds, outs = refs[:n], refs[n : len(refs) - n_out], refs[len(refs) - n_out :]
    left = columns(left_ref, at_ref, chips, each)
    at = 0
    for right_ref in rights:
        wide = right_ref.shape[2]
        acc = tn(left, right_ref[0])
        for j in range(chips):
            put(outs, adds, j, at, wide, acc[j * each : (j + 1) * each])
        at += wide


def by_cols_kernel(chips, n_out, each, at_ref, right_ref, left_ref, *refs):
    adds, outs = refs[: len(refs) - n_out], refs[len(refs) - n_out :]
    acc = tn(left_ref[0], columns(right_ref, at_ref, chips, each))
    for j in range(chips):
        put(outs, adds, j, 0, each, acc[:, j * each : (j + 1) * each])


def weight_grad(kernel, whole_side, parted, tall, wide, at, adds, chips, split, name):
    ways, rows, _ = parted[0].shape
    if split:
        shapes = [(2, ways, tall // 2, wide)] * 4
    else:
        shapes = [(chips, ways, tall, wide)]
    blocks = [pl.BlockSpec((c, 1, h, w), lambda t: (0, t, 0, 0)) for c, _, h, w in shapes]
    adds = list(adds or [])
    return pl.pallas_call(
        kernel,
        grid=(ways,),
        in_specs=[pl.BlockSpec(memory_space=pltpu.SMEM), whole(whole_side.shape)]
        + [pl.BlockSpec((1, rows, p.shape[2]), lambda t: (t, 0, 0)) for p in parted]
        + blocks[: len(adds)],
        out_specs=blocks,
        out_shape=[jax.ShapeDtypeStruct(s, BF16) for s in shapes],
        compiler_params=params(),
        name=name,
    )(at, whole_side, *parted, *adds)


def by_rows(left, rights, at, adds, chips, split):
    each = left.shape[1] // (2 * chips)
    kernel = functools.partial(by_rows_kernel, chips, len(rights), 4 if split else 1, each)
    wide = sum(r.shape[2] for r in rights)
    return weight_grad(kernel, left, rights, each, wide, at, adds, chips, split, "by_rows")


def by_cols(left, right, at, adds, chips, split):
    each = right.shape[1] // (2 * chips)
    kernel = functools.partial(by_cols_kernel, chips, 4 if split else 1, each)
    return weight_grad(kernel, right, [left], left.shape[2], each, at, adds, chips, split, "by_cols")


def norm_pullback(upstream_gradient, unit_rows, inverse_rms, gain_vector):
    scaled_rows = upstream_gradient * gain_vector
    return inverse_rms * (
        scaled_rows - unit_rows * jnp.mean(scaled_rows * unit_rows, axis=1, keepdims=True)
    )


SWAP = ((0, 1), (1, 0))
OVER_X = ((0, 1), (1, 0), (2, 3), (3, 2))
OVER_Y = ((0, 2), (2, 0), (1, 3), (3, 1))


def behind(value, *done):
    return lax.optimization_barrier((value,) + done)[0]


def from_all(value, axis):
    n = lax.axis_size(axis)
    if n > 4:
        return lax.all_gather(value, axis, axis=0)
    me = lax.axis_index(axis)
    seen = [value]
    for k in range(1, n):
        seen.append(lax.ppermute(value, axis, [((i + k) % n, i) for i in range(n)]))
    return lax.dynamic_slice_in_dim(jnp.stack(seen + seen), (n - me) % n, n, 0)


def local(
    tokens,
    lengths,
    first_norm_gain,
    w_in,
    w_forget,
    w_gate,
    lower_bound,
    gate_gain,
    w_out,
    feedforward_gain,
    w_up,
    w_glu,
    w_down,
    cotangent,
):
    rows, width = tokens.shape
    chans = w_in.shape[1]
    units = w_up.shape[1]
    ways = lax.axis_size("tensor")
    chips = lax.axis_size("chip")
    groups = 2 * chips
    way = lax.axis_index("tensor")
    core = lax.axis_index("core")
    chip = lax.axis_index("chip")
    group = chip * 2 + core
    every = ("tensor", "chip", "core")
    square = chips == 4 and ways == 4

    def gather(weights):
        tall = weights.shape[0] // groups
        piece = lax.dynamic_slice_in_dim(weights, group * tall, tall, 0)
        piece = lax.all_gather(piece, every, axis=0, tiled=True)
        return piece.reshape((ways,) + weights.shape)

    vectors = from_all(jnp.stack([lower_bound, gate_gain]), "tensor")
    lower, gain = vectors[:, 0:1], vectors[:, 1:2]
    l0, l1 = lengths[0, 0], lengths[0, 1]
    starts = jnp.stack([jnp.zeros_like(l0), l0, l0 + l1]) - way * rows
    x = tokens.astype(F32)
    inverse1 = lax.rsqrt(jnp.mean(x * x, axis=1, keepdims=True) + EPS)
    normed = (x * inverse1 * first_norm_gain).astype(BF16)

    shards = [jnp.concatenate([w_in, w_forget, w_gate], axis=1), w_out, w_glu, w_up]
    if square:
        w3, w_out_all, w_glu_all, w_up_all = gather_weights(shards, ways)
        w_down_all = gather(behind(w_down, w_out_all))
    else:
        w3, w_out_all, w_glu_all, w_up_all = [gather(w) for w in shards]
        w_down_all = gather(w_down)

    p = project(normed, w3, chans)
    totals = forward_total(p, lower, starts)
    all_totals = from_all(totals, "tensor")
    enter = jnp.zeros((ways, 1, chans), F32)
    seen = jnp.zeros((ways, 1, chans), F32)
    for k in range(ways - 1):
        seen = all_totals[k, :, 0:1] * seen + all_totals[k, :, 1:2]
        enter = jnp.where(way == k + 1, seen, enter)
    state, mixed, lam_sum = forward_scan(p, lower, gain, starts, enter)

    resid, middle = branch(mixed, w_out_all, tokens, feedforward_gain.reshape(1, width))
    hidden, act, slope = feed_up(middle, w_up_all, w_glu_all)

    places = jnp.arange(chips, dtype=jnp.int32)

    def blocks_of(c, split):
        return (jnp.bitwise_xor(places, chip) if split else places) * 2 + c

    def swap(arrays):
        return [lax.ppermute(a, "core", SWAP) for a in arrays]

    def add(a, b):
        return a.astype(F32) + b.astype(F32)

    def scatter(arrays):
        if len(arrays) == 1:
            part = lax.psum_scatter(arrays[0], "chip", scatter_dimension=0, tiled=True)
            part = part.reshape(part.shape[1:])
        else:
            y_send, y_keep, x_send, x_keep = arrays
            from_y = lax.ppermute(y_send, "chip", OVER_Y)
            from_x = lax.ppermute(x_send, "chip", OVER_X)
            upper = add(y_keep[1], from_y[1]).astype(BF16)
            lower_half = add(x_keep[1], from_x[1]).astype(BF16)
            upper = lax.ppermute(upper, "chip", OVER_X)
            lower_half = lax.ppermute(lower_half, "chip", OVER_Y)
            upper = add(add(y_keep[0], from_y[0]), upper).astype(BF16)
            lower_half = add(add(x_keep[0], from_x[0]), lower_half).astype(BF16)
            part = jnp.concatenate([upper, lower_half], axis=1)
        part = lax.psum_scatter(part, "tensor", scatter_dimension=0, tiled=True)
        return part.reshape(part.shape[1:]).astype(F32)

    split_down, split_up, split_glu, split_out, split_three = [square and s for s in SPLITS]
    gy = cotangent

    theirs_down = by_cols(hidden, gy, blocks_of(1 - core, split_down), None, chips, split_down)
    swap_down = swap(theirs_down)
    g_up, g_glu = hidden_grad(behind(gy, *theirs_down), w_down_all, act, slope)
    ours_down = by_cols(behind(hidden, g_up), gy, blocks_of(core, split_down), swap_down, chips, split_down)
    grad_w_down = scatter(ours_down)

    middle_now = behind(middle, *ours_down)
    theirs_up = by_rows(middle_now, [g_up], blocks_of(1 - core, split_up), None, chips, split_up)
    swap_up = swap(theirs_up)
    theirs_glu = by_rows(behind(middle, *theirs_up), [g_glu], blocks_of(1 - core, split_glu), None, chips, split_glu)
    swap_glu = swap(theirs_glu)
    ours_up = by_rows(behind(middle, *theirs_glu), [g_up], blocks_of(core, split_up), swap_up, chips, split_up)
    grad_w_up = scatter(ours_up)
    ours_glu = by_rows(behind(middle, *ours_up), [g_glu], blocks_of(core, split_glu), swap_glu, chips, split_glu)
    grad_w_glu = scatter(ours_glu)
    g_middle = back([behind(g_up, *ours_glu), g_glu], [w_up_all, w_glu_all], [0, 0], units)

    inverse2 = lax.rsqrt(jnp.mean(resid * resid, axis=1, keepdims=True) + EPS)
    unit2 = resid * inverse2
    mlp_gain_part = jnp.sum(g_middle * unit2, axis=0)
    g_resid = cotangent.astype(F32) + norm_pullback(g_middle, unit2, inverse2, feedforward_gain)
    g_branch = g_resid.astype(BF16)
    theirs_out = by_cols(mixed, g_branch, blocks_of(1 - core, split_out), None, chips, split_out)
    swap_out = swap(theirs_out)
    g_mixed = mixed_grad(behind(g_branch, *theirs_out), w_out_all)
    ours_out = by_cols(behind(mixed, g_mixed), g_branch, blocks_of(core, split_out), swap_out, chips, split_out)
    grad_w_out = scatter(ours_out)

    g_state, g_gate, gain_part, back_totals = backward_total(
        p, state, behind(g_mixed, *ours_out), lower, gain, starts
    )
    all_back = from_all(back_totals, "tensor")
    after = jnp.zeros((ways, 1, chans), F32)
    seen = jnp.zeros((ways, 1, chans), F32)
    for k in range(ways - 1, 0, -1):
        seen = all_totals[k, :, 0:1] * seen + all_back[k]
        after = jnp.where(way == k - 1, seen, after)
    g_in, g_forget, lower_part = backward_scan(p, state, g_state, lower, starts, enter, after)

    g_three = [g_in, g_forget, g_gate]
    theirs_three = by_rows(normed, g_three, blocks_of(1 - core, split_three), None, chips, split_three)
    swap_three = swap(theirs_three)
    output = feed_down(behind(hidden, *theirs_three), w_down_all, resid)
    ours_three = by_rows(behind(normed, output), g_three, blocks_of(core, split_three), swap_three, chips, split_three)
    grad_three = scatter(ours_three)
    g_normed = back([behind(g_in, *ours_three), g_forget, g_gate], [w3, w3, w3], [0, 1, 2], chans)

    unit1 = x * inverse1
    norm_gain_part = jnp.sum(g_normed * unit1, axis=0)
    token_gradient = g_resid + norm_pullback(g_normed, unit1, inverse1, first_norm_gain)

    small = jnp.stack(
        [
            norm_gain_part,
            mlp_gain_part,
            jnp.sum(gain_part, axis=1).reshape(width),
            jnp.sum(lower_part, axis=1).reshape(width),
            jnp.sum(lam_sum, axis=1).reshape(width),
        ]
    )
    small = lax.psum(small, every)
    mean_forget = jnp.sum(small[4]) / (rows * ways * groups * width)
    return (
        output,
        token_gradient,
        small[0],
        grad_three[:, :chans],
        grad_three[:, chans : 2 * chans],
        grad_three[:, 2 * chans :],
        small[3],
        small[2],
        grad_w_out,
        small[1],
        grad_w_up,
        grad_w_glu,
        grad_w_down,
        mean_forget,
    )


def solution(mesh):
    groups, ways = mesh.shape["dp"], mesh.shape["tensor"]
    parts = Mesh(mesh.devices.reshape(groups // 2, 2, ways), ("chip", "core", "tensor"))
    dp = ("chip", "core")
    tokens = P(("chip", "core", "tensor"), None)
    return jax.shard_map(
        local,
        mesh=parts,
        in_specs=(
            tokens,
            P(dp, None),
            P(),
            P(None, "tensor"),
            P(None, "tensor"),
            P(None, "tensor"),
            P("tensor"),
            P("tensor"),
            P("tensor", None),
            P(),
            P(None, "tensor"),
            P(None, "tensor"),
            P("tensor", None),
            tokens,
        ),
        out_specs=(
            tokens,
            tokens,
            P(),
            P(dp, "tensor"),
            P(dp, "tensor"),
            P(dp, "tensor"),
            P(),
            P(),
            P("tensor", dp),
            P(),
            P(dp, "tensor"),
            P(dp, "tensor"),
            P("tensor", dp),
            P(),
        ),
        check_vma=False,
    )
```

```python
import functools

import jax
import jax.numpy as jnp
from jax import lax
from jax.experimental import pallas as pl
from jax.experimental.pallas import tpu as pltpu
from jax.sharding import Mesh
from jax.sharding import PartitionSpec as P

EPS = 1e-06
VMEM_LIMIT = 60 * 1024 * 1024
F32 = jnp.float32
BF16 = jnp.bfloat16
MESH = pl.DeviceIdType.MESH
SPLITS = (False, False, False, False, False)


def params(**kw):
    return pltpu.CompilerParams(vmem_limit_bytes=VMEM_LIMIT, **kw)


def nn(left, right):
    return lax.dot_general(left, right, (((1,), (0,)), ((), ())), preferred_element_type=F32)


def nt(left, right):
    return lax.dot_general(left, right, (((1,), (1,)), ((), ())), preferred_element_type=F32)


def tn(left, right):
    return lax.dot_general(left, right, (((0,), (0,)), ((), ())), preferred_element_type=F32)


def sigmoid(v):
    return jax.nn.sigmoid(v)


def whole(shape):
    zeros = (0,) * len(shape)
    return pl.BlockSpec(shape, lambda *_: zeros)


GATHER_SLOTS = 9


def gather_kernel(n, ways, *refs):
    ins, outs, held = refs[:n], refs[n : 2 * n], refs[2 * n : 3 * n]
    in_sem, own_sem, send_sem, recv_sem = refs[3 * n :]
    way = lax.axis_index("tensor")
    chip = lax.axis_index("chip")
    core = lax.axis_index("core")
    chip_x = chip + 1 - 2 * lax.rem(chip, 2)
    chip_y = lax.rem(chip + 2, 4)
    chip_d = 3 - chip
    here = chip * 2 + core
    over_x, over_y, over_d = chip_x * 2 + core, chip_y * 2 + core, chip_d * 2 + core
    x_id, y_id, core_id = {"chip": chip_x}, {"chip": chip_y}, {"core": 1 - core}

    barrier = pltpu.get_barrier_semaphore()
    for target in (x_id, y_id, core_id):
        pl.semaphore_signal(barrier, inc=1, device_id=target, device_id_type=MESH)

    @pl.when(way > 0)
    def _():
        pl.semaphore_signal(barrier, inc=1, device_id={"tensor": way - 1}, device_id_type=MESH)

    @pl.when(way < ways - 1)
    def _():
        pl.semaphore_signal(barrier, inc=1, device_id={"tensor": way + 1}, device_id_type=MESH)

    ends = jnp.where(way == 0, 1, 0) + jnp.where(way == ways - 1, 1, 0)
    pl.semaphore_wait(barrier, 5 - ends)

    def piece(k, shard, owner, part=None):
        tall = ins[k].shape[0] // 8
        start, size = owner * tall, tall
        if part is not None:
            size = tall // 2
            start = start + part * size
        return outs[k].at[shard, pl.ds(pl.multiple_of(start, 8), size)]

    def copy(src, dst, k, kind, slot, target):
        return pltpu.make_async_remote_copy(
            src_ref=src,
            dst_ref=dst,
            send_sem=send_sem.at[k, kind, slot],
            recv_sem=recv_sem.at[k, kind, slot],
            device_id=target,
            device_id_type=MESH,
        )

    def along(block, k, kind, slot, target):
        return copy(block, block, k, kind, slot, target)

    def first(k, up):
        tall = ins[k].shape[0] // 8
        src = ins[k].at[pl.ds(pl.multiple_of(here * tall, 8), tall)]
        return copy(src, piece(k, way, here), k, 0 if up else 1, 0, {"tensor": way + (1 if up else -1)})

    def guard(hop, up):
        arrives = way >= hop if up else way + hop < ways
        goes_on = jnp.logical_and(arrives, way < ways - 1) if up else jnp.logical_and(arrives, way > 0)
        return arrives, goes_on

    def shard_of(hop, up):
        return way - hop if up else way + hop

    def z_copy(k, hop, up):
        kind = 2 * (hop - 1) + (0 if up else 1)
        return along(piece(k, shard_of(hop, up), here), k, kind, 0, {"tensor": way + (1 if up else -1)})

    def z_next(k, hop, up):
        kind = 2 * hop + (0 if up else 1)
        return along(piece(k, shard_of(hop, up), here), k, kind, 0, {"tensor": way + (1 if up else -1)})

    def plane(k, hop, up):
        kind = 2 * (hop - 1) + (0 if up else 1)
        s = shard_of(hop, up)
        make = lambda block, slot, target: (lambda: along(block, k, kind, slot, target))
        return dict(
            x=make(piece(k, s, here), 1, x_id),
            y=make(piece(k, s, here), 2, y_id),
            dy=make(piece(k, s, over_x, 0), 3, y_id),
            dx=make(piece(k, s, over_y, 1), 4, x_id),
            c0=make(piece(k, s, here), 5, core_id),
            c1=make(piece(k, s, over_x), 6, core_id),
            c2=make(piece(k, s, over_y), 7, core_id),
            c3=make(piece(k, s, over_d), 8, core_id),
        )

    def both(fn):
        for up in (True, False):
            fn(up)

    def start_own(k):
        @pl.when(way < ways - 1)
        def _():
            first(k, True).start()

        @pl.when(way > 0)
        def _():
            first(k, False).start()

    def stage1(k, hop):
        def run(up):
            arrives, goes_on = guard(hop, up)

            @pl.when(arrives)
            def _():
                z_copy(k, hop, up).wait_recv()
                to = plane(k, hop, up)
                to["x"]().start()
                to["y"]().start()
                to["c0"]().start()

            if hop < ways - 1:

                @pl.when(goes_on)
                def _():
                    z_next(k, hop, up).start()

        both(run)

    def stage2(k, hop):
        def run(up):
            @pl.when(guard(hop, up)[0])
            def _():
                to = plane(k, hop, up)
                to["x"]().wait_recv()
                to["dy"]().start()
                to["c1"]().start()
                to["y"]().wait_recv()
                to["dx"]().start()
                to["c2"]().start()

        both(run)

    def stage3(k, hop):
        def run(up):
            @pl.when(guard(hop, up)[0])
            def _():
                to = plane(k, hop, up)
                to["dy"]().wait_recv()
                to["dx"]().wait_recv()
                to["c3"]().start()

        both(run)

    def finish(k, hop):
        def run(up):
            arrives, goes_on = guard(hop, up)

            @pl.when(arrives)
            def _():
                to = plane(k, hop, up)
                for name in ("c0", "c1", "c2", "c3"):
                    to[name]().wait_recv()
                for name in to:
                    to[name]().wait_send()

            if hop < ways - 1:

                @pl.when(goes_on)
                def _():
                    z_next(k, hop, up).wait_send()

        both(run)

    steps = [(k, hop) for k in range(n) for hop in range(1, ways)]
    start_own(0)
    load = lambda k: pltpu.make_async_copy(ins[k], held[k], in_sem.at[k])
    own = lambda k: pltpu.make_async_copy(held[k], outs[k].at[way], own_sem.at[k])
    for k in range(n):
        load(k).start()
    for i in range(len(steps) + 2):
        if i < len(steps):
            k, hop = steps[i]
            if hop == 1:
                load(k).wait()
                own(k).start()
                if k + 1 < n:
                    start_own(k + 1)
            stage1(k, hop)
        if 0 <= i - 1 < len(steps):
            stage2(*steps[i - 1])
        if 0 <= i - 2 < len(steps):
            stage3(*steps[i - 2])
    for k in range(n):
        own(k).wait()

        @pl.when(way < ways - 1)
        def _():
            first(k, True).wait_send()

        @pl.when(way > 0)
        def _():
            first(k, False).wait_send()

        for hop in range(1, ways):
            finish(k, hop)


def gather_weights(shards, ways):
    n = len(shards)
    any_space = pl.BlockSpec(memory_space=pl.ANY)
    kinds = 2 * (ways - 1)
    return pl.pallas_call(
        functools.partial(gather_kernel, n, ways),
        in_specs=[any_space] * n,
        out_specs=[any_space] * n,
        out_shape=[jax.ShapeDtypeStruct((ways,) + w.shape, w.dtype) for w in shards],
        scratch_shapes=[pltpu.VMEM(w.shape, w.dtype) for w in shards]
        + [
            pltpu.SemaphoreType.DMA((n,)),
            pltpu.SemaphoreType.DMA((n,)),
            pltpu.SemaphoreType.DMA((n, kinds, GATHER_SLOTS)),
            pltpu.SemaphoreType.DMA((n, kinds, GATHER_SLOTS)),
        ],
        compiler_params=params(collective_id=1, has_side_effects=True),
        name="gather_weights",
    )(*shards)


def proj_kernel(x_ref, w_ref, o_ref):
    o_ref[0] = nn(x_ref[...], w_ref[0])


def project(normed, w3, chans):
    rows, width = normed.shape
    ways, _, wide = w3.shape
    return pl.pallas_call(
        proj_kernel,
        grid=(ways, wide // chans),
        in_specs=[
            whole((rows, width)),
            pl.BlockSpec((1, width, chans), lambda t, j: (t, 0, j)),
        ],
        out_specs=pl.BlockSpec((1, rows, chans), lambda t, j: (t, 0, j)),
        out_shape=jax.ShapeDtypeStruct((ways, rows, wide), F32),
        compiler_params=params(),
        name="project",
    )(normed, w3)


def gates(p_in, p_forget, lower, ids, starts):
    sig = sigmoid(p_forget)
    lam = lower + (1.0 - lower) * sig
    fresh = ids == starts[0]
    for s in starts[1:]:
        fresh = jnp.logical_or(fresh, ids == s)
    keep = jnp.where(fresh, 0.0, 1.0)
    return sig, lam, keep


def forward_total_kernel(starts_ref, p_ref, lower_ref, o_ref):
    rows, chans = p_ref.shape[1], p_ref.shape[2] // 2
    lower = lower_ref[0]
    starts = [starts_ref[i] for i in range(starts_ref.shape[0])]
    iota = lax.broadcasted_iota(jnp.int32, (8, chans), 0)

    def step(g, carry):
        total, last = carry
        at = pl.multiple_of(g * 8, 8)
        p_in = p_ref[0, pl.ds(at, 8), :chans]
        p_forget = p_ref[0, pl.ds(at, 8), chans:]
        _, lam, keep = gates(p_in, p_forget, lower, iota + at, starts)
        a = lam * keep
        b = p_in * sigmoid(p_in) * (1.0 - lam)
        for s in (1, 2, 4):
            b = a * pltpu.roll(b, s, 0) + b
            a = a * pltpu.roll(a, s, 0)
        a, b = a[7:8], b[7:8]
        return total * a, a * last + b

    total, last = lax.fori_loop(
        0, rows // 8, step, (jnp.ones((1, chans), F32), jnp.zeros((1, chans), F32)), unroll=2
    )
    o_ref[0, 0:1] = total
    o_ref[0, 1:2] = last


def forward_total(p, lower, starts):
    ways, rows, wide = p.shape
    chans = wide // 3
    return pl.pallas_call(
        forward_total_kernel,
        grid=(ways,),
        in_specs=[
            pl.BlockSpec(memory_space=pltpu.SMEM),
            pl.BlockSpec((1, rows, 2 * chans), lambda t: (t, 0, 0)),
            pl.BlockSpec((1, 1, chans), lambda t: (t, 0, 0)),
        ],
        out_specs=pl.BlockSpec((1, 2, chans), lambda t: (t, 0, 0)),
        out_shape=jax.ShapeDtypeStruct((ways, 2, chans), F32),
        compiler_params=params(),
        name="forward_total",
    )(starts, p, lower)


def forward_scan_kernel(starts_ref, p_ref, lower_ref, gain_ref, enter_ref, state_ref, mixed_ref, lam_ref, held):
    ways, rows, wide = p_ref.shape
    chans = wide // 3
    block = pl.program_id(0)
    starts = [starts_ref[i] for i in range(starts_ref.shape[0])]
    iota = lax.broadcasted_iota(jnp.int32, (8, chans), 0)

    @pl.when(block == 0)
    def _():
        held[...] = enter_ref[...]
        lam_ref[...] = jnp.zeros_like(lam_ref)

    for t in range(ways):
        lower = lower_ref[t]

        def step(g, carry):
            before, lam_sum = carry
            at = pl.multiple_of(g * 8, 8)
            p_in = p_ref[t, pl.ds(at, 8), :chans]
            p_forget = p_ref[t, pl.ds(at, 8), chans : 2 * chans]
            _, lam, keep = gates(p_in, p_forget, lower, iota + (at + block * rows), starts)
            a = lam * keep
            b = p_in * sigmoid(p_in) * (1.0 - lam)
            for s in (1, 2, 4):
                far = iota >= s
                b = jnp.where(far, a * pltpu.roll(b, s, 0) + b, b)
                a = jnp.where(far, a * pltpu.roll(a, s, 0), a)
            state = a * before + b
            state_ref[t, pl.ds(at, 8), :] = state
            return state[7:8], lam_sum + lam

        last, lam_sum = lax.fori_loop(
            0, rows // 8, step, (held[t], jnp.zeros((8, chans), F32)), unroll=2
        )
        held[t] = last
        lam_ref[t] += lam_sum

    squares = jnp.zeros((rows, 1), F32)
    for t in range(ways):
        state = state_ref[t]
        squares += jnp.sum(state * state, axis=1, keepdims=True)
    scale = lax.rsqrt(squares / (ways * chans) + EPS)
    for t in range(ways):
        gate = p_ref[t, :, 2 * chans :]
        mixed = state_ref[t] * scale * gain_ref[t] * (gate * sigmoid(gate))
        mixed_ref[t] = mixed.astype(BF16)


def forward_scan(p, lower, gain, starts, enter):
    ways, rows, wide = p.shape
    chans = wide // 3
    part = min(rows, 128)
    return pl.pallas_call(
        forward_scan_kernel,
        grid=(rows // part,),
        in_specs=[
            pl.BlockSpec(memory_space=pltpu.SMEM),
            pl.BlockSpec((ways, part, wide), lambda i: (0, i, 0)),
            whole((ways, 1, chans)),
            whole((ways, 1, chans)),
            whole((ways, 1, chans)),
        ],
        out_specs=[
            pl.BlockSpec((ways, part, chans), lambda i: (0, i, 0)),
            pl.BlockSpec((ways, part, chans), lambda i: (0, i, 0)),
            whole((ways, 8, chans)),
        ],
        out_shape=[
            jax.ShapeDtypeStruct((ways, rows, chans), F32),
            jax.ShapeDtypeStruct((ways, rows, chans), BF16),
            jax.ShapeDtypeStruct((ways, 8, chans), F32),
        ],
        scratch_shapes=[pltpu.VMEM((ways, 1, chans), F32)],
        compiler_params=params(),
        name="forward_scan",
    )(starts, p, lower, gain, enter)


def backward_total_kernel(
    starts_ref, pf_ref, pg_ref, state_ref, gm_ref, lower_ref, gain_ref,
    gstate_ref, ggate_ref, dgain_ref, total_ref, held,
):
    ways, rows, chans = pf_ref.shape
    step_id = pl.program_id(0)
    block = pl.num_programs(0) - 1 - step_id
    starts = [starts_ref[i] for i in range(starts_ref.shape[0])]
    iota = lax.broadcasted_iota(jnp.int32, (8, chans), 0)
    width = ways * chans

    @pl.when(step_id == 0)
    def _():
        held[...] = jnp.zeros_like(held)
        dgain_ref[...] = jnp.zeros_like(dgain_ref)

    squares = jnp.zeros((rows, 1), F32)
    cross = jnp.zeros((rows, 1), F32)
    for t in range(ways):
        state = state_ref[t]
        gate = pg_ref[t]
        inner = gm_ref[t] * gain_ref[t] * (gate * sigmoid(gate))
        gstate_ref[t] = inner
        squares += jnp.sum(state * state, axis=1, keepdims=True)
        cross += jnp.sum(inner * state, axis=1, keepdims=True)
    scale = lax.rsqrt(squares / width + EPS)
    pull = scale * scale * scale * cross / width
    for t in range(ways):
        state = state_ref[t]
        gate = pg_ref[t]
        sig = sigmoid(gate)
        slope = sig * (1.0 + gate * (1.0 - sig))
        unit = gm_ref[t] * state * scale
        ggate_ref[t] = (unit * gain_ref[t] * slope).astype(BF16)
        dgain_ref[t] += jnp.sum((unit * (gate * sig)).reshape(rows // 8, 8, chans), axis=0)
        gstate_ref[t] = gstate_ref[t] * scale - state * pull

    for t in range(ways):
        lower = lower_ref[t]

        def step(k, last):
            at = pl.multiple_of(rows - 8 - k * 8, 8)
            p_forget = pf_ref[t, pl.ds(at, 8), :]
            _, lam, keep = gates(None, p_forget, lower, iota + (at + block * rows), starts)
            a = lam * keep
            b = a * gstate_ref[t, pl.ds(at, 8), :]
            for s in (1, 2, 4):
                b = a * pltpu.roll(b, 8 - s, 0) + b
                a = a * pltpu.roll(a, 8 - s, 0)
            return a[0:1] * last + b[0:1]

        held[t] = lax.fori_loop(0, rows // 8, step, held[t], unroll=2)
    total_ref[...] = held[...]


def backward_total(p, state, g_mixed, lower, gain, starts):
    ways, rows, wide = p.shape
    chans = wide // 3
    part = min(rows, 128)
    last = rows // part - 1
    back = lambda i: (0, last - i, 0)
    block = pl.BlockSpec((ways, part, chans), back)
    return pl.pallas_call(
        backward_total_kernel,
        grid=(rows // part,),
        in_specs=[
            pl.BlockSpec(memory_space=pltpu.SMEM),
            pl.BlockSpec((ways, part, chans), lambda i: (0, last - i, 1)),
            pl.BlockSpec((ways, part, chans), lambda i: (0, last - i, 2)),
            block,
            block,
            whole((ways, 1, chans)),
            whole((ways, 1, chans)),
        ],
        out_specs=[block, block, whole((ways, 8, chans)), whole((ways, 1, chans))],
        out_shape=[
            jax.ShapeDtypeStruct((ways, rows, chans), F32),
            jax.ShapeDtypeStruct((ways, rows, chans), BF16),
            jax.ShapeDtypeStruct((ways, 8, chans), F32),
            jax.ShapeDtypeStruct((ways, 1, chans), F32),
        ],
        scratch_shapes=[pltpu.VMEM((ways, 1, chans), F32)],
        compiler_params=params(),
        name="backward_total",
    )(starts, p, p, state, g_mixed, lower, gain)


def backward_scan_kernel(
    starts_ref, pi_ref, pf_ref, state_ref, early_ref, gstate_ref, lower_ref, enter_ref, after_ref,
    gin_ref, gforget_ref, dlower_ref, held,
):
    ways, rows, chans = pi_ref.shape
    step_id = pl.program_id(0)
    block = pl.num_programs(0) - 1 - step_id
    starts = [starts_ref[i] for i in range(starts_ref.shape[0])]
    iota = lax.broadcasted_iota(jnp.int32, (8, chans), 0)

    @pl.when(step_id == 0)
    def _():
        held[...] = after_ref[...]
        dlower_ref[...] = jnp.zeros_like(dlower_ref)

    for t in range(ways):
        lower = lower_ref[t]
        first = jnp.where(block == 0, enter_ref[t], early_ref[t, 7:8])

        def eight(at, after, before):
            p_in = pi_ref[t, pl.ds(at, 8), :]
            p_forget = pf_ref[t, pl.ds(at, 8), :]
            grad = gstate_ref[t, pl.ds(at, 8), :]
            state = state_ref[t, pl.ds(at, 8), :]
            sig, lam, keep = gates(None, p_forget, lower, iota + (at + block * rows), starts)
            a = lam * keep
            b = a * grad
            for s in (1, 2, 4):
                near = iota < 8 - s
                b = jnp.where(near, a * pltpu.roll(b, 8 - s, 0) + b, b)
                a = jnp.where(near, a * pltpu.roll(a, 8 - s, 0), a)
            handed = a * after + b
            carry = grad + jnp.where(iota == 7, after, pltpu.roll(handed, 7, 0))
            previous = jnp.where(iota == 0, before, pltpu.roll(state, 1, 0))
            sig_in = sigmoid(p_in)
            act = p_in * sig_in
            g_lam = carry * previous * keep - carry * act
            g_in = carry * (1.0 - lam) * (sig_in * (1.0 + p_in * (1.0 - sig_in)))
            lower_part = g_lam * (1.0 - sig)
            g_forget = lower_part * (1.0 - lower) * sig
            return handed[0:1], g_in, g_forget, lower_part

        def step(k, carry):
            after, total = carry
            at = pl.multiple_of(rows - 16 - k * 16, 16)
            middle = state_ref[t, pl.ds(at, 8), :][7:8]
            ahead = jnp.maximum(at - 8, 0)
            held_before = state_ref[t, pl.ds(pl.multiple_of(ahead, 8), 8), :][7:8]
            before = jnp.where(at == 0, first, held_before)
            after, in_late, forget_late, part_late = eight(pl.multiple_of(at + 8, 8), after, middle)
            after, in_early, forget_early, part_early = eight(at, after, before)
            gin_ref[t, pl.ds(at, 16), :] = jnp.concatenate([in_early, in_late], 0).astype(BF16)
            gforget_ref[t, pl.ds(at, 16), :] = jnp.concatenate([forget_early, forget_late], 0).astype(BF16)
            return after, total + part_late + part_early

        after, total = lax.fori_loop(
            0, rows // 16, step, (held[t], jnp.zeros((8, chans), F32))
        )
        held[t] = after
        dlower_ref[t] += total


def backward_scan(p, state, g_state, lower, starts, enter, after):
    ways, rows, wide = p.shape
    chans = wide // 3
    part = min(rows, 128)
    last = rows // part - 1
    block = pl.BlockSpec((ways, part, chans), lambda i: (0, last - i, 0))
    eights = part // 8
    return pl.pallas_call(
        backward_scan_kernel,
        grid=(rows // part,),
        in_specs=[
            pl.BlockSpec(memory_space=pltpu.SMEM),
            pl.BlockSpec((ways, part, chans), lambda i: (0, last - i, 0)),
            pl.BlockSpec((ways, part, chans), lambda i: (0, last - i, 1)),
            block,
            pl.BlockSpec((ways, 8, chans), lambda i: (0, jnp.maximum((last - i) * eights - 1, 0), 0)),
            block,
            whole((ways, 1, chans)),
            whole((ways, 1, chans)),
            whole((ways, 1, chans)),
        ],
        out_specs=[block, block, whole((ways, 8, chans))],
        out_shape=[
            jax.ShapeDtypeStruct((ways, rows, chans), BF16),
            jax.ShapeDtypeStruct((ways, rows, chans), BF16),
            jax.ShapeDtypeStruct((ways, 8, chans), F32),
        ],
        scratch_shapes=[pltpu.VMEM((ways, 1, chans), F32)],
        compiler_params=params(),
        name="backward_scan",
    )(starts, p, p, state, state, g_state, lower, enter, after)


def branch_kernel(mixed_ref, w_ref, x_ref, gain_ref, resid_ref, middle_ref):
    ways = mixed_ref.shape[0]
    total = x_ref[...].astype(F32)
    acc = nn(mixed_ref[0], w_ref[0])
    for t in range(1, ways):
        acc += nn(mixed_ref[t], w_ref[t])
    resid = total + acc
    resid_ref[...] = resid
    inverse = lax.rsqrt(jnp.mean(resid * resid, axis=1, keepdims=True) + EPS)
    middle_ref[...] = (resid * inverse * gain_ref[...]).astype(BF16)


def branch(mixed, w_out, tokens, gain):
    ways, rows, chans = mixed.shape
    width = tokens.shape[1]
    part = min(rows, 256)
    line = pl.BlockSpec((part, width), lambda i: (i, 0))
    return pl.pallas_call(
        branch_kernel,
        grid=(rows // part,),
        in_specs=[
            pl.BlockSpec((ways, part, chans), lambda i: (0, i, 0)),
            whole((ways, chans, width)),
            line,
            whole((1, width)),
        ],
        out_specs=[line, line],
        out_shape=[
            jax.ShapeDtypeStruct((rows, width), F32),
            jax.ShapeDtypeStruct((rows, width), BF16),
        ],
        compiler_params=params(),
        name="branch",
    )(mixed, w_out, tokens, gain)


def up_kernel(x_ref, up_ref, glu_ref, hidden_ref, act_ref, slope_ref):
    x = x_ref[...]
    glu = nn(x, glu_ref[0])
    sig = sigmoid(glu)
    act = glu * sig
    up = nn(x, up_ref[0])
    hidden_ref[0] = (act * up).astype(BF16)
    act_ref[0] = act.astype(BF16)
    slope_ref[0] = (up * (sig * (1.0 + glu * (1.0 - sig)))).astype(BF16)


def feed_up(middle, w_up, w_glu):
    rows, width = middle.shape
    ways, _, units = w_up.shape
    part = min(rows, 512)
    weights = pl.BlockSpec((1, width, units), lambda t, i: (t, 0, 0))
    out = pl.BlockSpec((1, part, units), lambda t, i: (t, i, 0))
    return pl.pallas_call(
        up_kernel,
        grid=(ways, rows // part),
        in_specs=[pl.BlockSpec((part, width), lambda t, i: (i, 0)), weights, weights],
        out_specs=[out, out, out],
        out_shape=[jax.ShapeDtypeStruct((ways, rows, units), BF16)] * 3,
        compiler_params=params(),
        name="feed_up",
    )(middle, w_up, w_glu)


def down_kernel(h_ref, w_ref, resid_ref, o_ref):
    acc = nn(h_ref[0], w_ref[0])
    for t in range(1, h_ref.shape[0]):
        acc += nn(h_ref[t], w_ref[t])
    o_ref[...] = (resid_ref[...] + acc).astype(BF16)


def feed_down(hidden, w_down, resid):
    ways, rows, units = hidden.shape
    width = w_down.shape[2]
    part = 512
    return pl.pallas_call(
        down_kernel,
        grid=(width // part,),
        in_specs=[
            whole((ways, rows, units)),
            pl.BlockSpec((ways, units, part), lambda j: (0, 0, j)),
            pl.BlockSpec((rows, part), lambda j: (0, j)),
        ],
        out_specs=pl.BlockSpec((rows, part), lambda j: (0, j)),
        out_shape=jax.ShapeDtypeStruct((rows, width), BF16),
        compiler_params=params(),
        name="feed_down",
    )(hidden, w_down, resid)


def hidden_grad_kernel(dy_ref, w_ref, act_ref, slope_ref, gup_ref, gglu_ref):
    g_hidden = nt(dy_ref[...], w_ref[0])
    gup_ref[0] = (g_hidden * act_ref[0].astype(F32)).astype(BF16)
    gglu_ref[0] = (g_hidden * slope_ref[0].astype(F32)).astype(BF16)


def hidden_grad(dy, w_down, act, slope):
    rows, width = dy.shape
    ways, units, _ = w_down.shape
    part = min(rows, 1024)
    out = pl.BlockSpec((1, part, units), lambda t, i: (t, i, 0))
    return pl.pallas_call(
        hidden_grad_kernel,
        grid=(ways, rows // part),
        in_specs=[
            pl.BlockSpec((part, width), lambda t, i: (i, 0)),
            pl.BlockSpec((1, units, width), lambda t, i: (t, 0, 0)),
            out,
            out,
        ],
        out_specs=[out, out],
        out_shape=[jax.ShapeDtypeStruct((ways, rows, units), BF16)] * 2,
        compiler_params=params(),
        name="hidden_grad",
    )(dy, w_down, act, slope)


def back_kernel(n, *refs):
    g_refs, w_refs, o_ref = refs[:n], refs[n : 2 * n], refs[2 * n]
    acc = nt(g_refs[0][0], w_refs[0][0])
    for g_ref, w_ref in zip(g_refs[1:], w_refs[1:]):
        acc += nt(g_ref[0], w_ref[0])
    first = pl.program_id(1) == 0

    @pl.when(first)
    def _():
        o_ref[...] = acc

    @pl.when(jnp.logical_not(first))
    def _():
        o_ref[...] += acc


def back(grads, weights, picks, units):
    ways, rows, _ = grads[0].shape
    width = weights[0].shape[1]
    part = min(width, 1024)
    return pl.pallas_call(
        functools.partial(back_kernel, len(grads)),
        grid=(width // part, ways),
        in_specs=[pl.BlockSpec((1, rows, units), lambda j, t: (t, 0, 0)) for _ in grads]
        + [pl.BlockSpec((1, part, units), functools.partial(lambda k, j, t: (t, j, k), k)) for k in picks],
        out_specs=pl.BlockSpec((rows, part), lambda j, t: (0, j)),
        out_shape=jax.ShapeDtypeStruct((rows, width), F32),
        compiler_params=params(),
        name="back",
    )(*grads, *weights)


def mixed_grad_kernel(g_ref, w_ref, o_ref):
    o_ref[0] = nt(g_ref[...], w_ref[0])


def mixed_grad(g_branch, w_out):
    rows, width = g_branch.shape
    ways, chans, _ = w_out.shape
    return pl.pallas_call(
        mixed_grad_kernel,
        grid=(ways,),
        in_specs=[whole((rows, width)), pl.BlockSpec((1, chans, width), lambda t: (t, 0, 0))],
        out_specs=pl.BlockSpec((1, rows, chans), lambda t: (t, 0, 0)),
        out_shape=jax.ShapeDtypeStruct((ways, rows, chans), F32),
        compiler_params=params(),
        name="mixed_grad",
    )(g_branch, w_out)


def columns(ref, at_ref, chips, each):
    picks = [ref[:, pl.ds(pl.multiple_of(at_ref[j] * each, each), each)] for j in range(chips)]
    return jnp.concatenate(picks, axis=1)


def put(outs, adds, j, at, wide, value):
    if len(outs[0].shape) == 4 and len(outs) == 1:
        if adds:
            value = value + adds[0][j, 0, :, at : at + wide].astype(F32)
        outs[0][j, 0, :, at : at + wide] = value.astype(BF16)
        return
    half = value.shape[0] // 2
    far_y, far_x = j // 2, j % 2
    spots = ((0 if far_y else 1, far_x), (2 if far_x else 3, far_y))
    for part, (which, row) in enumerate(spots):
        got = value[part * half : (part + 1) * half]
        if adds:
            got = got + adds[0][which, row, 0, :, at : at + wide].astype(F32)
        got = got.astype(BF16)
        if len(outs) == 1:
            outs[0][which, row, 0, :, at : at + wide] = got
        else:
            outs[which][row, 0, :, at : at + wide] = got


def by_rows_kernel(chips, n, each, n_out, at_ref, left_ref, *refs):
    rights, adds, outs = refs[:n], refs[n : len(refs) - n_out], refs[len(refs) - n_out :]
    left = columns(left_ref, at_ref, chips, each)
    at = 0
    for right_ref in rights:
        wide = right_ref.shape[2]
        acc = tn(left, right_ref[0])
        for j in range(chips):
            put(outs, adds, j, at, wide, acc[j * each : (j + 1) * each])
        at += wide


def by_cols_kernel(chips, each, n_out, at_ref, right_ref, left_ref, *refs):
    adds, outs = refs[: len(refs) - n_out], refs[len(refs) - n_out :]
    acc = tn(left_ref[0], columns(right_ref, at_ref, chips, each))
    for j in range(chips):
        put(outs, adds, j, 0, each, acc[:, j * each : (j + 1) * each])


def weight_grad(kernel, whole_side, parted, tall, wide, at, adds, chips, split, name):
    ways, rows, _ = parted[0].shape
    adds = list(adds or [])
    if not split:
        shapes = [(chips, ways, tall, wide)]
    elif adds:
        shapes = [(2, ways, tall // 2, wide)] * 4
    else:
        shapes = [(4, 2, ways, tall // 2, wide)]

    def block(shape):
        front = len(shape) - 3
        return pl.BlockSpec(shape[:front] + (1,) + shape[-2:], lambda t: (0,) * front + (t, 0, 0))

    outs = [block(s) for s in shapes]
    return pl.pallas_call(
        functools.partial(kernel, len(shapes)),
        grid=(ways,),
        in_specs=[pl.BlockSpec(memory_space=pltpu.SMEM), whole(whole_side.shape)]
        + [pl.BlockSpec((1, rows, p.shape[2]), lambda t: (t, 0, 0)) for p in parted]
        + [block(a.shape) for a in adds],
        out_specs=outs,
        out_shape=[jax.ShapeDtypeStruct(s, BF16) for s in shapes],
        compiler_params=params(),
        name=name,
    )(at, whole_side, *parted, *adds)


def by_rows(left, rights, at, adds, chips, split):
    each = left.shape[1] // (2 * chips)
    kernel = functools.partial(by_rows_kernel, chips, len(rights), each)
    wide = sum(r.shape[2] for r in rights)
    return weight_grad(kernel, left, rights, each, wide, at, adds, chips, split, "by_rows")


def by_cols(left, right, at, adds, chips, split):
    each = right.shape[1] // (2 * chips)
    kernel = functools.partial(by_cols_kernel, chips, each)
    return weight_grad(kernel, right, [left], left.shape[2], each, at, adds, chips, split, "by_cols")


def norm_pullback(upstream_gradient, unit_rows, inverse_rms, gain_vector):
    scaled_rows = upstream_gradient * gain_vector
    return inverse_rms * (
        scaled_rows - unit_rows * jnp.mean(scaled_rows * unit_rows, axis=1, keepdims=True)
    )


SWAP = ((0, 1), (1, 0))
OVER_X = ((0, 1), (1, 0), (2, 3), (3, 2))
OVER_Y = ((0, 2), (2, 0), (1, 3), (3, 1))


def behind(value, *done):
    return lax.optimization_barrier((value,) + done)[0]


def from_all(value, axis):
    n = lax.axis_size(axis)
    if n > 4:
        return lax.all_gather(value, axis, axis=0)
    me = lax.axis_index(axis)
    seen = [value]
    for k in range(1, n):
        seen.append(lax.ppermute(value, axis, [((i + k) % n, i) for i in range(n)]))
    return lax.dynamic_slice_in_dim(jnp.stack(seen + seen), (n - me) % n, n, 0)


def local(
    tokens,
    lengths,
    first_norm_gain,
    w_in,
    w_forget,
    w_gate,
    lower_bound,
    gate_gain,
    w_out,
    feedforward_gain,
    w_up,
    w_glu,
    w_down,
    cotangent,
):
    rows, width = tokens.shape
    chans = w_in.shape[1]
    units = w_up.shape[1]
    ways = lax.axis_size("tensor")
    chips = lax.axis_size("chip")
    groups = 2 * chips
    way = lax.axis_index("tensor")
    core = lax.axis_index("core")
    chip = lax.axis_index("chip")
    group = chip * 2 + core
    every = ("tensor", "chip", "core")
    square = chips == 4 and ways == 4

    def gather(weights):
        tall = weights.shape[0] // groups
        piece = lax.dynamic_slice_in_dim(weights, group * tall, tall, 0)
        piece = lax.all_gather(piece, every, axis=0, tiled=True)
        return piece.reshape((ways,) + weights.shape)

    vectors = from_all(jnp.stack([lower_bound, gate_gain]), "tensor")
    lower, gain = vectors[:, 0:1], vectors[:, 1:2]
    l0, l1 = lengths[0, 0], lengths[0, 1]
    starts = jnp.stack([jnp.zeros_like(l0), l0, l0 + l1]) - way * rows
    x = tokens.astype(F32)
    inverse1 = lax.rsqrt(jnp.mean(x * x, axis=1, keepdims=True) + EPS)
    normed = (x * inverse1 * first_norm_gain).astype(BF16)

    shards = [jnp.concatenate([w_in, w_forget, w_gate], axis=1), w_out, w_glu, w_up]
    if square:
        w3, w_out_all, w_glu_all, w_up_all = gather_weights(shards, ways)
        w_down_all = gather(behind(w_down, w_out_all))
    else:
        w3, w_out_all, w_glu_all, w_up_all = [gather(w) for w in shards]
        w_down_all = gather(w_down)

    p = project(normed, w3, chans)
    totals = forward_total(p, lower, starts)
    all_totals = from_all(totals, "tensor")
    enter = jnp.zeros((ways, 1, chans), F32)
    seen = jnp.zeros((ways, 1, chans), F32)
    for k in range(ways - 1):
        seen = all_totals[k, :, 0:1] * seen + all_totals[k, :, 1:2]
        enter = jnp.where(way == k + 1, seen, enter)
    state, mixed, lam_sum = forward_scan(p, lower, gain, starts, enter)

    resid, middle = branch(mixed, w_out_all, tokens, feedforward_gain.reshape(1, width))
    hidden, act, slope = feed_up(middle, w_up_all, w_glu_all)

    places = jnp.arange(chips, dtype=jnp.int32)

    def blocks_of(c, split):
        return (jnp.bitwise_xor(places, chip) if split else places) * 2 + c

    def swap(arrays):
        return [lax.ppermute(a, "core", SWAP) for a in arrays]

    def add(a, b):
        return a.astype(F32) + b.astype(F32)

    class Scatter:
        def begin(self, arrays):
            part = lax.psum_scatter(arrays[0], "chip", scatter_dimension=0, tiled=True)
            self.part = lax.optimization_barrier(part.reshape(part.shape[1:]))
            self.parts = [self.block(0)]

        def block(self, k):
            return lax.dynamic_index_in_dim(self.part, (way + k) % ways, 0, False)

        def send(self, *steps):
            got = [
                lax.ppermute(self.block(k), "tensor", [(i, (i + k) % ways) for i in range(ways)])
                for k in steps
                if k < ways
            ]
            self.parts += got
            return tuple(got)

        def rest(self):
            part = lax.psum_scatter(self.part, "tensor", scatter_dimension=0, tiled=True)
            self.parts = [part.reshape(part.shape[1:])]

        def finish(self):
            return sum(a.astype(F32) for a in self.parts)

    last = [()]

    def run(fn, *arrays):
        out = fn(*lax.optimization_barrier(arrays + last[0])[: len(arrays)])
        last[0] = tuple(jax.tree.leaves(out))
        return out

    ours_at = {s: blocks_of(core, s) for s in (True, False)}
    theirs_at = {s: blocks_of(1 - core, s) for s in (True, False)}

    def rows_grad(split, at, rights, left, adds=None):
        n = len(rights)
        got = lambda left, *more: by_rows(left, more[:n], at[split], more[n:], chips, split)
        return run(got, left, *rights, *(adds or []))

    def cols_grad(split, at, left, right, adds=None):
        got = lambda left, right, *more: by_cols(left, right, at[split], more, chips, split)
        return run(got, left, right, *(adds or []))

    split_down, split_up, split_glu, split_out, split_three = [square and s for s in SPLITS]
    down, up, glu, out, three = [Scatter() for _ in range(5)]
    gy = cotangent

    def beside(arrived):
        last[0] = last[0] + arrived

    def send(scattered, *steps):
        return scattered.send(*steps) if few else ()

    few = ways <= 4

    swapped = swap(cols_grad(split_down, theirs_at, hidden, gy))
    down.begin(cols_grad(split_down, ours_at, hidden, gy, swapped))
    g_up, g_glu = run(hidden_grad, gy, w_down_all, act, slope)
    swapped_up = swap(rows_grad(split_up, theirs_at, [g_up], middle))
    swapped_glu = swap(rows_grad(split_glu, theirs_at, [g_glu], middle))
    up.begin(rows_grad(split_up, ours_at, [g_up], middle, swapped_up))
    glu.begin(rows_grad(split_glu, ours_at, [g_glu], middle, swapped_glu))
    g_middle = run(
        lambda a, b, c, d: back([a, b], [c, d], [0, 0], units), g_up, g_glu, w_up_all, w_glu_all
    )
    def second_norm(resid, g_middle, gy):
        inverse2 = lax.rsqrt(jnp.mean(resid * resid, axis=1, keepdims=True) + EPS)
        unit2 = resid * inverse2
        mlp_gain_part = jnp.sum(g_middle * unit2, axis=0)
        g_resid = gy.astype(F32) + norm_pullback(g_middle, unit2, inverse2, feedforward_gain)
        return mlp_gain_part, g_resid, g_resid.astype(BF16)

    moving = send(down, 1)
    mlp_gain_part, g_resid, g_branch = run(second_norm, resid, g_middle, gy)
    swapped_out = swap(cols_grad(split_out, theirs_at, mixed, g_branch))
    g_mixed = run(mixed_grad, g_branch, w_out_all)
    beside(moving)
    out.begin(cols_grad(split_out, ours_at, mixed, g_branch, swapped_out))
    moving = send(down, 2)
    g_state, g_gate, gain_part, back_totals = run(backward_total, p, state, g_mixed, lower, gain, starts)
    beside(moving)
    all_back = lax.all_gather(back_totals, "tensor", axis=0)
    after = jnp.zeros((ways, 1, chans), F32)
    seen = jnp.zeros((ways, 1, chans), F32)
    for k in range(ways - 1, 0, -1):
        seen = all_totals[k, :, 0:1] * seen + all_back[k]
        after = jnp.where(way == k - 1, seen, after)
    moving = send(down, 3)
    g_in, g_forget, lower_part = run(backward_scan, p, state, g_state, lower, starts, enter, after)
    beside(moving)

    g_three = [g_in, g_forget, g_gate]
    swapped = swap(rows_grad(split_three, theirs_at, g_three, normed))
    three.begin(rows_grad(split_three, ours_at, g_three, normed, swapped))
    moving = send(up, 1, 2, 3)
    output = run(feed_down, hidden, w_down_all, resid)
    beside(moving)
    moving = send(glu, 1)
    g_normed = run(
        lambda a, b, c, w: back([a, b, c], [w, w, w], [0, 1, 2], chans), g_in, g_forget, g_gate, w3
    )
    beside(moving)
    moving = send(glu, 2)

    def first_norm_back(x, g_normed, g_resid):
        x = x.astype(F32)
        inverse1 = lax.rsqrt(jnp.mean(x * x, axis=1, keepdims=True) + EPS)
        unit1 = x * inverse1
        norm_gain_part = jnp.sum(g_normed * unit1, axis=0)
        return norm_gain_part, g_resid + norm_pullback(g_normed, unit1, inverse1, first_norm_gain)

    norm_gain_part, token_gradient = run(first_norm_back, tokens, g_normed, g_resid)
    beside(moving)
    moving = send(glu, 3)

    small = jnp.stack(
        [
            norm_gain_part,
            mlp_gain_part,
            jnp.sum(gain_part, axis=1).reshape(width),
            jnp.sum(lower_part, axis=1).reshape(width),
            jnp.sum(lam_sum, axis=1).reshape(width),
        ]
    )
    moving += send(out, 1, 2, 3)
    small = run(lambda v: lax.psum(v, every), small)
    beside(moving)
    three.part = behind(three.part, *last[0])
    three.rest()
    if not few:
        for s in (down, up, glu, out):
            s.rest()
    grad_w_down, grad_w_up, grad_w_glu, grad_w_out, grad_three = [
        s.finish() for s in (down, up, glu, out, three)
    ]
    mean_forget = jnp.sum(small[4]) / (rows * ways * groups * width)
    return (
        output,
        token_gradient,
        small[0],
        grad_three[:, :chans],
        grad_three[:, chans : 2 * chans],
        grad_three[:, 2 * chans :],
        small[3],
        small[2],
        grad_w_out,
        small[1],
        grad_w_up,
        grad_w_glu,
        grad_w_down,
        mean_forget,
    )


def solution(mesh):
    groups, ways = mesh.shape["dp"], mesh.shape["tensor"]
    parts = Mesh(mesh.devices.reshape(groups // 2, 2, ways), ("chip", "core", "tensor"))
    dp = ("chip", "core")
    tokens = P(("chip", "core", "tensor"), None)
    return jax.shard_map(
        local,
        mesh=parts,
        in_specs=(
            tokens,
            P(dp, None),
            P(),
            P(None, "tensor"),
            P(None, "tensor"),
            P(None, "tensor"),
            P("tensor"),
            P("tensor"),
            P("tensor", None),
            P(),
            P(None, "tensor"),
            P(None, "tensor"),
            P("tensor", None),
            tokens,
        ),
        out_specs=(
            tokens,
            tokens,
            P(),
            P(dp, "tensor"),
            P(dp, "tensor"),
            P(dp, "tensor"),
            P(),
            P(),
            P("tensor", dp),
            P(),
            P(dp, "tensor"),
            P(dp, "tensor"),
            P("tensor", dp),
            P(),
        ),
        check_vma=False,
    )
```

```python
import functools

import jax
import jax.numpy as jnp
from jax import lax
from jax.experimental import pallas as pl
from jax.experimental.pallas import tpu as pltpu
from jax.sharding import Mesh
from jax.sharding import PartitionSpec as P

EPS = 1e-06
VMEM_LIMIT = 60 * 1024 * 1024
F32 = jnp.float32
BF16 = jnp.bfloat16
MESH = pl.DeviceIdType.MESH


def params(**kw):
    return pltpu.CompilerParams(vmem_limit_bytes=VMEM_LIMIT, **kw)


def nn(left, right):
    return lax.dot_general(left, right, (((1,), (0,)), ((), ())), preferred_element_type=F32)


def nt(left, right):
    return lax.dot_general(left, right, (((1,), (1,)), ((), ())), preferred_element_type=F32)


def tn(left, right):
    return lax.dot_general(left, right, (((0,), (0,)), ((), ())), preferred_element_type=F32)


def sigmoid(v):
    return jax.nn.sigmoid(v)


def whole(shape):
    zeros = (0,) * len(shape)
    return pl.BlockSpec(shape, lambda *_: zeros)


GATHER_SLOTS = 9


def gather_kernel(n, ways, *refs):
    ins, outs, held = refs[:n], refs[n : 2 * n], refs[2 * n : 3 * n]
    in_sem, own_sem, send_sem, recv_sem = refs[3 * n :]
    way = lax.axis_index("tensor")
    chip = lax.axis_index("chip")
    core = lax.axis_index("core")
    chip_x = chip + 1 - 2 * lax.rem(chip, 2)
    chip_y = lax.rem(chip + 2, 4)
    chip_d = 3 - chip
    here = chip * 2 + core
    over_x, over_y, over_d = chip_x * 2 + core, chip_y * 2 + core, chip_d * 2 + core
    x_id, y_id, core_id = {"chip": chip_x}, {"chip": chip_y}, {"core": 1 - core}

    barrier = pltpu.get_barrier_semaphore()
    for target in (x_id, y_id, core_id):
        pl.semaphore_signal(barrier, inc=1, device_id=target, device_id_type=MESH)

    @pl.when(way > 0)
    def _():
        pl.semaphore_signal(barrier, inc=1, device_id={"tensor": way - 1}, device_id_type=MESH)

    @pl.when(way < ways - 1)
    def _():
        pl.semaphore_signal(barrier, inc=1, device_id={"tensor": way + 1}, device_id_type=MESH)

    ends = jnp.where(way == 0, 1, 0) + jnp.where(way == ways - 1, 1, 0)
    pl.semaphore_wait(barrier, 5 - ends)

    def piece(k, shard, owner, part=None):
        tall = ins[k].shape[0] // 8
        start, size = owner * tall, tall
        if part is not None:
            size = tall // 2
            start = start + part * size
        return outs[k].at[shard, pl.ds(pl.multiple_of(start, 8), size)]

    def copy(src, dst, k, kind, slot, target):
        return pltpu.make_async_remote_copy(
            src_ref=src,
            dst_ref=dst,
            send_sem=send_sem.at[k, kind, slot],
            recv_sem=recv_sem.at[k, kind, slot],
            device_id=target,
            device_id_type=MESH,
        )

    def along(block, k, kind, slot, target):
        return copy(block, block, k, kind, slot, target)

    def first(k, up):
        tall = ins[k].shape[0] // 8
        src = ins[k].at[pl.ds(pl.multiple_of(here * tall, 8), tall)]
        return copy(src, piece(k, way, here), k, 0 if up else 1, 0, {"tensor": way + (1 if up else -1)})

    def guard(hop, up):
        arrives = way >= hop if up else way + hop < ways
        goes_on = jnp.logical_and(arrives, way < ways - 1) if up else jnp.logical_and(arrives, way > 0)
        return arrives, goes_on

    def shard_of(hop, up):
        return way - hop if up else way + hop

    def z_copy(k, hop, up):
        kind = 2 * (hop - 1) + (0 if up else 1)
        return along(piece(k, shard_of(hop, up), here), k, kind, 0, {"tensor": way + (1 if up else -1)})

    def z_next(k, hop, up):
        kind = 2 * hop + (0 if up else 1)
        return along(piece(k, shard_of(hop, up), here), k, kind, 0, {"tensor": way + (1 if up else -1)})

    def plane(k, hop, up):
        kind = 2 * (hop - 1) + (0 if up else 1)
        s = shard_of(hop, up)
        make = lambda block, slot, target: (lambda: along(block, k, kind, slot, target))
        return dict(
            x=make(piece(k, s, here), 1, x_id),
            y=make(piece(k, s, here), 2, y_id),
            dy=make(piece(k, s, over_x, 0), 3, y_id),
            dx=make(piece(k, s, over_y, 1), 4, x_id),
            c0=make(piece(k, s, here), 5, core_id),
            c1=make(piece(k, s, over_x), 6, core_id),
            c2=make(piece(k, s, over_y), 7, core_id),
            c3=make(piece(k, s, over_d), 8, core_id),
        )

    def both(fn):
        for up in (True, False):
            fn(up)

    def start_own(k):
        @pl.when(way < ways - 1)
        def _():
            first(k, True).start()

        @pl.when(way > 0)
        def _():
            first(k, False).start()

    def stage1(k, hop):
        def run(up):
            arrives, goes_on = guard(hop, up)

            @pl.when(arrives)
            def _():
                z_copy(k, hop, up).wait_recv()
                to = plane(k, hop, up)
                to["x"]().start()
                to["y"]().start()
                to["c0"]().start()

            if hop < ways - 1:

                @pl.when(goes_on)
                def _():
                    z_next(k, hop, up).start()

        both(run)

    def stage2(k, hop):
        def run(up):
            @pl.when(guard(hop, up)[0])
            def _():
                to = plane(k, hop, up)
                to["x"]().wait_recv()
                to["dy"]().start()
                to["c1"]().start()
                to["y"]().wait_recv()
                to["dx"]().start()
                to["c2"]().start()

        both(run)

    def stage3(k, hop):
        def run(up):
            @pl.when(guard(hop, up)[0])
            def _():
                to = plane(k, hop, up)
                to["dy"]().wait_recv()
                to["dx"]().wait_recv()
                to["c3"]().start()

        both(run)

    def finish(k, hop):
        def run(up):
            arrives, goes_on = guard(hop, up)

            @pl.when(arrives)
            def _():
                to = plane(k, hop, up)
                for name in ("c0", "c1", "c2", "c3"):
                    to[name]().wait_recv()
                for name in to:
                    to[name]().wait_send()

            if hop < ways - 1:

                @pl.when(goes_on)
                def _():
                    z_next(k, hop, up).wait_send()

        both(run)

    steps = [(k, hop) for k in range(n) for hop in range(1, ways)]
    start_own(0)
    load = lambda k: pltpu.make_async_copy(ins[k], held[k], in_sem.at[k])
    own = lambda k: pltpu.make_async_copy(held[k], outs[k].at[way], own_sem.at[k])
    for k in range(n):
        load(k).start()
    for i in range(len(steps) + 4):
        if i < len(steps):
            k, hop = steps[i]
            if hop == 1:
                load(k).wait()
                own(k).start()
                if k + 1 < n:
                    start_own(k + 1)
            stage1(k, hop)
        if 0 <= i - 2 < len(steps):
            stage2(*steps[i - 2])
        if 0 <= i - 4 < len(steps):
            stage3(*steps[i - 4])
    for k in range(n):
        own(k).wait()

        @pl.when(way < ways - 1)
        def _():
            first(k, True).wait_send()

        @pl.when(way > 0)
        def _():
            first(k, False).wait_send()

        for hop in range(1, ways):
            finish(k, hop)


def gather_weights(shards, ways):
    n = len(shards)
    any_space = pl.BlockSpec(memory_space=pl.ANY)
    kinds = 2 * (ways - 1)
    return pl.pallas_call(
        functools.partial(gather_kernel, n, ways),
        in_specs=[any_space] * n,
        out_specs=[any_space] * n,
        out_shape=[jax.ShapeDtypeStruct((ways,) + w.shape, w.dtype) for w in shards],
        scratch_shapes=[pltpu.VMEM(w.shape, w.dtype) for w in shards]
        + [
            pltpu.SemaphoreType.DMA((n,)),
            pltpu.SemaphoreType.DMA((n,)),
            pltpu.SemaphoreType.DMA((n, kinds, GATHER_SLOTS)),
            pltpu.SemaphoreType.DMA((n, kinds, GATHER_SLOTS)),
        ],
        compiler_params=params(collective_id=1, has_side_effects=True),
        name="gather_weights",
    )(*shards)


def proj_kernel(x_ref, in_ref, forget_ref, gate_ref, o_ref):
    for j, w_ref in enumerate((in_ref, forget_ref, gate_ref)):

        @pl.when(pl.program_id(1) == j)
        def _(w_ref=w_ref):
            o_ref[0] = nn(x_ref[...], w_ref[0])


def project(normed, w_in, w_forget, w_gate):
    rows, width = normed.shape
    ways, _, chans = w_in.shape

    def weights(k):
        following = lambda t, j: jnp.where(j > k, jnp.minimum(t + 1, ways - 1), t)
        return pl.BlockSpec((1, width, chans), lambda t, j: (following(t, j), 0, 0))

    return pl.pallas_call(
        proj_kernel,
        grid=(ways, 3),
        in_specs=[whole((rows, width)), weights(0), weights(1), weights(2)],
        out_specs=pl.BlockSpec((1, rows, chans), lambda t, j: (t, 0, j)),
        out_shape=jax.ShapeDtypeStruct((ways, rows, 3 * chans), F32),
        compiler_params=params(),
        name="project",
    )(normed, w_in, w_forget, w_gate)


def gates(p_in, p_forget, lower, ids, starts):
    sig = sigmoid(p_forget)
    lam = lower + (1.0 - lower) * sig
    fresh = ids == starts[0]
    for s in starts[1:]:
        fresh = jnp.logical_or(fresh, ids == s)
    keep = jnp.where(fresh, 0.0, 1.0)
    return sig, lam, keep


def forward_total_kernel(starts_ref, p_ref, lower_ref, o_ref):
    rows, chans = p_ref.shape[1], p_ref.shape[2] // 2
    lower = lower_ref[0]
    starts = [starts_ref[i] for i in range(starts_ref.shape[0])]
    iota = lax.broadcasted_iota(jnp.int32, (8, chans), 0)

    def step(g, carry):
        total, last = carry
        at = pl.multiple_of(g * 8, 8)
        p_in = p_ref[0, pl.ds(at, 8), :chans]
        p_forget = p_ref[0, pl.ds(at, 8), chans:]
        _, lam, keep = gates(p_in, p_forget, lower, iota + at, starts)
        a = lam * keep
        b = p_in * sigmoid(p_in) * (1.0 - lam)
        for s in (1, 2, 4):
            b = a * pltpu.roll(b, s, 0) + b
            a = a * pltpu.roll(a, s, 0)
        a, b = a[7:8], b[7:8]
        return total * a, a * last + b

    total, last = lax.fori_loop(
        0, rows // 8, step, (jnp.ones((1, chans), F32), jnp.zeros((1, chans), F32)), unroll=2
    )
    o_ref[0, 0:1] = total
    o_ref[0, 1:2] = last


def forward_total(p, lower, starts):
    ways, rows, wide = p.shape
    chans = wide // 3
    return pl.pallas_call(
        forward_total_kernel,
        grid=(ways,),
        in_specs=[
            pl.BlockSpec(memory_space=pltpu.SMEM),
            pl.BlockSpec((1, rows, 2 * chans), lambda t: (t, 0, 0)),
            pl.BlockSpec((1, 1, chans), lambda t: (t, 0, 0)),
        ],
        out_specs=pl.BlockSpec((1, 2, chans), lambda t: (t, 0, 0)),
        out_shape=jax.ShapeDtypeStruct((ways, 2, chans), F32),
        compiler_params=params(),
        name="forward_total",
    )(starts, p, lower)


def forward_scan_kernel(starts_ref, p_ref, lower_ref, gain_ref, enter_ref, state_ref, mixed_ref, lam_ref, held):
    ways, rows, wide = p_ref.shape
    chans = wide // 3
    block = pl.program_id(0)
    starts = [starts_ref[i] for i in range(starts_ref.shape[0])]
    iota = lax.broadcasted_iota(jnp.int32, (8, chans), 0)

    @pl.when(block == 0)
    def _():
        held[...] = enter_ref[...]
        lam_ref[...] = jnp.zeros_like(lam_ref)

    for t in range(ways):
        lower = lower_ref[t]

        def step(g, carry):
            before, lam_sum = carry
            at = pl.multiple_of(g * 8, 8)
            p_in = p_ref[t, pl.ds(at, 8), :chans]
            p_forget = p_ref[t, pl.ds(at, 8), chans : 2 * chans]
            _, lam, keep = gates(p_in, p_forget, lower, iota + (at + block * rows), starts)
            a = lam * keep
            b = p_in * sigmoid(p_in) * (1.0 - lam)
            for s in (1, 2, 4):
                far = iota >= s
                b = jnp.where(far, a * pltpu.roll(b, s, 0) + b, b)
                a = jnp.where(far, a * pltpu.roll(a, s, 0), a)
            state = a * before + b
            state_ref[t, pl.ds(at, 8), :] = state
            return state[7:8], lam_sum + lam

        last, lam_sum = lax.fori_loop(
            0, rows // 8, step, (held[t], jnp.zeros((8, chans), F32)), unroll=2
        )
        held[t] = last
        lam_ref[t] += lam_sum

    squares = jnp.zeros((rows, 1), F32)
    for t in range(ways):
        state = state_ref[t]
        squares += jnp.sum(state * state, axis=1, keepdims=True)
    scale = lax.rsqrt(squares / (ways * chans) + EPS)
    for t in range(ways):
        gate = p_ref[t, :, 2 * chans :]
        mixed = state_ref[t] * scale * gain_ref[t] * (gate * sigmoid(gate))
        mixed_ref[t] = mixed.astype(BF16)


def forward_scan(p, lower, gain, starts, enter):
    ways, rows, wide = p.shape
    chans = wide // 3
    part = min(rows, 128)
    return pl.pallas_call(
        forward_scan_kernel,
        grid=(rows // part,),
        in_specs=[
            pl.BlockSpec(memory_space=pltpu.SMEM),
            pl.BlockSpec((ways, part, wide), lambda i: (0, i, 0)),
            whole((ways, 1, chans)),
            whole((ways, 1, chans)),
            whole((ways, 1, chans)),
        ],
        out_specs=[
            pl.BlockSpec((ways, part, chans), lambda i: (0, i, 0)),
            pl.BlockSpec((ways, part, chans), lambda i: (0, i, 0)),
            whole((ways, 8, chans)),
        ],
        out_shape=[
            jax.ShapeDtypeStruct((ways, rows, chans), F32),
            jax.ShapeDtypeStruct((ways, rows, chans), BF16),
            jax.ShapeDtypeStruct((ways, 8, chans), F32),
        ],
        scratch_shapes=[pltpu.VMEM((ways, 1, chans), F32)],
        compiler_params=params(),
        name="forward_scan",
    )(starts, p, lower, gain, enter)


def backward_total_kernel(
    starts_ref, pf_ref, pg_ref, state_ref, gm_ref, lower_ref, gain_ref,
    gstate_ref, ggate_ref, dgain_ref, total_ref, held,
):
    ways, rows, chans = pf_ref.shape
    step_id = pl.program_id(0)
    block = pl.num_programs(0) - 1 - step_id
    starts = [starts_ref[i] for i in range(starts_ref.shape[0])]
    iota = lax.broadcasted_iota(jnp.int32, (8, chans), 0)
    width = ways * chans

    @pl.when(step_id == 0)
    def _():
        held[...] = jnp.zeros_like(held)
        dgain_ref[...] = jnp.zeros_like(dgain_ref)

    squares = jnp.zeros((rows, 1), F32)
    cross = jnp.zeros((rows, 1), F32)
    for t in range(ways):
        state = state_ref[t]
        gate = pg_ref[t]
        inner = gm_ref[t] * gain_ref[t] * (gate * sigmoid(gate))
        gstate_ref[t] = inner
        squares += jnp.sum(state * state, axis=1, keepdims=True)
        cross += jnp.sum(inner * state, axis=1, keepdims=True)
    scale = lax.rsqrt(squares / width + EPS)
    pull = scale * scale * scale * cross / width
    for t in range(ways):
        state = state_ref[t]
        gate = pg_ref[t]
        sig = sigmoid(gate)
        slope = sig * (1.0 + gate * (1.0 - sig))
        unit = gm_ref[t] * state * scale
        ggate_ref[t] = (unit * gain_ref[t] * slope).astype(BF16)
        dgain_ref[t] += jnp.sum((unit * (gate * sig)).reshape(rows // 8, 8, chans), axis=0)
        gstate_ref[t] = gstate_ref[t] * scale - state * pull

    for t in range(ways):
        lower = lower_ref[t]

        def step(k, last):
            at = pl.multiple_of(rows - 8 - k * 8, 8)
            p_forget = pf_ref[t, pl.ds(at, 8), :]
            _, lam, keep = gates(None, p_forget, lower, iota + (at + block * rows), starts)
            a = lam * keep
            b = a * gstate_ref[t, pl.ds(at, 8), :]
            for s in (1, 2, 4):
                b = a * pltpu.roll(b, 8 - s, 0) + b
                a = a * pltpu.roll(a, 8 - s, 0)
            return a[0:1] * last + b[0:1]

        held[t] = lax.fori_loop(0, rows // 8, step, held[t], unroll=2)
    total_ref[...] = held[...]


def backward_total(p, state, g_mixed, lower, gain, starts):
    ways, rows, wide = p.shape
    chans = wide // 3
    part = min(rows, 128)
    last = rows // part - 1
    back = lambda i: (0, last - i, 0)
    block = pl.BlockSpec((ways, part, chans), back)
    return pl.pallas_call(
        backward_total_kernel,
        grid=(rows // part,),
        in_specs=[
            pl.BlockSpec(memory_space=pltpu.SMEM),
            pl.BlockSpec((ways, part, chans), lambda i: (0, last - i, 1)),
            pl.BlockSpec((ways, part, chans), lambda i: (0, last - i, 2)),
            block,
            block,
            whole((ways, 1, chans)),
            whole((ways, 1, chans)),
        ],
        out_specs=[block, block, whole((ways, 8, chans)), whole((ways, 1, chans))],
        out_shape=[
            jax.ShapeDtypeStruct((ways, rows, chans), F32),
            jax.ShapeDtypeStruct((ways, rows, chans), BF16),
            jax.ShapeDtypeStruct((ways, 8, chans), F32),
            jax.ShapeDtypeStruct((ways, 1, chans), F32),
        ],
        scratch_shapes=[pltpu.VMEM((ways, 1, chans), F32)],
        compiler_params=params(),
        name="backward_total",
    )(starts, p, p, state, g_mixed, lower, gain)


def backward_scan_kernel(
    starts_ref, pi_ref, pf_ref, state_ref, early_ref, gstate_ref, lower_ref, enter_ref, after_ref,
    gin_ref, gforget_ref, dlower_ref, held,
):
    ways, rows, chans = pi_ref.shape
    step_id = pl.program_id(0)
    block = pl.num_programs(0) - 1 - step_id
    starts = [starts_ref[i] for i in range(starts_ref.shape[0])]
    iota = lax.broadcasted_iota(jnp.int32, (8, chans), 0)

    @pl.when(step_id == 0)
    def _():
        held[...] = after_ref[...]
        dlower_ref[...] = jnp.zeros_like(dlower_ref)

    for t in range(ways):
        lower = lower_ref[t]
        first = jnp.where(block == 0, enter_ref[t], early_ref[t, 7:8])

        def eight(at, after, before):
            p_in = pi_ref[t, pl.ds(at, 8), :]
            p_forget = pf_ref[t, pl.ds(at, 8), :]
            grad = gstate_ref[t, pl.ds(at, 8), :]
            state = state_ref[t, pl.ds(at, 8), :]
            sig, lam, keep = gates(None, p_forget, lower, iota + (at + block * rows), starts)
            a = lam * keep
            b = a * grad
            for s in (1, 2, 4):
                near = iota < 8 - s
                b = jnp.where(near, a * pltpu.roll(b, 8 - s, 0) + b, b)
                a = jnp.where(near, a * pltpu.roll(a, 8 - s, 0), a)
            handed = a * after + b
            carry = grad + jnp.where(iota == 7, after, pltpu.roll(handed, 7, 0))
            previous = jnp.where(iota == 0, before, pltpu.roll(state, 1, 0))
            sig_in = sigmoid(p_in)
            act = p_in * sig_in
            g_lam = carry * previous * keep - carry * act
            g_in = carry * (1.0 - lam) * (sig_in * (1.0 + p_in * (1.0 - sig_in)))
            lower_part = g_lam * (1.0 - sig)
            g_forget = lower_part * (1.0 - lower) * sig
            return handed[0:1], g_in, g_forget, lower_part

        def step(k, carry):
            after, total = carry
            at = pl.multiple_of(rows - 16 - k * 16, 16)
            middle = state_ref[t, pl.ds(at, 8), :][7:8]
            ahead = jnp.maximum(at - 8, 0)
            held_before = state_ref[t, pl.ds(pl.multiple_of(ahead, 8), 8), :][7:8]
            before = jnp.where(at == 0, first, held_before)
            after, in_late, forget_late, part_late = eight(pl.multiple_of(at + 8, 8), after, middle)
            after, in_early, forget_early, part_early = eight(at, after, before)
            gin_ref[t, pl.ds(at, 16), :] = jnp.concatenate([in_early, in_late], 0).astype(BF16)
            gforget_ref[t, pl.ds(at, 16), :] = jnp.concatenate([forget_early, forget_late], 0).astype(BF16)
            return after, total + part_late + part_early

        after, total = lax.fori_loop(
            0, rows // 16, step, (held[t], jnp.zeros((8, chans), F32))
        )
        held[t] = after
        dlower_ref[t] += total


def backward_scan(p, state, g_state, lower, starts, enter, after):
    ways, rows, wide = p.shape
    chans = wide // 3
    part = min(rows, 128)
    last = rows // part - 1
    block = pl.BlockSpec((ways, part, chans), lambda i: (0, last - i, 0))
    eights = part // 8
    return pl.pallas_call(
        backward_scan_kernel,
        grid=(rows // part,),
        in_specs=[
            pl.BlockSpec(memory_space=pltpu.SMEM),
            pl.BlockSpec((ways, part, chans), lambda i: (0, last - i, 0)),
            pl.BlockSpec((ways, part, chans), lambda i: (0, last - i, 1)),
            block,
            pl.BlockSpec((ways, 8, chans), lambda i: (0, jnp.maximum((last - i) * eights - 1, 0), 0)),
            block,
            whole((ways, 1, chans)),
            whole((ways, 1, chans)),
            whole((ways, 1, chans)),
        ],
        out_specs=[block, block, whole((ways, 8, chans))],
        out_shape=[
            jax.ShapeDtypeStruct((ways, rows, chans), BF16),
            jax.ShapeDtypeStruct((ways, rows, chans), BF16),
            jax.ShapeDtypeStruct((ways, 8, chans), F32),
        ],
        scratch_shapes=[pltpu.VMEM((ways, 1, chans), F32)],
        compiler_params=params(),
        name="backward_scan",
    )(starts, p, p, state, state, g_state, lower, enter, after)


def branch_kernel(mixed_ref, w_ref, x_ref, gain_ref, resid_ref, middle_ref):
    ways = mixed_ref.shape[0]
    total = x_ref[...].astype(F32)
    acc = nn(mixed_ref[0], w_ref[0])
    for t in range(1, ways):
        acc += nn(mixed_ref[t], w_ref[t])
    resid = total + acc
    resid_ref[...] = resid
    inverse = lax.rsqrt(jnp.mean(resid * resid, axis=1, keepdims=True) + EPS)
    middle_ref[...] = (resid * inverse * gain_ref[...]).astype(BF16)


def branch(mixed, w_out, tokens, gain):
    ways, rows, chans = mixed.shape
    width = tokens.shape[1]
    part = min(rows, 256)
    line = pl.BlockSpec((part, width), lambda i: (i, 0))
    return pl.pallas_call(
        branch_kernel,
        grid=(rows // part,),
        in_specs=[
            pl.BlockSpec((ways, part, chans), lambda i: (0, i, 0)),
            whole((ways, chans, width)),
            line,
            whole((1, width)),
        ],
        out_specs=[line, line],
        out_shape=[
            jax.ShapeDtypeStruct((rows, width), F32),
            jax.ShapeDtypeStruct((rows, width), BF16),
        ],
        compiler_params=params(),
        name="branch",
    )(mixed, w_out, tokens, gain)


def up_kernel(x_ref, up_ref, glu_ref, hidden_ref, act_ref, slope_ref):
    x = x_ref[...]
    glu = nn(x, glu_ref[0])
    sig = sigmoid(glu)
    act = glu * sig
    up = nn(x, up_ref[0])
    hidden_ref[0] = (act * up).astype(BF16)
    act_ref[0] = act.astype(BF16)
    slope_ref[0] = (up * (sig * (1.0 + glu * (1.0 - sig)))).astype(BF16)


def feed_up(middle, w_up, w_glu):
    rows, width = middle.shape
    ways, _, units = w_up.shape
    part = min(rows, 512)
    weights = pl.BlockSpec((1, width, units), lambda t, i: (t, 0, 0))
    out = pl.BlockSpec((1, part, units), lambda t, i: (t, i, 0))
    return pl.pallas_call(
        up_kernel,
        grid=(ways, rows // part),
        in_specs=[pl.BlockSpec((part, width), lambda t, i: (i, 0)), weights, weights],
        out_specs=[out, out, out],
        out_shape=[jax.ShapeDtypeStruct((ways, rows, units), BF16)] * 3,
        compiler_params=params(),
        name="feed_up",
    )(middle, w_up, w_glu)


def down_kernel(h_ref, w_ref, resid_ref, o_ref):
    acc = nn(h_ref[0], w_ref[0])
    for t in range(1, h_ref.shape[0]):
        acc += nn(h_ref[t], w_ref[t])
    o_ref[...] = (resid_ref[...] + acc).astype(BF16)


def feed_down(hidden, w_down, resid):
    ways, rows, units = hidden.shape
    width = w_down.shape[2]
    part = 512
    return pl.pallas_call(
        down_kernel,
        grid=(width // part,),
        in_specs=[
            whole((ways, rows, units)),
            pl.BlockSpec((ways, units, part), lambda j: (0, 0, j)),
            pl.BlockSpec((rows, part), lambda j: (0, j)),
        ],
        out_specs=pl.BlockSpec((rows, part), lambda j: (0, j)),
        out_shape=jax.ShapeDtypeStruct((rows, width), BF16),
        compiler_params=params(),
        name="feed_down",
    )(hidden, w_down, resid)


def hidden_grad_kernel(dy_ref, w_ref, act_ref, slope_ref, gup_ref, gglu_ref):
    g_hidden = nt(dy_ref[...], w_ref[0])
    gup_ref[0] = (g_hidden * act_ref[0].astype(F32)).astype(BF16)
    gglu_ref[0] = (g_hidden * slope_ref[0].astype(F32)).astype(BF16)


def hidden_grad(dy, w_down, act, slope):
    rows, width = dy.shape
    ways, units, _ = w_down.shape
    part = min(rows, 1024)
    out = pl.BlockSpec((1, part, units), lambda t, i: (t, i, 0))
    return pl.pallas_call(
        hidden_grad_kernel,
        grid=(ways, rows // part),
        in_specs=[
            pl.BlockSpec((part, width), lambda t, i: (i, 0)),
            pl.BlockSpec((1, units, width), lambda t, i: (t, 0, 0)),
            out,
            out,
        ],
        out_specs=[out, out],
        out_shape=[jax.ShapeDtypeStruct((ways, rows, units), BF16)] * 2,
        compiler_params=params(),
        name="hidden_grad",
    )(dy, w_down, act, slope)


def back_kernel(n, *refs):
    g_refs, w_refs, o_ref = refs[:n], refs[n : 2 * n], refs[2 * n]
    acc = nt(g_refs[0][0], w_refs[0][0])
    for g_ref, w_ref in zip(g_refs[1:], w_refs[1:]):
        acc += nt(g_ref[0], w_ref[0])
    first = pl.program_id(1) == 0

    @pl.when(first)
    def _():
        o_ref[...] = acc

    @pl.when(jnp.logical_not(first))
    def _():
        o_ref[...] += acc


def back(grads, weights, units):
    ways, rows, _ = grads[0].shape
    width = weights[0].shape[1]
    part = min(width, 1024)
    return pl.pallas_call(
        functools.partial(back_kernel, len(grads)),
        grid=(width // part, ways),
        in_specs=[pl.BlockSpec((1, rows, units), lambda j, t: (t, 0, 0)) for _ in grads]
        + [pl.BlockSpec((1, part, units), lambda j, t: (t, j, 0)) for _ in weights],
        out_specs=pl.BlockSpec((rows, part), lambda j, t: (0, j)),
        out_shape=jax.ShapeDtypeStruct((rows, width), F32),
        compiler_params=params(),
        name="back",
    )(*grads, *weights)


def mixed_grad_kernel(g_ref, w_ref, o_ref):
    o_ref[0] = nt(g_ref[...], w_ref[0])


def mixed_grad(g_branch, w_out):
    rows, width = g_branch.shape
    ways, chans, _ = w_out.shape
    return pl.pallas_call(
        mixed_grad_kernel,
        grid=(ways,),
        in_specs=[whole((rows, width)), pl.BlockSpec((1, chans, width), lambda t: (t, 0, 0))],
        out_specs=pl.BlockSpec((1, rows, chans), lambda t: (t, 0, 0)),
        out_shape=jax.ShapeDtypeStruct((ways, rows, chans), F32),
        compiler_params=params(),
        name="mixed_grad",
    )(g_branch, w_out)


def columns(ref, at_ref, chips, each):
    picks = [ref[:, pl.ds(pl.multiple_of(at_ref[j] * each, each), each)] for j in range(chips)]
    return jnp.concatenate(picks, axis=1)


def put(o_ref, adds, j, at, wide, value):
    if adds:
        value = value + adds[0][j, 0, :, at : at + wide].astype(F32)
    o_ref[j, 0, :, at : at + wide] = value.astype(BF16)


def by_rows_kernel(chips, n, each, at_ref, left_ref, *refs):
    rights, adds, o_ref = refs[:n], refs[n:-1], refs[-1]
    left = columns(left_ref, at_ref, chips, each)
    at = 0
    for right_ref in rights:
        wide = right_ref.shape[2]
        acc = tn(left, right_ref[0])
        for j in range(chips):
            put(o_ref, adds, j, at, wide, acc[j * each : (j + 1) * each])
        at += wide


def by_cols_kernel(chips, each, at_ref, right_ref, left_ref, *refs):
    adds, o_ref = refs[:-1], refs[-1]
    acc = tn(left_ref[0], columns(right_ref, at_ref, chips, each))
    for j in range(chips):
        put(o_ref, adds, j, 0, each, acc[:, j * each : (j + 1) * each])


def weight_grad(kernel, whole_side, parted, tall, wide, at, adds, chips, name):
    ways, rows, _ = parted[0].shape
    block = pl.BlockSpec((chips, 1, tall, wide), lambda t: (0, t, 0, 0))
    return pl.pallas_call(
        kernel,
        grid=(ways,),
        in_specs=[pl.BlockSpec(memory_space=pltpu.SMEM), whole(whole_side.shape)]
        + [pl.BlockSpec((1, rows, p.shape[2]), lambda t: (t, 0, 0)) for p in parted]
        + [block for _ in adds],
        out_specs=block,
        out_shape=jax.ShapeDtypeStruct((chips, ways, tall, wide), BF16),
        compiler_params=params(),
        name=name,
    )(at, whole_side, *parted, *adds)


def by_rows(left, rights, at, adds, chips):
    each = left.shape[1] // (2 * chips)
    kernel = functools.partial(by_rows_kernel, chips, len(rights), each)
    wide = sum(r.shape[2] for r in rights)
    return weight_grad(kernel, left, rights, each, wide, at, adds, chips, "by_rows")


def by_cols(left, right, at, adds, chips):
    each = right.shape[1] // (2 * chips)
    kernel = functools.partial(by_cols_kernel, chips, each)
    return weight_grad(kernel, right, [left], left.shape[2], each, at, adds, chips, "by_cols")


def norm_pullback(upstream_gradient, unit_rows, inverse_rms, gain_vector):
    scaled_rows = upstream_gradient * gain_vector
    return inverse_rms * (
        scaled_rows - unit_rows * jnp.mean(scaled_rows * unit_rows, axis=1, keepdims=True)
    )


SWAP = ((0, 1), (1, 0))


def behind(value, *done):
    return lax.optimization_barrier((value,) + done)[0]


def from_all(value, axis):
    n = lax.axis_size(axis)
    if n > 4:
        return lax.all_gather(value, axis, axis=0)
    me = lax.axis_index(axis)
    seen = [value]
    for k in range(1, n):
        seen.append(lax.ppermute(value, axis, [((i + k) % n, i) for i in range(n)]))
    return lax.dynamic_slice_in_dim(jnp.stack(seen + seen), (n - me) % n, n, 0)


def local(
    tokens,
    lengths,
    first_norm_gain,
    w_in,
    w_forget,
    w_gate,
    lower_bound,
    gate_gain,
    w_out,
    feedforward_gain,
    w_up,
    w_glu,
    w_down,
    cotangent,
):
    rows, width = tokens.shape
    chans = w_in.shape[1]
    units = w_up.shape[1]
    ways = lax.axis_size("tensor")
    chips = lax.axis_size("chip")
    groups = 2 * chips
    way = lax.axis_index("tensor")
    core = lax.axis_index("core")
    chip = lax.axis_index("chip")
    group = chip * 2 + core
    every = ("tensor", "chip", "core")
    square = chips == 4 and ways == 4

    def gather(weights):
        tall = weights.shape[0] // groups
        piece = lax.dynamic_slice_in_dim(weights, group * tall, tall, 0)
        piece = lax.all_gather(piece, every, axis=0, tiled=True)
        return piece.reshape((ways,) + weights.shape)

    vectors = from_all(jnp.stack([lower_bound, gate_gain]), "tensor")
    lower, gain = vectors[:, 0:1], vectors[:, 1:2]
    l0, l1 = lengths[0, 0], lengths[0, 1]
    starts = jnp.stack([jnp.zeros_like(l0), l0, l0 + l1]) - way * rows
    x = tokens.astype(F32)
    inverse1 = lax.rsqrt(jnp.mean(x * x, axis=1, keepdims=True) + EPS)
    normed = (x * inverse1 * first_norm_gain).astype(BF16)

    shards = [w_in, w_forget, w_gate, w_glu, w_up, w_out]
    if square:
        all_shards = gather_weights(shards, ways)
        w_down_all = gather(behind(w_down, all_shards[5]))
    else:
        all_shards = [gather(w) for w in shards]
        w_down_all = gather(w_down)
    w_three, (w_glu_all, w_up_all, w_out_all) = all_shards[:3], all_shards[3:]

    p = project(normed, *w_three)
    totals = forward_total(p, lower, starts)
    all_totals = from_all(totals, "tensor")
    enter = jnp.zeros((ways, 1, chans), F32)
    seen = jnp.zeros((ways, 1, chans), F32)
    for k in range(ways - 1):
        seen = all_totals[k, :, 0:1] * seen + all_totals[k, :, 1:2]
        enter = jnp.where(way == k + 1, seen, enter)
    state, mixed, lam_sum = forward_scan(p, lower, gain, starts, enter)

    resid, middle = branch(mixed, w_out_all, tokens, feedforward_gain.reshape(1, width))
    hidden, act, slope = feed_up(middle, w_up_all, w_glu_all)

    places = jnp.arange(chips, dtype=jnp.int32)

    ours_at, theirs_at = places * 2 + core, places * 2 + (1 - core)

    def swap(array):
        return lax.ppermute(array, "core", SWAP)

    class Scatter:
        def begin(self, array):
            part = lax.psum_scatter(array, "chip", scatter_dimension=0, tiled=True)
            self.part = lax.optimization_barrier(part.reshape(part.shape[1:]))
            self.parts = [self.block(0)]

        def block(self, k):
            return lax.dynamic_index_in_dim(self.part, (way + k) % ways, 0, False)

        def send(self, *steps):
            got = [
                lax.ppermute(self.block(k), "tensor", [(i, (i + k) % ways) for i in range(ways)])
                for k in steps
                if k < ways
            ]
            self.parts += got
            return tuple(got)

        def rest(self):
            part = lax.psum_scatter(self.part, "tensor", scatter_dimension=0, tiled=True)
            self.parts = [part.reshape(part.shape[1:])]

        def finish(self):
            return sum(a.astype(F32) for a in self.parts)

    last = [()]

    def run(fn, *arrays):
        out = fn(*lax.optimization_barrier(arrays + last[0])[: len(arrays)])
        last[0] = tuple(jax.tree.leaves(out))
        return out

    def rows_grad(at, rights, left, *adds):
        n = len(rights)
        got = lambda left, *more: by_rows(left, more[:n], at, more[n:], chips)
        return run(got, left, *rights, *adds)

    def cols_grad(at, left, right, *adds):
        return run(lambda left, right, *more: by_cols(left, right, at, more, chips), left, right, *adds)

    down, up, glu, out, three = [Scatter() for _ in range(5)]
    gy = cotangent

    def beside(arrived):
        last[0] = last[0] + arrived

    def send(scattered, *steps):
        return scattered.send(*steps) if few else ()

    few = ways <= 4

    swapped = swap(cols_grad(theirs_at, hidden, gy))
    down.begin(cols_grad(ours_at, hidden, gy, swapped))
    g_up, g_glu = run(hidden_grad, gy, w_down_all, act, slope)
    swapped_up = swap(rows_grad(theirs_at, [g_up], middle))
    swapped_glu = swap(rows_grad(theirs_at, [g_glu], middle))
    up.begin(rows_grad(ours_at, [g_up], middle, swapped_up))
    glu.begin(rows_grad(ours_at, [g_glu], middle, swapped_glu))
    g_middle = run(
        lambda a, b, c, d: back([a, b], [c, d], units), g_up, g_glu, w_up_all, w_glu_all
    )
    def second_norm(resid, g_middle, gy):
        inverse2 = lax.rsqrt(jnp.mean(resid * resid, axis=1, keepdims=True) + EPS)
        unit2 = resid * inverse2
        mlp_gain_part = jnp.sum(g_middle * unit2, axis=0)
        g_resid = gy.astype(F32) + norm_pullback(g_middle, unit2, inverse2, feedforward_gain)
        return mlp_gain_part, g_resid, g_resid.astype(BF16)

    moving = send(down, 1)
    mlp_gain_part, g_resid, g_branch = run(second_norm, resid, g_middle, gy)
    swapped_out = swap(cols_grad(theirs_at, mixed, g_branch))
    g_mixed = run(mixed_grad, g_branch, w_out_all)
    beside(moving)
    out.begin(cols_grad(ours_at, mixed, g_branch, swapped_out))
    moving = send(down, 2)
    g_state, g_gate, gain_part, back_totals = run(backward_total, p, state, g_mixed, lower, gain, starts)
    beside(moving)
    all_back = lax.all_gather(back_totals, "tensor", axis=0)
    after = jnp.zeros((ways, 1, chans), F32)
    seen = jnp.zeros((ways, 1, chans), F32)
    for k in range(ways - 1, 0, -1):
        seen = all_totals[k, :, 0:1] * seen + all_back[k]
        after = jnp.where(way == k - 1, seen, after)
    moving = send(down, 3)
    g_in, g_forget, lower_part = run(backward_scan, p, state, g_state, lower, starts, enter, after)
    beside(moving)

    g_three = [g_in, g_forget, g_gate]
    swapped = swap(rows_grad(theirs_at, g_three, normed))
    three.begin(rows_grad(ours_at, g_three, normed, swapped))
    moving = send(up, 1, 2, 3)
    output = run(feed_down, hidden, w_down_all, resid)
    beside(moving)
    moving = send(glu, 1)
    g_normed = run(
        lambda *a: back(a[:3], a[3:], chans), *g_three, *w_three
    )
    beside(moving)
    moving = send(glu, 2) + send(out, 1, 2, 3)

    def first_norm_back(x, g_normed, g_resid):
        x = x.astype(F32)
        inverse1 = lax.rsqrt(jnp.mean(x * x, axis=1, keepdims=True) + EPS)
        unit1 = x * inverse1
        norm_gain_part = jnp.sum(g_normed * unit1, axis=0)
        return norm_gain_part, g_resid + norm_pullback(g_normed, unit1, inverse1, first_norm_gain)

    norm_gain_part, token_gradient = run(first_norm_back, tokens, g_normed, g_resid)
    beside(moving)
    moving = send(glu, 3)

    small = jnp.stack(
        [
            norm_gain_part,
            mlp_gain_part,
            jnp.sum(gain_part, axis=1).reshape(width),
            jnp.sum(lower_part, axis=1).reshape(width),
            jnp.sum(lam_sum, axis=1).reshape(width),
        ]
    )
    beside(moving)
    three.part = behind(three.part, *last[0])
    beside((three.part,))
    three.rest()
    small = run(lambda v: lax.psum(v, every), small)
    three.parts = [behind(three.parts[0], small)]
    if not few:
        for s in (down, up, glu, out):
            s.rest()
    grad_w_down, grad_w_up, grad_w_glu, grad_w_out, grad_three = [
        s.finish() for s in (down, up, glu, out, three)
    ]
    mean_forget = jnp.sum(small[4]) / (rows * ways * groups * width)
    return (
        output,
        token_gradient,
        small[0],
        grad_three[:, :chans],
        grad_three[:, chans : 2 * chans],
        grad_three[:, 2 * chans :],
        small[3],
        small[2],
        grad_w_out,
        small[1],
        grad_w_up,
        grad_w_glu,
        grad_w_down,
        mean_forget,
    )


def solution(mesh):
    groups, ways = mesh.shape["dp"], mesh.shape["tensor"]
    parts = Mesh(mesh.devices.reshape(groups // 2, 2, ways), ("chip", "core", "tensor"))
    dp = ("chip", "core")
    tokens = P(("chip", "core", "tensor"), None)
    return jax.shard_map(
        local,
        mesh=parts,
        in_specs=(
            tokens,
            P(dp, None),
            P(),
            P(None, "tensor"),
            P(None, "tensor"),
            P(None, "tensor"),
            P("tensor"),
            P("tensor"),
            P("tensor", None),
            P(),
            P(None, "tensor"),
            P(None, "tensor"),
            P("tensor", None),
            tokens,
        ),
        out_specs=(
            tokens,
            tokens,
            P(),
            P(dp, "tensor"),
            P(dp, "tensor"),
            P(dp, "tensor"),
            P(),
            P(),
            P("tensor", dp),
            P(),
            P(dp, "tensor"),
            P(dp, "tensor"),
            P("tensor", dp),
            P(),
        ),
        check_vma=False,
    )
```

```python
import functools

import jax
import jax.numpy as jnp
from jax import lax
from jax.experimental import pallas as pl
from jax.experimental.pallas import tpu as pltpu
from jax.sharding import Mesh
from jax.sharding import PartitionSpec as P

EPS = 1e-06
VMEM_LIMIT = 60 * 1024 * 1024
F32 = jnp.float32
BF16 = jnp.bfloat16
MESH = pl.DeviceIdType.MESH


def params(**kw):
    return pltpu.CompilerParams(vmem_limit_bytes=VMEM_LIMIT, **kw)


def nn(left, right):
    return lax.dot_general(left, right, (((1,), (0,)), ((), ())), preferred_element_type=F32)


def nt(left, right):
    return lax.dot_general(left, right, (((1,), (1,)), ((), ())), preferred_element_type=F32)


def tn(left, right):
    return lax.dot_general(left, right, (((0,), (0,)), ((), ())), preferred_element_type=F32)


def sigmoid(v):
    return jax.nn.sigmoid(v)


def whole(shape):
    zeros = (0,) * len(shape)
    return pl.BlockSpec(shape, lambda *_: zeros)


GATHER_SLOTS = 9


def gather_kernel(n, ways, *refs):
    ins, normed_ref, outs, p_ref = refs[:n], refs[n], refs[n + 1 : 2 * n + 1], refs[2 * n + 1]
    held = refs[2 * n + 2 : 3 * n + 2]
    w_buf, p_buf, w_sem, p_sem, in_sem, own_sem, send_sem, recv_sem = refs[3 * n + 2 :]
    way = lax.axis_index("tensor")
    chip = lax.axis_index("chip")
    core = lax.axis_index("core")
    chip_x = chip + 1 - 2 * lax.rem(chip, 2)
    chip_y = lax.rem(chip + 2, 4)
    chip_d = 3 - chip
    here = chip * 2 + core
    over_x, over_y, over_d = chip_x * 2 + core, chip_y * 2 + core, chip_d * 2 + core
    x_id, y_id, core_id = {"chip": chip_x}, {"chip": chip_y}, {"core": 1 - core}

    barrier = pltpu.get_barrier_semaphore()
    for target in (x_id, y_id, core_id):
        pl.semaphore_signal(barrier, inc=1, device_id=target, device_id_type=MESH)

    @pl.when(way > 0)
    def _():
        pl.semaphore_signal(barrier, inc=1, device_id={"tensor": way - 1}, device_id_type=MESH)

    @pl.when(way < ways - 1)
    def _():
        pl.semaphore_signal(barrier, inc=1, device_id={"tensor": way + 1}, device_id_type=MESH)

    ends = jnp.where(way == 0, 1, 0) + jnp.where(way == ways - 1, 1, 0)
    pl.semaphore_wait(barrier, 5 - ends)

    def piece(k, shard, owner, part=None):
        tall = ins[k].shape[0] // 8
        start, size = owner * tall, tall
        if part is not None:
            size = tall // 2
            start = start + part * size
        return outs[k].at[shard, pl.ds(pl.multiple_of(start, 8), size)]

    def copy(src, dst, k, kind, slot, target):
        return pltpu.make_async_remote_copy(
            src_ref=src,
            dst_ref=dst,
            send_sem=send_sem.at[k, kind, slot],
            recv_sem=recv_sem.at[k, kind, slot],
            device_id=target,
            device_id_type=MESH,
        )

    def along(block, k, kind, slot, target):
        return copy(block, block, k, kind, slot, target)

    def first(k, up):
        tall = ins[k].shape[0] // 8
        src = ins[k].at[pl.ds(pl.multiple_of(here * tall, 8), tall)]
        return copy(src, piece(k, way, here), k, 0 if up else 1, 0, {"tensor": way + (1 if up else -1)})

    def guard(hop, up):
        arrives = way >= hop if up else way + hop < ways
        goes_on = jnp.logical_and(arrives, way < ways - 1) if up else jnp.logical_and(arrives, way > 0)
        return arrives, goes_on

    def shard_of(hop, up):
        return way - hop if up else way + hop

    def z_copy(k, hop, up):
        kind = 2 * (hop - 1) + (0 if up else 1)
        return along(piece(k, shard_of(hop, up), here), k, kind, 0, {"tensor": way + (1 if up else -1)})

    def z_next(k, hop, up):
        kind = 2 * hop + (0 if up else 1)
        return along(piece(k, shard_of(hop, up), here), k, kind, 0, {"tensor": way + (1 if up else -1)})

    def plane(k, hop, up):
        kind = 2 * (hop - 1) + (0 if up else 1)
        s = shard_of(hop, up)
        make = lambda block, slot, target: (lambda: along(block, k, kind, slot, target))
        return dict(
            x=make(piece(k, s, here), 1, x_id),
            y=make(piece(k, s, here), 2, y_id),
            dy=make(piece(k, s, over_x, 0), 3, y_id),
            dx=make(piece(k, s, over_y, 1), 4, x_id),
            c0=make(piece(k, s, here), 5, core_id),
            c1=make(piece(k, s, over_x), 6, core_id),
            c2=make(piece(k, s, over_y), 7, core_id),
            c3=make(piece(k, s, over_d), 8, core_id),
        )

    def both(fn):
        for up in (True, False):
            fn(up)

    def start_own(k):
        @pl.when(way < ways - 1)
        def _():
            first(k, True).start()

        @pl.when(way > 0)
        def _():
            first(k, False).start()

    def stage1(k, hop):
        def run(up):
            arrives, goes_on = guard(hop, up)

            @pl.when(arrives)
            def _():
                z_copy(k, hop, up).wait_recv()
                to = plane(k, hop, up)
                to["x"]().start()
                to["y"]().start()
                to["c0"]().start()

            if hop < ways - 1:

                @pl.when(goes_on)
                def _():
                    z_next(k, hop, up).start()

        both(run)

    def stage2(k, hop):
        def run(up):
            @pl.when(guard(hop, up)[0])
            def _():
                to = plane(k, hop, up)
                to["x"]().wait_recv()
                to["dy"]().start()
                to["c1"]().start()
                to["y"]().wait_recv()
                to["dx"]().start()
                to["c2"]().start()

        both(run)

    def stage3(k, hop):
        def run(up):
            @pl.when(guard(hop, up)[0])
            def _():
                to = plane(k, hop, up)
                to["dy"]().wait_recv()
                to["dx"]().wait_recv()
                to["c3"]().start()

        both(run)

    def finish(k, hop):
        def run(up):
            arrives, goes_on = guard(hop, up)

            @pl.when(arrives)
            def _():
                to = plane(k, hop, up)
                for name in to:
                    to[name]().wait_send()

            if hop < ways - 1:

                @pl.when(goes_on)
                def _():
                    z_next(k, hop, up).wait_send()

        both(run)

    def whole_shards(k):
        own(k).wait()

        def run(hop, up):
            @pl.when(guard(hop, up)[0])
            def _():
                to = plane(k, hop, up)
                for name in ("c0", "c1", "c2", "c3"):
                    to[name]().wait_recv()

        for hop in range(1, ways):
            both(functools.partial(run, hop))

    rows, chans = p_buf.shape[1:]
    part = min(rows, 256)

    def fetch(m):
        return pltpu.make_async_copy(outs[m // ways].at[m % ways], w_buf.at[m % 2], w_sem.at[m % 2])

    def put_back(m):
        place = p_ref.at[m % ways, :, pl.ds((m // ways) * chans, chans)]
        return pltpu.make_async_copy(p_buf.at[m % 2], place, p_sem.at[m % 2])

    def tile(m):
        fetch(m).wait()
        if m >= 2:
            put_back(m - 2).wait()

        def rows_of(r, carry):
            at = pl.ds(pl.multiple_of(r * part, part), part)
            p_buf[m % 2, at, :] = nn(normed_ref[at, :], w_buf[m % 2])
            return carry

        lax.fori_loop(0, rows // part, rows_of, 0)
        put_back(m).start()
        if m + 2 < (m // ways + 1) * ways:
            fetch(m + 2).start()

    steps = [(k, hop) for k in range(n) for hop in range(1, ways)]
    start_own(0)
    load = lambda k: pltpu.make_async_copy(ins[k], held[k], in_sem.at[k])
    own = lambda k: pltpu.make_async_copy(held[k], outs[k].at[way], own_sem.at[k])
    for k in range(n):
        load(k).start()
    todo = []
    for i in range(len(steps) + 4):
        if i < len(steps):
            k, hop = steps[i]
            if hop == 1:
                load(k).wait()
                own(k).start()
                if k + 1 < n:
                    start_own(k + 1)
            stage1(k, hop)
        if 0 <= i - 2 < len(steps):
            stage2(*steps[i - 2])
        if 0 <= i - 4 < len(steps):
            stage3(*steps[i - 4])
        if i >= 4 + ways and (i - 4 - ways) % (ways - 1) == 0 and (i - 4 - ways) // (ways - 1) < 3:
            j = (i - 4 - ways) // (ways - 1)
            whole_shards(j)
            todo += range(j * ways, (j + 1) * ways)
            for m in todo[-ways:][:2]:
                fetch(m).start()
            tile(todo.pop(0))
        if todo:
            tile(todo.pop(0))
    put_back(3 * ways - 2).wait()
    put_back(3 * ways - 1).wait()
    for k in range(n):
        if k >= 3:
            whole_shards(k)

        @pl.when(way < ways - 1)
        def _():
            first(k, True).wait_send()

        @pl.when(way > 0)
        def _():
            first(k, False).wait_send()

        for hop in range(1, ways):
            finish(k, hop)


def gather_weights(shards, ways, normed):
    n = len(shards)
    any_space = pl.BlockSpec(memory_space=pl.ANY)
    kinds = 2 * (ways - 1)
    rows, width = normed.shape
    chans = shards[0].shape[1]
    outs = pl.pallas_call(
        functools.partial(gather_kernel, n, ways),
        in_specs=[any_space] * n + [pl.BlockSpec(memory_space=pltpu.VMEM)],
        out_specs=[any_space] * (n + 1),
        out_shape=[jax.ShapeDtypeStruct((ways,) + w.shape, w.dtype) for w in shards]
        + [jax.ShapeDtypeStruct((ways, rows, 3 * chans), F32)],
        scratch_shapes=[pltpu.VMEM(w.shape, w.dtype) for w in shards]
        + [
            pltpu.VMEM((2, width, chans), BF16),
            pltpu.VMEM((2, rows, chans), F32),
            pltpu.SemaphoreType.DMA((2,)),
            pltpu.SemaphoreType.DMA((2,)),
            pltpu.SemaphoreType.DMA((n,)),
            pltpu.SemaphoreType.DMA((n,)),
            pltpu.SemaphoreType.DMA((n, kinds, GATHER_SLOTS)),
            pltpu.SemaphoreType.DMA((n, kinds, GATHER_SLOTS)),
        ],
        compiler_params=params(collective_id=1, has_side_effects=True),
        name="gather_weights",
    )(*shards, normed)
    return outs[:n], outs[n]


def proj_kernel(x_ref, in_ref, forget_ref, gate_ref, o_ref):
    for j, w_ref in enumerate((in_ref, forget_ref, gate_ref)):

        @pl.when(pl.program_id(1) == j)
        def _(w_ref=w_ref):
            o_ref[0] = nn(x_ref[...], w_ref[0])


def project(normed, w_in, w_forget, w_gate):
    rows, width = normed.shape
    ways, _, chans = w_in.shape

    def weights(k):
        following = lambda t, j: jnp.where(j > k, jnp.minimum(t + 1, ways - 1), t)
        return pl.BlockSpec((1, width, chans), lambda t, j: (following(t, j), 0, 0))

    return pl.pallas_call(
        proj_kernel,
        grid=(ways, 3),
        in_specs=[whole((rows, width)), weights(0), weights(1), weights(2)],
        out_specs=pl.BlockSpec((1, rows, chans), lambda t, j: (t, 0, j)),
        out_shape=jax.ShapeDtypeStruct((ways, rows, 3 * chans), F32),
        compiler_params=params(),
        name="project",
    )(normed, w_in, w_forget, w_gate)


def gates(p_in, p_forget, lower, ids, starts):
    sig = sigmoid(p_forget)
    lam = lower + (1.0 - lower) * sig
    fresh = ids == starts[0]
    for s in starts[1:]:
        fresh = jnp.logical_or(fresh, ids == s)
    keep = jnp.where(fresh, 0.0, 1.0)
    return sig, lam, keep


def forward_total_kernel(starts_ref, p_ref, lower_ref, o_ref):
    rows, chans = p_ref.shape[1], p_ref.shape[2] // 2
    lower = lower_ref[0]
    starts = [starts_ref[i] for i in range(starts_ref.shape[0])]
    iota = lax.broadcasted_iota(jnp.int32, (8, chans), 0)

    def step(g, carry):
        total, last = carry
        at = pl.multiple_of(g * 8, 8)
        p_in = p_ref[0, pl.ds(at, 8), :chans]
        p_forget = p_ref[0, pl.ds(at, 8), chans:]
        _, lam, keep = gates(p_in, p_forget, lower, iota + at, starts)
        a = lam * keep
        b = p_in * sigmoid(p_in) * (1.0 - lam)
        for s in (1, 2, 4):
            b = a * pltpu.roll(b, s, 0) + b
            a = a * pltpu.roll(a, s, 0)
        a, b = a[7:8], b[7:8]
        return total * a, a * last + b

    total, last = lax.fori_loop(
        0, rows // 8, step, (jnp.ones((1, chans), F32), jnp.zeros((1, chans), F32)), unroll=2
    )
    o_ref[0, 0:1] = total
    o_ref[0, 1:2] = last


def forward_total(p, lower, starts):
    ways, rows, wide = p.shape
    chans = wide // 3
    return pl.pallas_call(
        forward_total_kernel,
        grid=(ways,),
        in_specs=[
            pl.BlockSpec(memory_space=pltpu.SMEM),
            pl.BlockSpec((1, rows, 2 * chans), lambda t: (t, 0, 0)),
            pl.BlockSpec((1, 1, chans), lambda t: (t, 0, 0)),
        ],
        out_specs=pl.BlockSpec((1, 2, chans), lambda t: (t, 0, 0)),
        out_shape=jax.ShapeDtypeStruct((ways, 2, chans), F32),
        compiler_params=params(),
        name="forward_total",
    )(starts, p, lower)


def forward_scan_kernel(starts_ref, p_ref, lower_ref, gain_ref, enter_ref, state_ref, mixed_ref, lam_ref, held):
    ways, rows, wide = p_ref.shape
    chans = wide // 3
    block = pl.program_id(0)
    starts = [starts_ref[i] for i in range(starts_ref.shape[0])]
    iota = lax.broadcasted_iota(jnp.int32, (8, chans), 0)

    @pl.when(block == 0)
    def _():
        held[...] = enter_ref[...]
        lam_ref[...] = jnp.zeros_like(lam_ref)

    for t in range(ways):
        lower = lower_ref[t]

        def step(g, carry):
            before, lam_sum = carry
            at = pl.multiple_of(g * 8, 8)
            p_in = p_ref[t, pl.ds(at, 8), :chans]
            p_forget = p_ref[t, pl.ds(at, 8), chans : 2 * chans]
            _, lam, keep = gates(p_in, p_forget, lower, iota + (at + block * rows), starts)
            a = lam * keep
            b = p_in * sigmoid(p_in) * (1.0 - lam)
            for s in (1, 2, 4):
                far = iota >= s
                b = jnp.where(far, a * pltpu.roll(b, s, 0) + b, b)
                a = jnp.where(far, a * pltpu.roll(a, s, 0), a)
            state = a * before + b
            state_ref[t, pl.ds(at, 8), :] = state
            return state[7:8], lam_sum + lam

        last, lam_sum = lax.fori_loop(
            0, rows // 8, step, (held[t], jnp.zeros((8, chans), F32)), unroll=2
        )
        held[t] = last
        lam_ref[t] += lam_sum

    squares = jnp.zeros((rows, 1), F32)
    for t in range(ways):
        state = state_ref[t]
        squares += jnp.sum(state * state, axis=1, keepdims=True)
    scale = lax.rsqrt(squares / (ways * chans) + EPS)
    for t in range(ways):
        gate = p_ref[t, :, 2 * chans :]
        mixed = state_ref[t] * scale * gain_ref[t] * (gate * sigmoid(gate))
        mixed_ref[t] = mixed.astype(BF16)


def forward_scan(p, lower, gain, starts, enter):
    ways, rows, wide = p.shape
    chans = wide // 3
    part = min(rows, 128)
    return pl.pallas_call(
        forward_scan_kernel,
        grid=(rows // part,),
        in_specs=[
            pl.BlockSpec(memory_space=pltpu.SMEM),
            pl.BlockSpec((ways, part, wide), lambda i: (0, i, 0)),
            whole((ways, 1, chans)),
            whole((ways, 1, chans)),
            whole((ways, 1, chans)),
        ],
        out_specs=[
            pl.BlockSpec((ways, part, chans), lambda i: (0, i, 0)),
            pl.BlockSpec((ways, part, chans), lambda i: (0, i, 0)),
            whole((ways, 8, chans)),
        ],
        out_shape=[
            jax.ShapeDtypeStruct((ways, rows, chans), F32),
            jax.ShapeDtypeStruct((ways, rows, chans), BF16),
            jax.ShapeDtypeStruct((ways, 8, chans), F32),
        ],
        scratch_shapes=[pltpu.VMEM((ways, 1, chans), F32)],
        compiler_params=params(),
        name="forward_scan",
    )(starts, p, lower, gain, enter)


def backward_total_kernel(
    starts_ref, pf_ref, pg_ref, state_ref, gm_ref, lower_ref, gain_ref,
    gstate_ref, ggate_ref, dgain_ref, total_ref, held,
):
    ways, rows, chans = pf_ref.shape
    step_id = pl.program_id(0)
    block = pl.num_programs(0) - 1 - step_id
    starts = [starts_ref[i] for i in range(starts_ref.shape[0])]
    iota = lax.broadcasted_iota(jnp.int32, (8, chans), 0)
    width = ways * chans

    @pl.when(step_id == 0)
    def _():
        held[...] = jnp.zeros_like(held)
        dgain_ref[...] = jnp.zeros_like(dgain_ref)

    squares = jnp.zeros((rows, 1), F32)
    cross = jnp.zeros((rows, 1), F32)
    for t in range(ways):
        state = state_ref[t]
        gate = pg_ref[t]
        inner = gm_ref[t] * gain_ref[t] * (gate * sigmoid(gate))
        gstate_ref[t] = inner
        squares += jnp.sum(state * state, axis=1, keepdims=True)
        cross += jnp.sum(inner * state, axis=1, keepdims=True)
    scale = lax.rsqrt(squares / width + EPS)
    pull = scale * scale * scale * cross / width
    for t in range(ways):
        state = state_ref[t]
        gate = pg_ref[t]
        sig = sigmoid(gate)
        slope = sig * (1.0 + gate * (1.0 - sig))
        unit = gm_ref[t] * state * scale
        ggate_ref[t] = (unit * gain_ref[t] * slope).astype(BF16)
        dgain_ref[t] += jnp.sum((unit * (gate * sig)).reshape(rows // 8, 8, chans), axis=0)
        gstate_ref[t] = gstate_ref[t] * scale - state * pull

    for t in range(ways):
        lower = lower_ref[t]

        def step(k, last):
            at = pl.multiple_of(rows - 8 - k * 8, 8)
            p_forget = pf_ref[t, pl.ds(at, 8), :]
            _, lam, keep = gates(None, p_forget, lower, iota + (at + block * rows), starts)
            a = lam * keep
            b = a * gstate_ref[t, pl.ds(at, 8), :]
            for s in (1, 2, 4):
                b = a * pltpu.roll(b, 8 - s, 0) + b
                a = a * pltpu.roll(a, 8 - s, 0)
            return a[0:1] * last + b[0:1]

        held[t] = lax.fori_loop(0, rows // 8, step, held[t], unroll=2)
    total_ref[...] = held[...]


def backward_total(p, state, g_mixed, lower, gain, starts):
    ways, rows, wide = p.shape
    chans = wide // 3
    part = min(rows, 128)
    last = rows // part - 1
    back = lambda i: (0, last - i, 0)
    block = pl.BlockSpec((ways, part, chans), back)
    return pl.pallas_call(
        backward_total_kernel,
        grid=(rows // part,),
        in_specs=[
            pl.BlockSpec(memory_space=pltpu.SMEM),
            pl.BlockSpec((ways, part, chans), lambda i: (0, last - i, 1)),
            pl.BlockSpec((ways, part, chans), lambda i: (0, last - i, 2)),
            block,
            block,
            whole((ways, 1, chans)),
            whole((ways, 1, chans)),
        ],
        out_specs=[block, block, whole((ways, 8, chans)), whole((ways, 1, chans))],
        out_shape=[
            jax.ShapeDtypeStruct((ways, rows, chans), F32),
            jax.ShapeDtypeStruct((ways, rows, chans), BF16),
            jax.ShapeDtypeStruct((ways, 8, chans), F32),
            jax.ShapeDtypeStruct((ways, 1, chans), F32),
        ],
        scratch_shapes=[pltpu.VMEM((ways, 1, chans), F32)],
        compiler_params=params(),
        name="backward_total",
    )(starts, p, p, state, g_mixed, lower, gain)


def backward_scan_kernel(
    starts_ref, pi_ref, pf_ref, state_ref, early_ref, gstate_ref, lower_ref, enter_ref, after_ref,
    gin_ref, gforget_ref, dlower_ref, held,
):
    ways, rows, chans = pi_ref.shape
    step_id = pl.program_id(0)
    block = pl.num_programs(0) - 1 - step_id
    starts = [starts_ref[i] for i in range(starts_ref.shape[0])]
    iota = lax.broadcasted_iota(jnp.int32, (8, chans), 0)

    @pl.when(step_id == 0)
    def _():
        held[...] = after_ref[...]
        dlower_ref[...] = jnp.zeros_like(dlower_ref)

    for t in range(ways):
        lower = lower_ref[t]
        first = jnp.where(block == 0, enter_ref[t], early_ref[t, 7:8])

        def eight(at, after, before):
            p_in = pi_ref[t, pl.ds(at, 8), :]
            p_forget = pf_ref[t, pl.ds(at, 8), :]
            grad = gstate_ref[t, pl.ds(at, 8), :]
            state = state_ref[t, pl.ds(at, 8), :]
            sig, lam, keep = gates(None, p_forget, lower, iota + (at + block * rows), starts)
            a = lam * keep
            b = a * grad
            for s in (1, 2, 4):
                near = iota < 8 - s
                b = jnp.where(near, a * pltpu.roll(b, 8 - s, 0) + b, b)
                a = jnp.where(near, a * pltpu.roll(a, 8 - s, 0), a)
            handed = a * after + b
            carry = grad + jnp.where(iota == 7, after, pltpu.roll(handed, 7, 0))
            previous = jnp.where(iota == 0, before, pltpu.roll(state, 1, 0))
            sig_in = sigmoid(p_in)
            act = p_in * sig_in
            g_lam = carry * previous * keep - carry * act
            g_in = carry * (1.0 - lam) * (sig_in * (1.0 + p_in * (1.0 - sig_in)))
            lower_part = g_lam * (1.0 - sig)
            g_forget = lower_part * (1.0 - lower) * sig
            return handed[0:1], g_in, g_forget, lower_part

        def step(k, carry):
            after, total = carry
            at = pl.multiple_of(rows - 16 - k * 16, 16)
            middle = state_ref[t, pl.ds(at, 8), :][7:8]
            ahead = jnp.maximum(at - 8, 0)
            held_before = state_ref[t, pl.ds(pl.multiple_of(ahead, 8), 8), :][7:8]
            before = jnp.where(at == 0, first, held_before)
            after, in_late, forget_late, part_late = eight(pl.multiple_of(at + 8, 8), after, middle)
            after, in_early, forget_early, part_early = eight(at, after, before)
            gin_ref[t, pl.ds(at, 16), :] = jnp.concatenate([in_early, in_late], 0).astype(BF16)
            gforget_ref[t, pl.ds(at, 16), :] = jnp.concatenate([forget_early, forget_late], 0).astype(BF16)
            return after, total + part_late + part_early

        after, total = lax.fori_loop(
            0, rows // 16, step, (held[t], jnp.zeros((8, chans), F32))
        )
        held[t] = after
        dlower_ref[t] += total


def backward_scan(p, state, g_state, lower, starts, enter, after):
    ways, rows, wide = p.shape
    chans = wide // 3
    part = min(rows, 128)
    last = rows // part - 1
    block = pl.BlockSpec((ways, part, chans), lambda i: (0, last - i, 0))
    eights = part // 8
    return pl.pallas_call(
        backward_scan_kernel,
        grid=(rows // part,),
        in_specs=[
            pl.BlockSpec(memory_space=pltpu.SMEM),
            pl.BlockSpec((ways, part, chans), lambda i: (0, last - i, 0)),
            pl.BlockSpec((ways, part, chans), lambda i: (0, last - i, 1)),
            block,
            pl.BlockSpec((ways, 8, chans), lambda i: (0, jnp.maximum((last - i) * eights - 1, 0), 0)),
            block,
            whole((ways, 1, chans)),
            whole((ways, 1, chans)),
            whole((ways, 1, chans)),
        ],
        out_specs=[block, block, whole((ways, 8, chans))],
        out_shape=[
            jax.ShapeDtypeStruct((ways, rows, chans), BF16),
            jax.ShapeDtypeStruct((ways, rows, chans), BF16),
            jax.ShapeDtypeStruct((ways, 8, chans), F32),
        ],
        scratch_shapes=[pltpu.VMEM((ways, 1, chans), F32)],
        compiler_params=params(),
        name="backward_scan",
    )(starts, p, p, state, state, g_state, lower, enter, after)


def branch_kernel(mixed_ref, w_ref, x_ref, gain_ref, resid_ref, middle_ref):
    ways = mixed_ref.shape[0]
    total = x_ref[...].astype(F32)
    acc = nn(mixed_ref[0], w_ref[0])
    for t in range(1, ways):
        acc += nn(mixed_ref[t], w_ref[t])
    resid = total + acc
    resid_ref[...] = resid
    inverse = lax.rsqrt(jnp.mean(resid * resid, axis=1, keepdims=True) + EPS)
    middle_ref[...] = (resid * inverse * gain_ref[...]).astype(BF16)


def branch(mixed, w_out, tokens, gain):
    ways, rows, chans = mixed.shape
    width = tokens.shape[1]
    part = min(rows, 256)
    line = pl.BlockSpec((part, width), lambda i: (i, 0))
    return pl.pallas_call(
        branch_kernel,
        grid=(rows // part,),
        in_specs=[
            pl.BlockSpec((ways, part, chans), lambda i: (0, i, 0)),
            whole((ways, chans, width)),
            line,
            whole((1, width)),
        ],
        out_specs=[line, line],
        out_shape=[
            jax.ShapeDtypeStruct((rows, width), F32),
            jax.ShapeDtypeStruct((rows, width), BF16),
        ],
        compiler_params=params(),
        name="branch",
    )(mixed, w_out, tokens, gain)


def up_kernel(x_ref, up_ref, glu_ref, hidden_ref, act_ref, slope_ref):
    x = x_ref[...]
    glu = nn(x, glu_ref[0])
    sig = sigmoid(glu)
    act = glu * sig
    up = nn(x, up_ref[0])
    hidden_ref[0] = (act * up).astype(BF16)
    act_ref[0] = act.astype(BF16)
    slope_ref[0] = (up * (sig * (1.0 + glu * (1.0 - sig)))).astype(BF16)


def feed_up(middle, w_up, w_glu):
    rows, width = middle.shape
    ways, _, units = w_up.shape
    part = min(rows, 512)
    weights = pl.BlockSpec((1, width, units), lambda t, i: (t, 0, 0))
    out = pl.BlockSpec((1, part, units), lambda t, i: (t, i, 0))
    return pl.pallas_call(
        up_kernel,
        grid=(ways, rows // part),
        in_specs=[pl.BlockSpec((part, width), lambda t, i: (i, 0)), weights, weights],
        out_specs=[out, out, out],
        out_shape=[jax.ShapeDtypeStruct((ways, rows, units), BF16)] * 3,
        compiler_params=params(),
        name="feed_up",
    )(middle, w_up, w_glu)


def down_kernel(h_ref, w_ref, resid_ref, o_ref):
    acc = nn(h_ref[0], w_ref[0])
    for t in range(1, h_ref.shape[0]):
        acc += nn(h_ref[t], w_ref[t])
    o_ref[...] = (resid_ref[...] + acc).astype(BF16)


def feed_down(hidden, w_down, resid):
    ways, rows, units = hidden.shape
    width = w_down.shape[2]
    part = 512
    return pl.pallas_call(
        down_kernel,
        grid=(width // part,),
        in_specs=[
            whole((ways, rows, units)),
            pl.BlockSpec((ways, units, part), lambda j: (0, 0, j)),
            pl.BlockSpec((rows, part), lambda j: (0, j)),
        ],
        out_specs=pl.BlockSpec((rows, part), lambda j: (0, j)),
        out_shape=jax.ShapeDtypeStruct((rows, width), BF16),
        compiler_params=params(),
        name="feed_down",
    )(hidden, w_down, resid)


def hidden_grad_kernel(dy_ref, w_ref, act_ref, slope_ref, gup_ref, gglu_ref):
    g_hidden = nt(dy_ref[...], w_ref[0])
    gup_ref[0] = (g_hidden * act_ref[0].astype(F32)).astype(BF16)
    gglu_ref[0] = (g_hidden * slope_ref[0].astype(F32)).astype(BF16)


def hidden_grad(dy, w_down, act, slope):
    rows, width = dy.shape
    ways, units, _ = w_down.shape
    part = min(rows, 1024)
    out = pl.BlockSpec((1, part, units), lambda t, i: (t, i, 0))
    return pl.pallas_call(
        hidden_grad_kernel,
        grid=(ways, rows // part),
        in_specs=[
            pl.BlockSpec((part, width), lambda t, i: (i, 0)),
            pl.BlockSpec((1, units, width), lambda t, i: (t, 0, 0)),
            out,
            out,
        ],
        out_specs=[out, out],
        out_shape=[jax.ShapeDtypeStruct((ways, rows, units), BF16)] * 2,
        compiler_params=params(),
        name="hidden_grad",
    )(dy, w_down, act, slope)


def back_kernel(n, *refs):
    g_refs, w_refs, o_ref = refs[:n], refs[n : 2 * n], refs[2 * n]
    acc = nt(g_refs[0][0], w_refs[0][0])
    for g_ref, w_ref in zip(g_refs[1:], w_refs[1:]):
        acc += nt(g_ref[0], w_ref[0])
    first = pl.program_id(1) == 0

    @pl.when(first)
    def _():
        o_ref[...] = acc

    @pl.when(jnp.logical_not(first))
    def _():
        o_ref[...] += acc


def back(grads, weights, units):
    ways, rows, _ = grads[0].shape
    width = weights[0].shape[1]
    part = min(width, 1024)
    return pl.pallas_call(
        functools.partial(back_kernel, len(grads)),
        grid=(width // part, ways),
        in_specs=[pl.BlockSpec((1, rows, units), lambda j, t: (t, 0, 0)) for _ in grads]
        + [pl.BlockSpec((1, part, units), lambda j, t: (t, j, 0)) for _ in weights],
        out_specs=pl.BlockSpec((rows, part), lambda j, t: (0, j)),
        out_shape=jax.ShapeDtypeStruct((rows, width), F32),
        compiler_params=params(),
        name="back",
    )(*grads, *weights)


def mixed_grad_kernel(g_ref, w_ref, o_ref):
    o_ref[0] = nt(g_ref[...], w_ref[0])


def mixed_grad(g_branch, w_out):
    rows, width = g_branch.shape
    ways, chans, _ = w_out.shape
    return pl.pallas_call(
        mixed_grad_kernel,
        grid=(ways,),
        in_specs=[whole((rows, width)), pl.BlockSpec((1, chans, width), lambda t: (t, 0, 0))],
        out_specs=pl.BlockSpec((1, rows, chans), lambda t: (t, 0, 0)),
        out_shape=jax.ShapeDtypeStruct((ways, rows, chans), F32),
        compiler_params=params(),
        name="mixed_grad",
    )(g_branch, w_out)


def columns(ref, at_ref, chips, each):
    picks = [ref[:, pl.ds(pl.multiple_of(at_ref[j] * each, each), each)] for j in range(chips)]
    return jnp.concatenate(picks, axis=1)


def put(o_ref, adds, j, at, wide, value):
    if adds:
        value = value + adds[0][j, 0, :, at : at + wide].astype(F32)
    o_ref[j, 0, :, at : at + wide] = value.astype(BF16)


def by_rows_kernel(chips, n, each, at_ref, left_ref, *refs):
    rights, adds, o_ref = refs[:n], refs[n:-1], refs[-1]
    left = columns(left_ref, at_ref, chips, each)
    at = 0
    for right_ref in rights:
        wide = right_ref.shape[2]
        acc = tn(left, right_ref[0])
        for j in range(chips):
            put(o_ref, adds, j, at, wide, acc[j * each : (j + 1) * each])
        at += wide


def by_cols_kernel(chips, each, at_ref, right_ref, left_ref, *refs):
    adds, o_ref = refs[:-1], refs[-1]
    acc = tn(left_ref[0], columns(right_ref, at_ref, chips, each))
    for j in range(chips):
        put(o_ref, adds, j, 0, each, acc[:, j * each : (j + 1) * each])


def weight_grad(kernel, whole_side, parted, tall, wide, at, adds, chips, name):
    ways, rows, _ = parted[0].shape
    block = pl.BlockSpec((chips, 1, tall, wide), lambda t: (0, t, 0, 0))
    return pl.pallas_call(
        kernel,
        grid=(ways,),
        in_specs=[pl.BlockSpec(memory_space=pltpu.SMEM), whole(whole_side.shape)]
        + [pl.BlockSpec((1, rows, p.shape[2]), lambda t: (t, 0, 0)) for p in parted]
        + [block for _ in adds],
        out_specs=block,
        out_shape=jax.ShapeDtypeStruct((chips, ways, tall, wide), BF16),
        compiler_params=params(),
        name=name,
    )(at, whole_side, *parted, *adds)


def by_rows(left, rights, at, adds, chips):
    each = left.shape[1] // (2 * chips)
    kernel = functools.partial(by_rows_kernel, chips, len(rights), each)
    wide = sum(r.shape[2] for r in rights)
    return weight_grad(kernel, left, rights, each, wide, at, adds, chips, "by_rows")


def by_cols(left, right, at, adds, chips):
    each = right.shape[1] // (2 * chips)
    kernel = functools.partial(by_cols_kernel, chips, each)
    return weight_grad(kernel, right, [left], left.shape[2], each, at, adds, chips, "by_cols")


def norm_pullback(upstream_gradient, unit_rows, inverse_rms, gain_vector):
    scaled_rows = upstream_gradient * gain_vector
    return inverse_rms * (
        scaled_rows - unit_rows * jnp.mean(scaled_rows * unit_rows, axis=1, keepdims=True)
    )


SWAP = ((0, 1), (1, 0))


def behind(value, *done):
    return lax.optimization_barrier((value,) + done)[0]


def from_all(value, axis):
    n = lax.axis_size(axis)
    if n > 4:
        return lax.all_gather(value, axis, axis=0)
    me = lax.axis_index(axis)
    seen = [value]
    for k in range(1, n):
        seen.append(lax.ppermute(value, axis, [((i + k) % n, i) for i in range(n)]))
    return lax.dynamic_slice_in_dim(jnp.stack(seen + seen), (n - me) % n, n, 0)


def local(
    tokens,
    lengths,
    first_norm_gain,
    w_in,
    w_forget,
    w_gate,
    lower_bound,
    gate_gain,
    w_out,
    feedforward_gain,
    w_up,
    w_glu,
    w_down,
    cotangent,
):
    rows, width = tokens.shape
    chans = w_in.shape[1]
    units = w_up.shape[1]
    ways = lax.axis_size("tensor")
    chips = lax.axis_size("chip")
    groups = 2 * chips
    way = lax.axis_index("tensor")
    core = lax.axis_index("core")
    chip = lax.axis_index("chip")
    group = chip * 2 + core
    every = ("tensor", "chip", "core")
    square = chips == 4 and ways == 4

    def gather(weights):
        tall = weights.shape[0] // groups
        piece = lax.dynamic_slice_in_dim(weights, group * tall, tall, 0)
        piece = lax.all_gather(piece, every, axis=0, tiled=True)
        return piece.reshape((ways,) + weights.shape)

    vectors = from_all(jnp.stack([lower_bound, gate_gain]), "tensor")
    lower, gain = vectors[:, 0:1], vectors[:, 1:2]
    l0, l1 = lengths[0, 0], lengths[0, 1]
    starts = jnp.stack([jnp.zeros_like(l0), l0, l0 + l1]) - way * rows
    x = tokens.astype(F32)
    inverse1 = lax.rsqrt(jnp.mean(x * x, axis=1, keepdims=True) + EPS)
    normed = (x * inverse1 * first_norm_gain).astype(BF16)

    shards = [w_in, w_forget, w_gate, w_glu, w_up, w_out]
    if square:
        all_shards, p = gather_weights(shards, ways, normed)
        w_down_all = gather(behind(w_down, all_shards[5]))
    else:
        all_shards = [gather(w) for w in shards]
        w_down_all = gather(w_down)
    w_three, (w_glu_all, w_up_all, w_out_all) = all_shards[:3], all_shards[3:]

    if not square:
        p = project(normed, *w_three)
    totals = forward_total(p, lower, starts)
    all_totals = from_all(totals, "tensor")
    enter = jnp.zeros((ways, 1, chans), F32)
    seen = jnp.zeros((ways, 1, chans), F32)
    for k in range(ways - 1):
        seen = all_totals[k, :, 0:1] * seen + all_totals[k, :, 1:2]
        enter = jnp.where(way == k + 1, seen, enter)
    state, mixed, lam_sum = forward_scan(p, lower, gain, starts, enter)

    resid, middle = branch(mixed, w_out_all, tokens, feedforward_gain.reshape(1, width))
    hidden, act, slope = feed_up(middle, w_up_all, w_glu_all)

    places = jnp.arange(chips, dtype=jnp.int32)

    ours_at, theirs_at = places * 2 + core, places * 2 + (1 - core)

    def swap(array):
        return lax.ppermute(array, "core", SWAP)

    class Scatter:
        def begin(self, array):
            part = lax.psum_scatter(array, "chip", scatter_dimension=0, tiled=True)
            self.part = lax.optimization_barrier(part.reshape(part.shape[1:]))
            self.parts = [self.block(0)]

        def block(self, k):
            return lax.dynamic_index_in_dim(self.part, (way + k) % ways, 0, False)

        def send(self, *steps):
            got = [
                lax.ppermute(self.block(k), "tensor", [(i, (i + k) % ways) for i in range(ways)])
                for k in steps
                if k < ways
            ]
            self.parts += got
            return tuple(got)

        def rest(self):
            part = lax.psum_scatter(self.part, "tensor", scatter_dimension=0, tiled=True)
            self.parts = [part.reshape(part.shape[1:])]

        def finish(self):
            return sum(a.astype(F32) for a in self.parts)

    last = [()]

    def run(fn, *arrays):
        out = fn(*lax.optimization_barrier(arrays + last[0])[: len(arrays)])
        last[0] = tuple(jax.tree.leaves(out))
        return out

    def rows_grad(at, rights, left, *adds):
        n = len(rights)
        got = lambda left, *more: by_rows(left, more[:n], at, more[n:], chips)
        return run(got, left, *rights, *adds)

    def cols_grad(at, left, right, *adds):
        return run(lambda left, right, *more: by_cols(left, right, at, more, chips), left, right, *adds)

    down, up, glu, out, three = [Scatter() for _ in range(5)]
    gy = cotangent

    def beside(arrived):
        last[0] = last[0] + arrived

    def send(scattered, *steps):
        return scattered.send(*steps) if few else ()

    few = ways <= 4

    swapped = swap(cols_grad(theirs_at, hidden, gy))
    down.begin(cols_grad(ours_at, hidden, gy, swapped))
    g_up, g_glu = run(hidden_grad, gy, w_down_all, act, slope)
    swapped_up = swap(rows_grad(theirs_at, [g_up], middle))
    swapped_glu = swap(rows_grad(theirs_at, [g_glu], middle))
    up.begin(rows_grad(ours_at, [g_up], middle, swapped_up))
    glu.begin(rows_grad(ours_at, [g_glu], middle, swapped_glu))
    g_middle = run(
        lambda a, b, c, d: back([a, b], [c, d], units), g_up, g_glu, w_up_all, w_glu_all
    )
    def second_norm(resid, g_middle, gy):
        inverse2 = lax.rsqrt(jnp.mean(resid * resid, axis=1, keepdims=True) + EPS)
        unit2 = resid * inverse2
        mlp_gain_part = jnp.sum(g_middle * unit2, axis=0)
        g_resid = gy.astype(F32) + norm_pullback(g_middle, unit2, inverse2, feedforward_gain)
        return mlp_gain_part, g_resid, g_resid.astype(BF16)

    moving = send(down, 1)
    mlp_gain_part, g_resid, g_branch = run(second_norm, resid, g_middle, gy)
    swapped_out = swap(cols_grad(theirs_at, mixed, g_branch))
    g_mixed = run(mixed_grad, g_branch, w_out_all)
    beside(moving)
    out.begin(cols_grad(ours_at, mixed, g_branch, swapped_out))
    moving = send(down, 2)
    g_state, g_gate, gain_part, back_totals = run(backward_total, p, state, g_mixed, lower, gain, starts)
    beside(moving)
    all_back = lax.all_gather(back_totals, "tensor", axis=0)
    after = jnp.zeros((ways, 1, chans), F32)
    seen = jnp.zeros((ways, 1, chans), F32)
    for k in range(ways - 1, 0, -1):
        seen = all_totals[k, :, 0:1] * seen + all_back[k]
        after = jnp.where(way == k - 1, seen, after)
    moving = send(down, 3)
    g_in, g_forget, lower_part = run(backward_scan, p, state, g_state, lower, starts, enter, after)
    beside(moving)

    g_three = [g_in, g_forget, g_gate]
    swapped = swap(rows_grad(theirs_at, g_three, normed))
    three.begin(rows_grad(ours_at, g_three, normed, swapped))
    moving = send(up, 1, 2, 3)
    output = run(feed_down, hidden, w_down_all, resid)
    beside(moving)
    moving = send(glu, 1)
    g_normed = run(
        lambda *a: back(a[:3], a[3:], chans), *g_three, *w_three
    )
    beside(moving)
    moving = send(glu, 2) + send(out, 1, 2, 3)

    def first_norm_back(x, g_normed, g_resid):
        x = x.astype(F32)
        inverse1 = lax.rsqrt(jnp.mean(x * x, axis=1, keepdims=True) + EPS)
        unit1 = x * inverse1
        norm_gain_part = jnp.sum(g_normed * unit1, axis=0)
        return norm_gain_part, g_resid + norm_pullback(g_normed, unit1, inverse1, first_norm_gain)

    norm_gain_part, token_gradient = run(first_norm_back, tokens, g_normed, g_resid)
    beside(moving)
    moving = send(glu, 3)

    small = jnp.stack(
        [
            norm_gain_part,
            mlp_gain_part,
            jnp.sum(gain_part, axis=1).reshape(width),
            jnp.sum(lower_part, axis=1).reshape(width),
            jnp.sum(lam_sum, axis=1).reshape(width),
        ]
    )
    beside(moving)
    three.part = behind(three.part, *last[0])
    beside((three.part,))
    three.rest()
    small = run(lambda v: lax.psum(v, every), small)
    three.parts = [behind(three.parts[0], small)]
    if not few:
        for s in (down, up, glu, out):
            s.rest()
    grad_w_down, grad_w_up, grad_w_glu, grad_w_out, grad_three = [
        s.finish() for s in (down, up, glu, out, three)
    ]
    mean_forget = jnp.sum(small[4]) / (rows * ways * groups * width)
    return (
        output,
        token_gradient,
        small[0],
        grad_three[:, :chans],
        grad_three[:, chans : 2 * chans],
        grad_three[:, 2 * chans :],
        small[3],
        small[2],
        grad_w_out,
        small[1],
        grad_w_up,
        grad_w_glu,
        grad_w_down,
        mean_forget,
    )


def solution(mesh):
    groups, ways = mesh.shape["dp"], mesh.shape["tensor"]
    parts = Mesh(mesh.devices.reshape(groups // 2, 2, ways), ("chip", "core", "tensor"))
    dp = ("chip", "core")
    tokens = P(("chip", "core", "tensor"), None)
    return jax.shard_map(
        local,
        mesh=parts,
        in_specs=(
            tokens,
            P(dp, None),
            P(),
            P(None, "tensor"),
            P(None, "tensor"),
            P(None, "tensor"),
            P("tensor"),
            P("tensor"),
            P("tensor", None),
            P(),
            P(None, "tensor"),
            P(None, "tensor"),
            P("tensor", None),
            tokens,
        ),
        out_specs=(
            tokens,
            tokens,
            P(),
            P(dp, "tensor"),
            P(dp, "tensor"),
            P(dp, "tensor"),
            P(),
            P(),
            P("tensor", dp),
            P(),
            P(dp, "tensor"),
            P(dp, "tensor"),
            P("tensor", dp),
            P(),
        ),
        check_vma=False,
    )
```
